32 devices in a mesh: tok: 8 (over z, x), ch: 4 (over y, core).
Axes of the slice: x: 2, y: 2, z: 4, core: 2. Of those that a mesh axis runs over, the one named last changes fastest.
Arguments:
- h_in: bfloat16 [16384, 768], P('tok'), may hold values from -6 to 6
- cotangent: bfloat16 [16384, 768], P('tok'), may hold values from -16 to 16
- carried: bfloat16 [2, 8, 256, 2, 768], P(None, 'tok', None, None, 'ch'), may hold values from -6 to 6
- centres: int32 [256], replicated, may hold values from 0 to 1023
- sticky: int32 [8, 3, 256], P('tok'), may hold values from 0 to 1023
- flags: int32 [8], P('tok'), may hold values 0 or 1
- w_qkv: float32 [2, 3, 768, 768], P(None, None, 'tok', 'ch'), may hold values from -0.21875 to 0.21875
- w_qkv_first: float32 [2, 3, 768, 768], P(None, None, 'tok', 'ch'), may hold values from -1 to 1
- w_qkv_second: float32 [2, 3, 768, 768], P(None, None, 'tok', 'ch'), may hold values from 0 to 1
- w_out_t: float32 [2, 768, 768], P(None, 'tok', 'ch'), may hold values from -3.5 to 3.5
- w_out_first: float32 [2, 768, 768], P(None, 'tok', 'ch'), may hold values from -1 to 1
- w_out_second: float32 [2, 768, 768], P(None, 'tok', 'ch'), may hold values from 0 to 1
- w_up: float32 [2, 768, 3072], P(None, 'tok', 'ch'), may hold values from -0.21875 to 0.21875
- w_up_first: float32 [2, 768, 3072], P(None, 'tok', 'ch'), may hold values from -1 to 1
- w_up_second: float32 [2, 768, 3072], P(None, 'tok', 'ch'), may hold values from 0 to 1
- w_down_t: float32 [2, 768, 3072], P(None, 'tok', 'ch'), may hold values from -1 to 1
- w_down_first: float32 [2, 768, 3072], P(None, 'tok', 'ch'), may hold values from -1 to 1
- w_down_second: float32 [2, 768, 3072], P(None, 'tok', 'ch'), may hold values from 0 to 1
- vec_d: float32 [2, 6, 768], replicated, may hold values from -3 to 3
- vec_d_first: float32 [2, 6, 768], replicated, may hold values from -1 to 1
- vec_d_second: float32 [2, 6, 768], replicated, may hold values from 0 to 1
- vec_c: float32 [2, 6, 768], P(None, None, 'ch'), may hold values from -3 to 3
- vec_c_first: float32 [2, 6, 768], P(None, None, 'ch'), may hold values from -1 to 1
- vec_c_second: float32 [2, 6, 768], P(None, None, 'ch'), may hold values from 0 to 1
Outputs:
- activations: float32 [16384, 768], P('tok')
- input_grad: float32 [16384, 768], P('tok')
- grad_norm: float32 [], replicated
- new_w_qkv: float32 [2, 3, 768, 768], P(None, None, 'tok', 'ch')
- new_qkv_first: float32 [2, 3, 768, 768], P(None, None, 'tok', 'ch')
- new_qkv_second: float32 [2, 3, 768, 768], P(None, None, 'tok', 'ch')
- new_w_out: float32 [2, 768, 768], P(None, 'tok', 'ch')
- new_out_first: float32 [2, 768, 768], P(None, 'tok', 'ch')
- new_out_second: float32 [2, 768, 768], P(None, 'tok', 'ch')
- new_w_up: float32 [2, 768, 3072], P(None, 'tok', 'ch')
- new_up_first: float32 [2, 768, 3072], P(None, 'tok', 'ch')
- new_up_second: float32 [2, 768, 3072], P(None, 'tok', 'ch')
- new_w_down: float32 [2, 768, 3072], P(None, 'tok', 'ch')
- new_down_first: float32 [2, 768, 3072], P(None, 'tok', 'ch')
- new_down_second: float32 [2, 768, 3072], P(None, 'tok', 'ch')
- new_vec_d: float32 [2, 6, 768], replicated
- new_vec_d_first: float32 [2, 6, 768], replicated
- new_vec_d_second: float32 [2, 6, 768], replicated
- new_vec_c: float32 [2, 6, 768], P(None, None, 'ch')
- new_vec_c_first: float32 [2, 6, 768], P(None, None, 'ch')
- new_vec_c_second: float32 [2, 6, 768], P(None, None, 'ch')
The draws below stay inside these ranges and needn't reach their ends.
All inputs are finite; a program needn't handle non-finite values. No bound on the sum of `flags` on one device may be relied on, other than what follows from the above.
Results may differ from the reference program's by a relative error of at most 0.02.
Values may be sent and summed in bfloat16 or wider, within the bound.
No kernel may reach another device: no remote copies, remote signals or barrier semaphores. Data moves between devices by JAX's collectives and lax.ppermute only.
A program may use at most 256 MiB of HBM per device.

```python
from functools import partial
import jax
import jax.numpy as jnp
from jax import lax

D = 768
HEAD_DIM = 64
FF = 3072
BASIS = 256
SAMPLES = 256
SEG = 512
SEGS = 4
CRES = 1024
LAYERS = 2
STEP = 10
SEQ_LEN = 2048
SEQS = 8
TOKENS = 16384


def grad_scale():
    return 1.0 / (LAYERS * (4 * D * D + 2 * D * FF + 12 * D)) ** 0.5


def first_moment(key, array_shape, entry_scale):
    return jax.random.normal(key, array_shape, jnp.float32) * (entry_scale / 9.0)


def second_moment(key, array_shape, entry_scale):
    spread = jax.random.uniform(key, array_shape, jnp.float32, minval=-0.7, maxval=2.08)
    return jnp.exp(spread) * (entry_scale * entry_scale / 19.0)


def draw_cotangent(key, part):
    own_key = jax.random.fold_in(key, 101)
    column = jnp.arange(D).astype(jnp.float32) / D
    return ((0.6 + 1.2 * column) * jax.random.normal(own_key, (TOKENS, D), jnp.float32)).astype(jnp.bfloat16)


def draw_w_down_t(key, part):
    own_key = jax.random.fold_in(key, 102)
    column = jnp.arange(FF).astype(jnp.float32) / FF
    noise_draw = jax.random.normal(own_key, (LAYERS, D, FF), jnp.float32)
    return (0.6 + 1.2 * column) * noise_draw / FF ** 0.5


def draw_vec_d(key, part):
    own_key = jax.random.fold_in(key, 103)
    column = jnp.arange(D).astype(jnp.float32) / D
    rise_scale = 0.5 + column
    noise_draw = jnp.clip(jax.random.normal(own_key, (LAYERS, 6, D), jnp.float32), -4.0, 4.0)
    gain_rows = rise_scale * (1.0 + 0.15 * noise_draw)
    shift_rows = 0.2 * noise_draw
    row_index = jnp.arange(6)
    is_gain = (row_index == 0) | (row_index == 2)
    return jnp.where(is_gain[None, :, None], gain_rows, shift_rows)


def draw_w_qkv_first(key, part):
    return first_moment(jax.random.fold_in(key, 111), (LAYERS, 3, D, D), grad_scale())


def draw_w_qkv_second(key, part):
    return second_moment(jax.random.fold_in(key, 112), (LAYERS, 3, D, D), grad_scale())


def draw_w_out_first(key, part):
    return first_moment(jax.random.fold_in(key, 121), (LAYERS, D, D), 0.3 * grad_scale())


def draw_w_out_second(key, part):
    return second_moment(jax.random.fold_in(key, 122), (LAYERS, D, D), 0.3 * grad_scale())


def draw_w_up_first(key, part):
    return first_moment(jax.random.fold_in(key, 131), (LAYERS, D, FF), grad_scale())


def draw_w_up_second(key, part):
    return second_moment(jax.random.fold_in(key, 132), (LAYERS, D, FF), grad_scale())


def draw_w_down_first(key, part):
    return first_moment(jax.random.fold_in(key, 141), (LAYERS, D, FF), grad_scale())


def draw_w_down_second(key, part):
    return second_moment(jax.random.fold_in(key, 142), (LAYERS, D, FF), grad_scale())


def draw_vec_d_first(key, part):
    return first_moment(jax.random.fold_in(key, 151), (LAYERS, 6, D), 4.0 * grad_scale())


def draw_vec_d_second(key, part):
    return second_moment(jax.random.fold_in(key, 152), (LAYERS, 6, D), 4.0 * grad_scale())


def draw_vec_c_first(key, part):
    return first_moment(jax.random.fold_in(key, 161), (LAYERS, 6, D), 4.0 * grad_scale())


def draw_vec_c_second(key, part):
    return second_moment(jax.random.fold_in(key, 162), (LAYERS, 6, D), 4.0 * grad_scale())


def with_ends(values, key, low, top_value):
    longest = values.shape.index(max(values.shape))
    spots = []
    for shift in (0, 1):
        where = [jax.random.randint(jax.random.fold_in(key, axis), (), 0, length) for axis, length in enumerate(values.shape)]
        where[longest] = (where[longest] + shift) % values.shape[longest]
        spots.append(tuple(where))
    return values.at[spots[0]].set(low).at[spots[1]].set(top_value)


def shard_levels(key, dims, pieces, least, top_value):
    def one(dim, parts):
        heights = jax.random.uniform(jax.random.fold_in(jax.random.fold_in(key, 6), dim), (parts,), jnp.float32, least / len(pieces), top_value / len(pieces))
        return jnp.repeat(jnp.exp(heights), dims[dim] // parts).reshape((-1,) + (1,) * (len(dims) - dim - 1))

    loudness = one(*pieces[0])
    for cut in pieces[1:]:
        loudness = loudness * one(*cut)
    return loudness


def noise(key, dims, deviation, most, shards=(), held_as=jnp.bfloat16):
    factor_of = shard_levels(key, dims, shards, -0.22, 0.18) if shards else 1.0
    result = jax.random.normal(key, dims, jnp.float32) * deviation * factor_of
    return jnp.minimum(jnp.maximum(result, -most), most).astype(held_as)


def setup_inputs(seed: int = 0) -> dict:
    key_list = jax.random.split(jax.random.key(seed), 25)
    return {
        "h_in": noise(key_list[0], (TOKENS, D), 1.0, 6.0, ((0, 8),)),
        "cotangent": draw_cotangent(jax.random.fold_in(key_list[24], 71), 0),
        "carried": noise(key_list[2], (LAYERS, SEQS, BASIS, 2, D), 1.0, 6.0, ((1, 8), (4, 4))),
        "centres": with_ends(jax.random.randint(key_list[3], (BASIS,), 0, CRES), jax.random.fold_in(key_list[3], 1), 0, CRES - 1).astype(jnp.int32),
        "sticky": with_ends(jax.random.randint(key_list[4], (SEQS, SEGS - 1, SAMPLES), 0, CRES), jax.random.fold_in(key_list[4], 1), 0, CRES - 1).astype(jnp.int32),
        "flags": with_ends((jax.random.randint(key_list[5], (SEQS,), 0, 2) < 1).astype(jnp.int32), jax.random.fold_in(key_list[5], 1), 0, 1),
        "w_qkv": noise(key_list[6], (LAYERS, 3, D, D), D ** -0.5, 0.21875, ((2, 8), (3, 4)), jnp.float32),
        "w_qkv_first": draw_w_qkv_first(jax.random.fold_in(key_list[24], 71), 0),
        "w_qkv_second": draw_w_qkv_second(jax.random.fold_in(key_list[24], 71), 0),
        "w_out_t": noise(key_list[9], (LAYERS, D, D), (max(D // 256, 1)) ** -0.5, 3.5, ((1, 8), (2, 4)), jnp.float32),
        "w_out_first": draw_w_out_first(jax.random.fold_in(key_list[24], 71), 0),
        "w_out_second": draw_w_out_second(jax.random.fold_in(key_list[24], 71), 0),
        "w_up": noise(key_list[12], (LAYERS, D, FF), D ** -0.5, 0.21875, ((1, 8), (2, 4)), jnp.float32),
        "w_up_first": draw_w_up_first(jax.random.fold_in(key_list[24], 71), 0),
        "w_up_second": draw_w_up_second(jax.random.fold_in(key_list[24], 71), 0),
        "w_down_t": draw_w_down_t(jax.random.fold_in(key_list[24], 71), 0),
        "w_down_first": draw_w_down_first(jax.random.fold_in(key_list[24], 71), 0),
        "w_down_second": draw_w_down_second(jax.random.fold_in(key_list[24], 71), 0),
        "vec_d": draw_vec_d(jax.random.fold_in(key_list[24], 71), 0),
        "vec_d_first": draw_vec_d_first(jax.random.fold_in(key_list[24], 71), 0),
        "vec_d_second": draw_vec_d_second(jax.random.fold_in(key_list[24], 71), 0),
        "vec_c": noise(key_list[21], (LAYERS, 6, D), 0.2, 3.0, ((2, 4),), jnp.float32),
        "vec_c_first": draw_vec_c_first(jax.random.fold_in(key_list[24], 71), 0),
        "vec_c_second": draw_vec_c_second(jax.random.fold_in(key_list[24], 71), 0),
    }


PRECISE = lax.Precision.HIGHEST
STICKY_RATIO = 0.5
RIDGE_WEIGHT = 0.5
BASIS_WIDTH = 0.01
NORM_EPS = 1e-05
CLIP_LIMIT = 1.0
FIRST_DECAY = 0.9
SECOND_DECAY = 0.95
ADAM_EPS = 1e-08
WEIGHT_DECAY = 0.1
RATE_QKV = 0.05
RATE_OUT = 0.5
RATE_UP = 0.05
RATE_DOWN = 0.03
RATE_VECTOR = 0.5
MASKED = -1e+30

@jax.custom_vjp
def low(v):
    return lax.optimization_barrier(v.astype(jnp.bfloat16)).astype(jnp.float32)

@jax.custom_vjp
def low_back(v):
    return v

def low_keep(v):
    return (low(v), None)

def low_pass(kept, grad):
    return (grad,)

def back_keep(v):
    return (v, None)

def back_low(kept, grad):
    return (low(grad),)
low.defvjp(low_keep, low_pass)
low_back.defvjp(back_keep, back_low)

def layer_norm(inputs, gain_vec, shift_vec):
    mean_row = lax.optimization_barrier(jnp.mean(inputs, axis=-1, keepdims=True))
    centred = inputs - mean_row
    variance = lax.optimization_barrier(jnp.mean(centred * centred, axis=-1, keepdims=True))
    return centred * lax.rsqrt(variance + NORM_EPS) * gain_vec + shift_vec

def basis_table(centres, times):
    middle = (centres.astype(jnp.float32) + 0.5) / CRES
    offset = (times[None, :] - middle[:, None]) / BASIS_WIDTH
    return jnp.exp(-0.5 * offset * offset)

def gram_tables(centres, sticky):
    token_times = STICKY_RATIO + (1.0 - STICKY_RATIO) * (jnp.arange(SEG).astype(jnp.float32) + 0.5) / SEG
    token_basis = basis_table(centres, token_times)
    places = (sticky.astype(jnp.float32) + 0.5) / CRES
    old_basis = jax.vmap(partial(basis_table, centres))(places)
    new_basis = jax.vmap(partial(basis_table, centres))(STICKY_RATIO * places)
    design = jnp.concatenate([new_basis, jnp.broadcast_to(token_basis, (places.shape[0],) + token_basis.shape)], axis=2)
    gram = jnp.einsum('snl,sml->snm', design, design, precision=PRECISE) + RIDGE_WEIGHT * jnp.eye(BASIS, dtype=jnp.float32)
    factor_lower = jnp.linalg.cholesky(gram)
    identity = jnp.broadcast_to(jnp.eye(BASIS, dtype=jnp.float32), gram.shape)
    inverse_factor = jax.scipy.linalg.solve_triangular(factor_lower, identity, lower=True)
    inverse = jnp.einsum('sln,slm->snm', inverse_factor, inverse_factor, precision=PRECISE)
    return (old_basis, design, inverse)

def adamw(weight, first, second, grad, rate, decay):
    first_new = FIRST_DECAY * first + (1.0 - FIRST_DECAY) * grad
    second_new = SECOND_DECAY * second + (1.0 - SECOND_DECAY) * grad * grad
    first_hat = first_new / (1.0 - FIRST_DECAY ** STEP)
    second_hat = second_new / (1.0 - SECOND_DECAY ** STEP)
    weight_new = weight * (1.0 - rate * decay) - rate * first_hat / (jnp.sqrt(second_hat) + ADAM_EPS)
    return (weight_new, first_new, second_new)

def memory_fit(key_rows, values, carried_start, old_basis, design, inverse):
    signal = jnp.stack([key_rows, values], axis=1).reshape(SEGS, SEG, 2 * D)
    current = carried_start
    collected = [current]
    for segment in range(1, SEGS):
        sampled = jnp.dot(old_basis[segment - 1].T, current, precision=PRECISE)
        stacked = jnp.concatenate([sampled, signal[segment - 1]], axis=0)
        fitted = jnp.dot(design[segment - 1], stacked, precision=PRECISE)
        current = jnp.dot(inverse[segment - 1], fitted, precision=PRECISE)
        collected.append(current)
    return jnp.stack(collected)

def segment_attention(block):
    queries, key_cat, value_cat, memory_on = block
    head_count = D // HEAD_DIM
    query_heads = queries.reshape(SEG, head_count, HEAD_DIM)
    key_heads = key_cat.reshape(SEG + BASIS, head_count, HEAD_DIM)
    value_heads = value_cat.reshape(SEG + BASIS, head_count, HEAD_DIM)
    scores = low_back(jnp.einsum('ihe,jhe->hij', query_heads, key_heads, precision=PRECISE) * HEAD_DIM ** (-0.5))
    row_index = jnp.arange(SEG)[:, None]
    col_index = jnp.arange(SEG + BASIS)[None, :]
    visible = jnp.where(col_index < SEG, col_index <= row_index, memory_on > 0)
    scores = jnp.where(visible[None], scores, MASKED)
    weights = low(jax.nn.softmax(scores, axis=-1))
    return jnp.einsum('hij,jhe->ihe', weights, value_heads, precision=PRECISE).reshape(SEG, D)

def sequence_forward(params, stream, memory, flag_value, old_basis, design, inverse):
    w_qkv, w_out_t, w_up, w_down_t, vec_d, vec_c = params
    memory_on = jnp.where(jnp.arange(SEGS) > 0, 1, flag_value)
    for layer_index in range(LAYERS):
        qkv_low = low(w_qkv[layer_index])
        out_low = low(w_out_t[layer_index])
        up_low = low(w_up[layer_index])
        down_low = low(w_down_t[layer_index])
        gain_rows = vec_d[layer_index]
        bias_rows = vec_c[layer_index]
        normed = low(layer_norm(stream, gain_rows[0], gain_rows[1]))
        queries = low(low_back(jnp.dot(normed, qkv_low[0], precision=PRECISE) + bias_rows[0]))
        key_rows = low(low_back(jnp.dot(normed, qkv_low[1], precision=PRECISE)))
        values = low(low_back(jnp.dot(normed, qkv_low[2], precision=PRECISE) + bias_rows[1]))
        carried_start = memory[layer_index].reshape(BASIS, 2 * D) * flag_value.astype(jnp.float32)
        coefficients = memory_fit(key_rows, values, carried_start, old_basis, design, inverse)
        memory_low = low(coefficients).reshape(SEGS, BASIS, 2, D)
        key_cat = jnp.concatenate([key_rows.reshape(SEGS, SEG, D), memory_low[:, :, 0]], axis=1)
        value_cat = jnp.concatenate([values.reshape(SEGS, SEG, D), memory_low[:, :, 1]], axis=1)
        attended = lax.map(jax.checkpoint(segment_attention), (queries.reshape(SEGS, SEG, D), key_cat, value_cat, memory_on))
        attended = low(low_back(attended.reshape(SEGS * SEG, D)))
        middle = stream + low_back(jnp.dot(attended, out_low.T, precision=PRECISE) + gain_rows[4])
        normed_two = low(layer_norm(middle, gain_rows[2], gain_rows[3]))
        hidden = low_back(jnp.dot(normed_two, up_low, precision=PRECISE) + bias_rows[2:6].T.reshape(FF))
        active = low(jax.nn.gelu(hidden, approximate=True))
        stream = middle + low_back(jnp.dot(active, down_low.T, precision=PRECISE) + gain_rows[5])
    return stream

def reference(h_in, cotangent, carried, centres, sticky, flags, w_qkv, w_qkv_first, w_qkv_second, w_out_t, w_out_first, w_out_second, w_up, w_up_first, w_up_second, w_down_t, w_down_first, w_down_second, vec_d, vec_d_first, vec_d_second, vec_c, vec_c_first, vec_c_second):
    params = (w_qkv, w_out_t, w_up, w_down_t, vec_d, vec_c)
    old_all, design_all, inverse_all = jax.vmap(partial(gram_tables, centres))(sticky)
    inputs = h_in.astype(jnp.float32).reshape(SEQS, SEQ_LEN, D)
    grads_in = cotangent.astype(jnp.float32).reshape(SEQS, SEQ_LEN, D)
    memories = jnp.swapaxes(carried.astype(jnp.float32), 0, 1)

    def per_sequence(totals, sequence_item):
        stream, grad_rows, memory, flag_value, old_basis, design, inverse = sequence_item

        def forward_run(weights, start_rows):
            return sequence_forward(weights, start_rows, memory, flag_value, old_basis, design, inverse)
        output, backward = jax.vjp(forward_run, params, stream)
        weight_grads, stream_grad = backward(grad_rows)
        totals = jax.tree.map(lambda first_term, second_term: first_term + second_term, totals, weight_grads)
        return (totals, (output, stream_grad))
    zero_grads = jax.tree.map(jnp.zeros_like, params)
    totals, (outputs, input_grads) = lax.scan(per_sequence, zero_grads, (inputs, grads_in, memories, flags, old_all, design_all, inverse_all))
    square_total = sum((jnp.sum(entry * entry) for entry in totals))
    grad_norm = jnp.sqrt(square_total)
    factor = CLIP_LIMIT / jnp.maximum(grad_norm, CLIP_LIMIT)
    attention_update = adamw(w_qkv, w_qkv_first, w_qkv_second, totals[0] * factor, RATE_QKV, WEIGHT_DECAY)
    output_update = adamw(w_out_t, w_out_first, w_out_second, totals[1] * factor, RATE_OUT, WEIGHT_DECAY)
    expand_update = adamw(w_up, w_up_first, w_up_second, totals[2] * factor, RATE_UP, WEIGHT_DECAY)
    reduce_update = adamw(w_down_t, w_down_first, w_down_second, totals[3] * factor, RATE_DOWN, WEIGHT_DECAY)
    width_update = adamw(vec_d, vec_d_first, vec_d_second, totals[4] * factor, RATE_VECTOR, 0.0)
    channel_update = adamw(vec_c, vec_c_first, vec_c_second, totals[5] * factor, RATE_VECTOR, 0.0)
    return (outputs.reshape(TOKENS, D), input_grads.reshape(TOKENS, D), grad_norm, attention_update[0], attention_update[1], attention_update[2], output_update[0], output_update[1], output_update[2], expand_update[0], expand_update[1], expand_update[2], reduce_update[0], reduce_update[1], reduce_update[2], width_update[0], width_update[1], width_update[2], channel_update[0], channel_update[1], channel_update[2])
```

```python
from functools import partial

import jax
import jax.numpy as jnp
from jax import lax
from jax.experimental import pallas as pl
from jax.experimental.pallas import tpu as pltpu
from jax.sharding import Mesh
from jax.sharding import PartitionSpec as P

HEAD_DIM = 64
BASIS = 256
SAMPLES = 256
SEG = 512
SEGS = 4
CRES = 1024
LAYERS = 2
STEP = 10

PRECISE = lax.Precision.HIGHEST
STICKY_RATIO = 0.5
RIDGE_WEIGHT = 0.5
BASIS_WIDTH = 0.01
NORM_EPS = 1e-05
CLIP_LIMIT = 1.0
FIRST_DECAY = 0.9
SECOND_DECAY = 0.95
ADAM_EPS = 1e-08
WEIGHT_DECAY = 0.1
RATE_QKV = 0.05
RATE_OUT = 0.5
RATE_UP = 0.05
RATE_DOWN = 0.03
RATE_VECTOR = 0.5
MASKED = -1e30
F32 = jnp.float32
BF16 = jnp.bfloat16
SWAP = ((0, 1), (1, 0))
NN = (((1,), (0,)), ((), ()))
NT = (((1,), (1,)), ((), ()))
TN = (((0,), (0,)), ((), ()))


def dot(left, right, dims, precision=None):
    return lax.dot_general(left, right, dims, precision=precision, preferred_element_type=F32)


def table_kernel(old_ref, design_ref, out_ref, inv_ref, gram_ref):
    design = design_ref[...]
    eye = (
        lax.broadcasted_iota(jnp.int32, (BASIS, BASIS), 0)
        == lax.broadcasted_iota(jnp.int32, (BASIS, BASIS), 1)
    ).astype(F32)
    gram = dot(design, design, NT, PRECISE) + RIDGE_WEIGHT * eye
    gram_ref[...] = gram
    bound = jnp.max(jnp.sum(jnp.abs(gram), axis=0))
    inv_ref[...] = eye * (1.0 / bound)

    def step(low):
        scale = 2.0 / (1.0 + low)
        now = inv_ref[...]
        inner = dot(gram_ref[...], now, NN, PRECISE)
        inv_ref[...] = scale * (2.0 * now - scale * dot(now, inner, NN, PRECISE))
        return 4.0 * low / ((1.0 + low) * (1.0 + low))

    lax.while_loop(lambda low: low < 0.999, step, 0.99 * RIDGE_WEIGHT / bound)
    for _ in range(2):
        now = inv_ref[...]
        inner = dot(gram_ref[...], now, NN, PRECISE)
        inv_ref[...] = 2.0 * now - dot(now, inner, NN, PRECISE)
    fitted = dot(inv_ref[...], design, NN, PRECISE)
    out_ref[:, BASIS:] = fitted[:, SAMPLES:].astype(BF16)
    out_ref[:, :BASIS] = dot(fitted[:, :SAMPLES], old_ref[...], NT, PRECISE).astype(BF16)


def basis_table(centres, times):
    middle = (centres.astype(F32) + 0.5) / CRES
    offset = (times[None, :] - middle[:, None]) / BASIS_WIDTH
    return jnp.exp(-0.5 * offset * offset)


def make_tables(centres, sticky_row):
    token_times = STICKY_RATIO + (1.0 - STICKY_RATIO) * (jnp.arange(SEG).astype(F32) + 0.5) / SEG
    places = (sticky_row.astype(F32) + 0.5) / CRES
    old_basis = basis_table(centres, places)
    design = basis_table(centres, jnp.concatenate([STICKY_RATIO * places, token_times]))
    return pl.pallas_call(
        table_kernel,
        out_shape=jax.ShapeDtypeStruct((BASIS, BASIS + SEG), BF16),
        scratch_shapes=[pltpu.VMEM((BASIS, BASIS), F32), pltpu.VMEM((BASIS, BASIS), F32)],
        compiler_params=pltpu.CompilerParams(vmem_limit_bytes=32 * 2**20),
        cost_estimate=pl.CostEstimate(flops=6 * 10**9, bytes_accessed=2 * 10**6, transcendentals=0),
    )(old_basis, design)


QT = 256


def causal(shape):
    return lax.broadcasted_iota(jnp.int32, shape, 0) <= lax.broadcasted_iota(jnp.int32, shape, 1)


def attention_forward_kernel(
    bias_ref, q_ref, k_ref, v_ref, mk_ref, mv_ref, out_ref, lse_ref
):
    memory_bias = bias_ref[pl.program_id(0)]
    pair = q_ref.shape[1] // HEAD_DIM
    queries = q_ref[...] * HEAD_DIM ** (-0.5)
    for tile in range(SEG // QT):
        rows = slice(tile * QT, (tile + 1) * QT)
        stacked = []
        for head in range(pair):
            lanes = slice(head * HEAD_DIM, (head + 1) * HEAD_DIM)
            query = queries[rows, lanes]
            scores = []
            values = []
            for part in range(tile + 1):
                keys = slice(part * QT, (part + 1) * QT)
                score = dot(k_ref[keys, lanes], query, NT)
                if part == tile:
                    score = jnp.where(causal(score.shape), score, MASKED)
                scores.append(score)
                values.append(v_ref[keys, lanes])
            scores.append(dot(mk_ref[0, :, lanes], query, NT) + memory_bias)
            values.append(mv_ref[0, :, lanes])
            top = scores[0].max(axis=0, keepdims=True)
            for score in scores[1:]:
                top = jnp.maximum(top, score.max(axis=0, keepdims=True))
            total = jnp.zeros_like(top)
            result = jnp.zeros((HEAD_DIM, QT), F32)
            for score, value in zip(scores, values):
                weight = jnp.exp(score - top)
                total = total + weight.sum(axis=0, keepdims=True)
                result = result + dot(value, weight.astype(BF16), TN)
            stacked.append(result / total)
            lse_ref[0, head : head + 1, rows] = top + jnp.log(total)
        out_ref[rows, :] = jnp.concatenate(stacked, axis=0).T.astype(BF16)


def attention_forward(qkv, memory, memory_bias):
    rows, width = qkv.shape[0], qkv.shape[1] // 3
    pairs = width // 128
    segs = rows // SEG
    return pl.pallas_call(
        attention_forward_kernel,
        grid=(segs, pairs),
        in_specs=[
            pl.BlockSpec(memory_space=pltpu.SMEM),
            pl.BlockSpec((SEG, 128), lambda s, h: (s, h)),
            pl.BlockSpec((SEG, 128), lambda s, h: (s, pairs + h)),
            pl.BlockSpec((SEG, 128), lambda s, h: (s, 2 * pairs + h)),
            pl.BlockSpec((1, BASIS, 128), lambda s, h: (s, 0, h)),
            pl.BlockSpec((1, BASIS, 128), lambda s, h: (s, 0, pairs + h)),
        ],
        out_specs=[
            pl.BlockSpec((SEG, 128), lambda s, h: (s, h)),
            pl.BlockSpec((1, 2, SEG), lambda s, h: (s * pairs + h, 0, 0)),
        ],
        out_shape=[
            jax.ShapeDtypeStruct((rows, width), BF16),
            jax.ShapeDtypeStruct((segs * pairs, 2, SEG), F32),
        ],
        compiler_params=pltpu.CompilerParams(vmem_limit_bytes=48 * 2**20),
        cost_estimate=pl.CostEstimate(
            flops=12 * 10**9, bytes_accessed=5 * 10**6, transcendentals=4 * 10**6
        ),
    )(memory_bias, qkv, qkv, qkv, memory, memory)


def attention_backward_kernel(
    bias_ref,
    q_ref,
    k_ref,
    v_ref,
    mk_ref,
    mv_ref,
    lse_ref,
    out_ref,
    grad_ref,
    dq_ref,
    dk_ref,
    dv_ref,
    dmk_ref,
    dmv_ref,
):
    memory_bias = bias_ref[pl.program_id(0)]
    pair = q_ref.shape[1] // HEAD_DIM
    scale = HEAD_DIM ** (-0.5)
    tiles = SEG // QT
    product = (out_ref[...].astype(F32) * grad_ref[...].astype(F32)).T
    query_grads = []
    for head in range(pair):
        lanes = slice(head * HEAD_DIM, (head + 1) * HEAD_DIM)
        query = q_ref[:, lanes] * scale
        grad = grad_ref[:, lanes]
        dots = product[lanes, :].sum(axis=0, keepdims=True)
        log_total = lse_ref[0, head : head + 1, :]
        head_grads = [jnp.zeros((HEAD_DIM, QT), F32) for _ in range(tiles)]
        for part in range(tiles + 1):
            if part < tiles:
                keys = slice(part * QT, (part + 1) * QT)
                key, value = k_ref[keys, lanes], v_ref[keys, lanes]
            else:
                key, value = mk_ref[0, :, lanes], mv_ref[0, :, lanes]
            key_grad = jnp.zeros((QT, HEAD_DIM), F32)
            value_grad = jnp.zeros((QT, HEAD_DIM), F32)
            for tile in range(part if part < tiles else 0, tiles):
                rows = slice(tile * QT, (tile + 1) * QT)
                score = dot(key, query[rows], NT)
                if part == tile:
                    score = jnp.where(causal(score.shape), score, MASKED)
                if part == tiles:
                    score = score + memory_bias
                weight = jnp.exp(score - log_total[:, rows])
                weight_grad = dot(value, grad[rows], NT)
                score_grad = (weight * (weight_grad - dots[:, rows])).astype(BF16)
                value_grad = value_grad + dot(weight.astype(BF16), grad[rows], NN)
                key_grad = key_grad + dot(score_grad, query[rows], NN)
                head_grads[tile] = head_grads[tile] + dot(key, score_grad, TN)
            if part < tiles:
                dk_ref[keys, lanes] = key_grad
                dv_ref[keys, lanes] = value_grad
            else:
                dmk_ref[0, :, lanes] = key_grad
                dmv_ref[0, :, lanes] = value_grad
        query_grads.append(jnp.concatenate(head_grads, axis=1) * scale)
    dq_ref[...] = jnp.concatenate(query_grads, axis=0).T.astype(BF16)


def attention_backward(qkv, memory, memory_bias, log_totals, attended, grad):
    rows, width = attended.shape
    pairs = width // 128
    segs = rows // SEG
    block = pl.BlockSpec((SEG, 128), lambda s, h: (s, h))
    memory_block = pl.BlockSpec((1, BASIS, 128), lambda s, h: (s, 0, h))
    return pl.pallas_call(
        attention_backward_kernel,
        grid=(segs, pairs),
        in_specs=[
            pl.BlockSpec(memory_space=pltpu.SMEM),
            block,
            pl.BlockSpec((SEG, 128), lambda s, h: (s, pairs + h)),
            pl.BlockSpec((SEG, 128), lambda s, h: (s, 2 * pairs + h)),
            memory_block,
            pl.BlockSpec((1, BASIS, 128), lambda s, h: (s, 0, pairs + h)),
            pl.BlockSpec((1, 2, SEG), lambda s, h: (s * pairs + h, 0, 0)),
            block,
            block,
        ],
        out_specs=[block, block, block, memory_block, memory_block],
        out_shape=[
            jax.ShapeDtypeStruct((rows, width), BF16),
            jax.ShapeDtypeStruct((rows, width), F32),
            jax.ShapeDtypeStruct((rows, width), F32),
            jax.ShapeDtypeStruct((segs, BASIS, width), F32),
            jax.ShapeDtypeStruct((segs, BASIS, width), F32),
        ],
        compiler_params=pltpu.CompilerParams(vmem_limit_bytes=48 * 2**20),
        cost_estimate=pl.CostEstimate(
            flops=24 * 10**9, bytes_accessed=9 * 10**6, transcendentals=4 * 10**6
        ),
    )(memory_bias, qkv, qkv, qkv, memory, memory, log_totals, attended, grad)


def adamw(weight, first, second, grad, rate, decay):
    first_new = FIRST_DECAY * first + (1.0 - FIRST_DECAY) * grad
    second_new = SECOND_DECAY * second + (1.0 - SECOND_DECAY) * grad * grad
    first_hat = first_new / (1.0 - FIRST_DECAY**STEP)
    second_hat = second_new / (1.0 - SECOND_DECAY**STEP)
    weight_new = weight * (1.0 - rate * decay) - rate * first_hat / (
        jnp.sqrt(second_hat) + ADAM_EPS
    )
    return (weight_new, first_new, second_new)


def norm_stats(inputs):
    mean_row = jnp.mean(inputs, axis=-1, keepdims=True)
    centred = inputs - mean_row
    variance = jnp.mean(centred * centred, axis=-1, keepdims=True)
    rstd = lax.rsqrt(variance + NORM_EPS)
    return centred * rstd, rstd


def layer_norm(inputs, gain_vec, shift_vec):
    unit, _ = norm_stats(inputs)
    return unit * gain_vec + shift_vec


def norm_backward(inputs, grad, gain_vec):
    unit, rstd = norm_stats(inputs)
    scaled = grad * gain_vec
    back = rstd * (
        scaled
        - jnp.mean(scaled, axis=-1, keepdims=True)
        - unit * jnp.mean(scaled * unit, axis=-1, keepdims=True)
    )
    return back, jnp.sum(grad * unit, axis=0), jnp.sum(grad, axis=0)


def flip(array, axis):
    return lax.ppermute(array, axis, SWAP)


def pair_sum(part):
    own = lax.optimization_barrier(part.astype(BF16))
    return own.astype(F32) + flip(own, "cc").astype(F32)


def swap_halves(array):
    shape = array.shape
    parts = array.reshape(shape[:-1] + (2, 2, shape[-1] // 4))
    return parts[..., ::-1, :].reshape(shape)


def all_gather_slabs(shard, depth, first_axis, second_axis):
    spread = jnp.broadcast_to(shard[None], (depth,) + shard.shape)
    own = lax.all_to_all(spread, "tz", 0, 0, tiled=True).reshape(-1, shard.shape[-1])
    near = flip(own, first_axis)
    far = flip(own, second_axis)
    both = flip(near, second_axis)
    return (own, near, far, both) if first_axis == "tx" else (own, far, near, both)


def reduce_slabs(slabs, depth, first_axis):
    own, by_x, by_y, by_both = slabs
    if first_axis == "cy":
        got_own, got_other = flip(by_y, "cy"), flip(by_both, "cy")
        keep, give, second_axis = own, by_x, "tx"
    else:
        got_own, got_other = flip(by_x, "tx"), flip(by_both, "tx")
        keep, give, second_axis = own, by_y, "cy"
    give = (give.astype(F32) + got_other.astype(F32)).astype(BF16)
    keep = keep.astype(F32) + got_own.astype(F32)
    total = (keep + flip(give, second_axis).astype(F32)).astype(BF16)
    pieces = total.reshape(depth, -1, total.shape[-1])
    return lax.all_to_all(pieces, "tz", 0, 0, tiled=True).astype(F32).sum(axis=0)


def butterfly(array, axes):
    for axis in axes:
        size = lax.axis_size(axis)
        bit = 1
        while bit < size:
            array = array + lax.ppermute(array, axis, [(i, i ^ bit) for i in range(size)])
            bit *= 2
    return array


def shards(
    h_in,
    cotangent,
    carried,
    centres,
    sticky,
    flags,
    w_qkv,
    w_qkv_first,
    w_qkv_second,
    w_out_t,
    w_out_first,
    w_out_second,
    w_up,
    w_up_first,
    w_up_second,
    w_down_t,
    w_down_first,
    w_down_second,
    vec_d,
    vec_d_first,
    vec_d_second,
    vec_c,
    vec_c_first,
    vec_c_second,
):
    depth = lax.axis_size("tz")
    tok_count = depth * 2
    ch_count = 2 * lax.axis_size("cc")
    context = lax.axis_index("cy")
    core = lax.axis_index("cc")
    x_place = lax.axis_index("tx")
    block_rows = w_qkv.shape[2]
    width = w_qkv.shape[1 + 2] * 1
    features = h_in.shape[1]
    half = features // 2
    rows = h_in.shape[0] // 2
    hidden_own = w_up.shape[2]

    place = jnp.arange(features)
    turned = place // half
    block_z = (place % half) // block_rows
    source = block_z * (2 * block_rows) + jnp.where(
        turned == 0, x_place, 1 - x_place
    ) * block_rows + place % block_rows
    order = (jnp.arange(features)[:, None] == source[None, :]).astype(BF16)
    order_wide = order.astype(F32)

    table_index = jnp.where(context == 0, core, 2)
    sticky_row = lax.dynamic_index_in_dim(sticky[0], table_index, 0, keepdims=False)
    table_own = make_tables(centres, sticky_row)
    table_other = flip(table_own, "cc")
    table_near = jnp.where(core == 0, table_own, table_other)
    table_far = jnp.where(core == 0, table_other, table_own)
    a_near, b_near = table_near[:, :BASIS], table_near[:, BASIS:]
    a_far, b_far = table_far[:, :BASIS], table_far[:, BASIS:]

    slabs = []
    for layer in range(LAYERS):
        attn_shard = jnp.concatenate(
            [w_qkv[layer, 0], w_qkv[layer, 1], w_qkv[layer, 2], w_out_t[layer]], axis=1
        ).astype(BF16)
        ffn_shard = jnp.concatenate([w_up[layer], w_down_t[layer]], axis=1).astype(BF16)
        slabs.append(
            (
                all_gather_slabs(attn_shard, depth, "tx", "cy"),
                all_gather_slabs(ffn_shard, depth, "cy", "tx"),
            )
        )

    def whole(parts, low, high):
        own, by_x, by_y, by_both = parts
        return (
            jnp.concatenate([own[:, low:high], by_x[:, low:high]], axis=0),
            jnp.concatenate([by_y[:, low:high], by_both[:, low:high]], axis=0),
        )

    vec_c_other = flip(vec_c, "cy")
    gains = jnp.dot(
        vec_d.reshape(-1, features), order_wide, precision=PRECISE
    ).reshape(vec_d.shape)
    flag_on = flags[0] > 0
    carried_own = carried[:, 0].reshape(LAYERS, BASIS, 2, width)
    carried_other = flip(carried_own, "cy")
    starts = jnp.stack([carried_own, carried_other], axis=3).reshape(LAYERS, BASIS, 4 * width)
    starts = jnp.where(flag_on, starts, jnp.zeros_like(starts))
    memory_bias = jnp.stack(
        [jnp.where((context == 0) & ~flag_on, MASKED, 0.0), jnp.float32(0.0)]
    ).astype(F32)

    own_h = lax.dynamic_slice_in_dim(h_in, context * rows, rows, axis=0)
    own_cot = lax.dynamic_slice_in_dim(cotangent, context * rows, rows, axis=0)
    stream = jnp.dot(own_h, order, preferred_element_type=F32)
    stream_grad = jnp.dot(own_cot, order, preferred_element_type=F32)

    saved = []
    for layer in range(LAYERS):
        attn_slabs, ffn_slabs = slabs[layer]
        wq, wk, wv = (whole(attn_slabs, i * width, (i + 1) * width) for i in range(3))
        w_in = jnp.concatenate([*wq, *wk, *wv], axis=1)
        w_out = jnp.concatenate(whole(attn_slabs, 3 * width, 4 * width), axis=1)
        w_big = jnp.concatenate(whole(ffn_slabs, 0, hidden_own), axis=1)
        w_small = jnp.concatenate(whole(ffn_slabs, hidden_own, 2 * hidden_own), axis=1)
        gain = gains[layer]
        bias_own, bias_other = vec_c[layer], vec_c_other[layer]
        zeros = jnp.zeros((2 * width,), F32)
        in_bias = jnp.concatenate(
            [bias_own[0], bias_other[0], zeros, bias_own[1], bias_other[1]]
        )
        up_bias = jnp.concatenate([bias_own[2:6].T.reshape(-1), bias_other[2:6].T.reshape(-1)])

        normed = layer_norm(stream, gain[0], gain[1]).astype(BF16)
        qkv = (dot(normed, w_in, NN) + in_bias).astype(BF16)
        signal = qkv[:, 2 * width :].reshape(2, SEG, 4 * width)
        fit_near = dot(b_near, signal[0], NN)
        fit_far = dot(b_far, signal[1], NN)
        ahead = dot(a_near, starts[layer], NN) + fit_near
        ahead = (dot(a_far, ahead.astype(BF16), NN) + fit_far).astype(BF16)
        received = lax.ppermute(swap_halves(ahead), "cy", ((0, 1),))
        memory_first = jnp.where(context == 0, starts[layer], received)
        memory_second = (dot(a_near, memory_first, NN) + fit_near).astype(BF16)
        memory = jnp.stack([memory_first, memory_second])
        attended, log_totals = attention_forward(qkv, memory, memory_bias)
        branch = pair_sum(dot(attended, w_out, NT))
        middle = stream + (branch + gain[4])
        normed_two = layer_norm(middle, gain[2], gain[3]).astype(BF16)
        hidden = dot(normed_two, w_big, NN) + up_bias
        active = jax.nn.gelu(hidden, approximate=True).astype(BF16)
        mixed = pair_sum(dot(active, w_small, NT))
        saved.append(
            (
                (w_in, w_out, w_big, w_small),
                stream,
                normed,
                qkv,
                memory,
                log_totals,
                attended,
                middle,
                normed_two,
                hidden,
                active,
            )
        )
        stream = middle + (mixed + gain[5])

    def gathered_rows(array):
        own = lax.optimization_barrier(array.astype(BF16))
        other = flip(own, "cy")
        both = jnp.where(
            context == 0,
            jnp.concatenate([own, other], axis=0),
            jnp.concatenate([other, own], axis=0),
        )
        return dot(both, order, NT)

    activations = gathered_rows(stream)

    vector_d = [None] * LAYERS
    vector_own = [None] * LAYERS
    vector_other = [None] * LAYERS
    reduced = [None] * LAYERS

    def grad_slabs(left, right):
        columns = right.shape[1] // 2
        return [
            dot(left[:, low : low + half], right[:, col : col + columns], TN).astype(BF16)
            for low, col in ((0, 0), (half, 0), (0, columns), (half, columns))
        ]

    for layer in reversed(range(LAYERS)):
        (
            (w_in, w_out, w_big, w_small),
            stream,
            normed,
            qkv,
            memory,
            log_totals,
            attended,
            middle,
            normed_two,
            hidden,
            active,
        ) = saved[layer]
        gain = gains[layer]
        down = stream_grad.astype(BF16)
        grad_down_bias = jnp.sum(down.astype(F32), axis=0)
        active_grad = dot(down, w_small, NN)
        _, gelu_back = jax.vjp(partial(jax.nn.gelu, approximate=True), hidden)
        hidden_grad = gelu_back(active_grad)[0].astype(BF16)
        grad_up_bias = jnp.sum(hidden_grad.astype(F32), axis=0)
        normed_two_grad = pair_sum(dot(hidden_grad, w_big, NT))
        down_slabs = grad_slabs(down, active)
        up_slabs = grad_slabs(normed_two, hidden_grad)
        reduced_down = reduce_slabs(down_slabs, depth, "cy")
        reduced_up = reduce_slabs(up_slabs, depth, "tx")
        middle_grad, grad_gain_two, grad_shift_two = norm_backward(
            middle, normed_two_grad, gain[2]
        )
        stream_grad = stream_grad + middle_grad
        branch_grad = stream_grad.astype(BF16)
        grad_out_bias = jnp.sum(branch_grad.astype(F32), axis=0)
        attended_grad = dot(branch_grad, w_out, NN).astype(BF16)
        out_slabs = grad_slabs(branch_grad, attended)
        reduced_out = reduce_slabs(out_slabs, depth, "cy")
        dq, dk, dv, dmk, dmv = attention_backward(
            qkv, memory, memory_bias, log_totals, attended, attended_grad
        )
        memory_grad = jnp.concatenate([dmk, dmv], axis=2)
        back = memory_grad[0] + dot(a_near, memory_grad[1].astype(BF16), TN)
        received = lax.ppermute(swap_halves(back.astype(BF16)), "cy", ((1, 0),))
        carry = (memory_grad[1] + dot(a_far, received, TN)).astype(BF16)
        signal_grad = jnp.concatenate([dot(b_near, carry, TN), dot(b_far, received, TN)], axis=0)
        dk = (dk + signal_grad[:, : 2 * width]).astype(BF16)
        dv = (dv + signal_grad[:, 2 * width :]).astype(BF16)
        grads_in = jnp.concatenate([dq, dk, dv], axis=1)
        normed_grad = pair_sum(dot(grads_in, w_in, NT))
        grad_query_bias = jnp.sum(dq.astype(F32), axis=0)
        grad_value_bias = jnp.sum(dv.astype(F32), axis=0)
        in_slabs = [grad_slabs(normed, member) for member in (dq, dk, dv)]
        in_slabs = [
            jnp.concatenate([in_slabs[i][j] for i in range(3)], axis=1) for j in range(4)
        ]
        reduced_in = reduce_slabs(in_slabs, depth, "tx")
        input_part, grad_gain_one, grad_shift_one = norm_backward(stream, normed_grad, gain[0])
        stream_grad = stream_grad + input_part
        vector_d[layer] = jnp.stack(
            [
                grad_gain_one,
                grad_shift_one,
                grad_gain_two,
                grad_shift_two,
                grad_out_bias,
                grad_down_bias,
            ]
        )
        ups = grad_up_bias.reshape(2, width, 4).transpose(0, 2, 1)
        pieces = [
            jnp.concatenate(
                [
                    grad_query_bias[None, side * width : (side + 1) * width],
                    grad_value_bias[None, side * width : (side + 1) * width],
                    ups[side],
                ],
                axis=0,
            )
            for side in range(2)
        ]
        vector_own[layer], vector_other[layer] = pieces
        reduced[layer] = (
            reduced_in.reshape(block_rows, 3, width).transpose(1, 0, 2),
            reduced_out,
            reduced_up,
            reduced_down,
        )
    input_grad = gathered_rows(stream_grad)

    matrix_grads = tuple(
        jnp.stack([reduced[layer][member] for layer in range(LAYERS)]) for member in range(4)
    )
    vec_d_grad = jnp.dot(
        jnp.stack(vector_d).reshape(-1, features), order_wide.T, precision=PRECISE
    ).reshape(-1)
    own_c = jnp.stack(vector_own).reshape(-1)
    other_c = jnp.stack(vector_other).reshape(-1)
    arrived = flip(jnp.concatenate([vec_d_grad, other_c]), "cy")
    vector = jnp.concatenate([vec_d_grad, own_c]) + arrived
    vector = butterfly(vector, ("tx", "tz"))
    vec_d_grad = vector[: vec_d.size].reshape(vec_d.shape)
    vec_c_grad = vector[vec_d.size :].reshape(vec_c.shape)

    square = sum(jnp.sum(grad * grad) for grad in matrix_grads)
    square = (
        square
        + jnp.sum(vec_d_grad * vec_d_grad) / (tok_count * ch_count)
        + jnp.sum(vec_c_grad * vec_c_grad) / tok_count
    )
    total_square = butterfly(jnp.full((8, 128), square), ("cc", "cy", "tx", "tz"))[0, 0]
    grad_norm = jnp.sqrt(total_square)
    factor = CLIP_LIMIT / jnp.maximum(grad_norm, CLIP_LIMIT)
    attention_update = adamw(
        w_qkv, w_qkv_first, w_qkv_second, matrix_grads[0] * factor, RATE_QKV, WEIGHT_DECAY
    )
    output_update = adamw(
        w_out_t, w_out_first, w_out_second, matrix_grads[1] * factor, RATE_OUT, WEIGHT_DECAY
    )
    expand_update = adamw(
        w_up, w_up_first, w_up_second, matrix_grads[2] * factor, RATE_UP, WEIGHT_DECAY
    )
    reduce_update = adamw(
        w_down_t, w_down_first, w_down_second, matrix_grads[3] * factor, RATE_DOWN, WEIGHT_DECAY
    )
    width_update = adamw(vec_d, vec_d_first, vec_d_second, vec_d_grad * factor, RATE_VECTOR, 0.0)
    channel_update = adamw(vec_c, vec_c_first, vec_c_second, vec_c_grad * factor, RATE_VECTOR, 0.0)
    return (
        activations,
        input_grad,
        grad_norm,
        *attention_update,
        *output_update,
        *expand_update,
        *reduce_update,
        *width_update,
        *channel_update,
    )


def solution(mesh):
    tok, ch = mesh.shape["tok"], mesh.shape["ch"]
    fine = Mesh(mesh.devices.reshape(tok // 2, 2, 2, ch // 2), ("tz", "tx", "cy", "cc"))
    t, c = ("tz", "tx"), ("cy", "cc")
    cube = P(None, None, t, c)
    matrix = P(None, t, c)
    channel = P(None, None, c)
    return jax.shard_map(
        shards,
        mesh=fine,
        in_specs=(
            P(t, None),
            P(t, None),
            P(None, t, None, None, c),
            P(),
            P(t, None, None),
            P(t),
            *(cube,) * 3,
            *(matrix,) * 9,
            *(P(),) * 3,
            *(channel,) * 3,
        ),
        out_specs=(
            P(t, None),
            P(t, None),
            P(),
            *(cube,) * 3,
            *(matrix,) * 9,
            *(P(),) * 3,
            *(channel,) * 3,
        ),
        check_vma=False,
    )
```

```python
from functools import partial
from typing import NamedTuple

import jax
import jax.numpy as jnp
from jax import lax
from jax.experimental import pallas as pl
from jax.experimental.pallas import tpu as pltpu
from jax.sharding import Mesh
from jax.sharding import PartitionSpec as P

HEAD_DIM = 64
BASIS = 256
SAMPLES = 256
SEG = 512
SEGS = 4
CRES = 1024
LAYERS = 2
STEP = 10

PRECISE = lax.Precision.HIGHEST
STICKY_RATIO = 0.5
RIDGE_WEIGHT = 0.5
BASIS_WIDTH = 0.01
NORM_EPS = 1e-05
CLIP_LIMIT = 1.0
FIRST_DECAY = 0.9
SECOND_DECAY = 0.95
ADAM_EPS = 1e-08
WEIGHT_DECAY = 0.1
RATE_QKV = 0.05
RATE_OUT = 0.5
RATE_UP = 0.05
RATE_DOWN = 0.03
RATE_VECTOR = 0.5
MASKED = -1e30
GELU_A = 0.7978845608028654
GELU_B = 0.044715
F32 = jnp.float32
BF16 = jnp.bfloat16
SWAP = ((0, 1), (1, 0))
NN = (((1,), (0,)), ((), ()))
NT = (((1,), (1,)), ((), ()))
TN = (((0,), (0,)), ((), ()))


def dot(left, right, dims, precision=None):
    return lax.dot_general(left, right, dims, precision=precision, preferred_element_type=F32)


VMEM_LIMIT = 56 * 2**20
TILE = 256
QT = 256


def cost(micros):
    return pl.CostEstimate(flops=int(micros * 1.1e9), bytes_accessed=10**6, transcendentals=0)


def table_kernel(old_ref, design_ref, out_ref, inv_ref, gram_ref):
    design = design_ref[...]
    eye = (
        lax.broadcasted_iota(jnp.int32, (BASIS, BASIS), 0)
        == lax.broadcasted_iota(jnp.int32, (BASIS, BASIS), 1)
    ).astype(F32)
    gram = dot(design, design, NT, PRECISE) + RIDGE_WEIGHT * eye
    gram_ref[...] = gram
    bound = jnp.max(jnp.sum(jnp.abs(gram), axis=0))
    inv_ref[...] = eye * (1.0 / bound)

    def step(low):
        scale = 2.0 / (1.0 + low)
        now = inv_ref[...]
        inner = dot(gram_ref[...], now, NN, PRECISE)
        inv_ref[...] = scale * (2.0 * now - scale * dot(now, inner, NN, PRECISE))
        return 4.0 * low / ((1.0 + low) * (1.0 + low))

    lax.while_loop(lambda low: low < 0.999, step, 0.99 * RIDGE_WEIGHT / bound)
    for _ in range(2):
        now = inv_ref[...]
        inner = dot(gram_ref[...], now, NN, PRECISE)
        inv_ref[...] = 2.0 * now - dot(now, inner, NN, PRECISE)
    fitted = dot(inv_ref[...], design, NN, PRECISE)
    out_ref[:, BASIS:] = fitted[:, SAMPLES:].astype(BF16)
    out_ref[:, :BASIS] = dot(fitted[:, :SAMPLES], old_ref[...], NT, PRECISE).astype(BF16)


def basis_table(centres, times):
    middle = (centres.astype(F32) + 0.5) / CRES
    offset = (times[None, :] - middle[:, None]) / BASIS_WIDTH
    return jnp.exp(-0.5 * offset * offset)


def make_tables(centres, sticky_row):
    token_times = STICKY_RATIO + (1.0 - STICKY_RATIO) * (jnp.arange(SEG).astype(F32) + 0.5) / SEG
    places = (sticky_row.astype(F32) + 0.5) / CRES
    old_basis = basis_table(centres, places)
    design = basis_table(centres, jnp.concatenate([STICKY_RATIO * places, token_times]))
    return pl.pallas_call(
        table_kernel,
        out_shape=jax.ShapeDtypeStruct((BASIS, BASIS + SEG), BF16),
        scratch_shapes=[pltpu.VMEM((BASIS, BASIS), F32), pltpu.VMEM((BASIS, BASIS), F32)],
        compiler_params=pltpu.CompilerParams(vmem_limit_bytes=VMEM_LIMIT),
        cost_estimate=cost(40),
    )(old_basis, design)


def slab_columns(slab, low, high):
    return slab[:, low:high] if len(slab.shape) == 2 else slab[0, 0, :, low:high]


def project(left, slabs, low, high):
    own, by_x, by_y, by_both = (slab_columns(slab, low, high) for slab in slabs)
    half = own.shape[0]
    first, second = left[:, :half], left[:, half:]
    return (
        dot(first, own, NN) + dot(second, by_x, NN),
        dot(first, by_y, NN) + dot(second, by_both, NN),
    )


def unproject(sides, slabs, low, high):
    own, by_x, by_y, by_both = (slab_columns(slab, low, high) for slab in slabs)
    return jnp.concatenate(
        [
            dot(sides[0], own, NT) + dot(sides[1], by_y, NT),
            dot(sides[0], by_x, NT) + dot(sides[1], by_both, NT),
        ],
        axis=1,
    )


def split_attention(refs, width):
    if len(refs[0].shape) == 2:
        return (refs[:4], 0), (refs[4:8], 0), refs[8:]
    return (refs[:4], 0), (refs[:4], 2 * width), refs[4:]


def split_ffn(refs):
    if len(refs[0].shape) == 2:
        return (refs[:4], 0), (refs[4:8], 0), refs[8:]
    return (refs[:4], 0), (refs[:4], refs[0].shape[-1] // 2), refs[4:]


TURNS = ((0, 0), (0, 1), (1, 0), (1, 1))


def cast_kernel(count, out_ref_index, *refs):
    out_ref = refs[out_ref_index]
    start = 0
    for ref in refs[:count]:
        for index in range(ref.shape[1]):
            columns = ref.shape[3]
            out_ref[:, start : start + columns] = ref[0, index].astype(BF16)
            start += columns


def cast(members, after=()):
    members = [
        (weight if weight.ndim == 4 else weight[:, None], layer) for weight, layer in members
    ]
    rows = members[0][0].shape[2]
    columns = sum(weight.shape[1] * weight.shape[3] for weight, _ in members)
    return pl.pallas_call(
        partial(cast_kernel, len(members), len(members) + len(after)),
        grid=(1,),
        in_specs=[
            pl.BlockSpec((1,) + weight.shape[1:], lambda i, layer=layer: (layer, 0, 0, 0))
            for weight, layer in members
        ]
        + [pl.BlockSpec(memory_space=pl.ANY)] * len(after),
        out_specs=pl.BlockSpec((rows, columns), lambda i: (0, 0)),
        out_shape=array((rows, columns), BF16),
        compiler_params=pltpu.CompilerParams(vmem_limit_bytes=VMEM_LIMIT),
        cost_estimate=cost(1),
    )(*(weight for weight, _ in members), *after)


def split_kernel(count, rows_ref, *refs):
    start = 0
    outs = refs[len(refs) - count - 1 :]
    for out_ref in outs[:count]:
        columns = out_ref.shape[1]
        out_ref[...] = rows_ref[:, start : start + columns]
        start += columns
    outs[count][...] = jnp.zeros_like(outs[count])


def split_columns(rows, widths, after):
    vmem = pl.BlockSpec(memory_space=pltpu.VMEM)
    *groups, zero = pl.pallas_call(
        partial(split_kernel, len(widths)),
        in_specs=[vmem] + [pl.BlockSpec(memory_space=pl.ANY)] * len(after),
        out_specs=[vmem] * (len(widths) + 1),
        out_shape=[array((rows.shape[0], columns), rows.dtype) for columns in widths]
        + [array((8, 128), jnp.int32)],
        compiler_params=pltpu.CompilerParams(vmem_limit_bytes=VMEM_LIMIT),
        cost_estimate=cost(1),
    )(rows, *after)
    return groups, zero[0, 0]


def pass_kernel(keep_a_ref, got_a_ref, keep_b_ref, got_b_ref, *refs):
    for keep_ref, got_ref, out_ref in (
        (keep_a_ref, got_a_ref, refs[-2]),
        (keep_b_ref, got_b_ref, refs[-1]),
    ):
        out_ref[...] = (keep_ref[0].astype(F32) + got_ref[0].astype(F32)).astype(BF16)


def pass_on(keep_a, got_a, keep_b, got_b, after):
    def slab(a):
        return pl.BlockSpec((1,) + a.shape[1:], lambda i: (1, 0, 0))

    def out(a):
        return pl.BlockSpec(a.shape[1:], lambda i: (0, 0))

    return pl.pallas_call(
        pass_kernel,
        grid=(1,),
        in_specs=[slab(a) for a in (keep_a, got_a, keep_b, got_b)]
        + [pl.BlockSpec(memory_space=pl.ANY)] * len(after),
        out_specs=[out(keep_a), out(keep_b)],
        out_shape=[array(keep_a.shape[1:], BF16), array(keep_b.shape[1:], BF16)],
        compiler_params=pltpu.CompilerParams(vmem_limit_bytes=VMEM_LIMIT),
        cost_estimate=cost(2),
    )(keep_a, got_a, keep_b, got_b, *after)


class Gathered(NamedTuple):
    whole: jax.Array
    columns: int
    index: int


def slab_operands(slabs, grid_rank):
    def fixed(shape):
        return pl.BlockSpec(shape, lambda *a: (0,) * len(shape))

    if not isinstance(slabs, Gathered):
        return list(slabs), [fixed(slab.shape) for slab in slabs]
    whole, columns, index = slabs
    specs = []
    for turn_y, turn_x in TURNS:
        specs.append(
            pl.BlockSpec(
                (1, 1, whole.shape[2], columns),
                lambda *a, turn_y=turn_y, turn_x=turn_x: (
                    a[grid_rank][0] ^ turn_y,
                    a[grid_rank][1] ^ turn_x,
                    0,
                    index,
                ),
            )
        )
    return [whole] * 4, specs


def norm_stats(inputs):
    centred = inputs - jnp.mean(inputs, axis=-1, keepdims=True)
    variance = jnp.mean(centred * centred, axis=-1, keepdims=True)
    rstd = lax.rsqrt(variance + NORM_EPS)
    return centred * rstd, rstd


def norm_backward(inputs, grad, gain_row):
    unit, rstd = norm_stats(inputs)
    scaled = grad * gain_row
    back = rstd * (
        scaled
        - jnp.mean(scaled, axis=-1, keepdims=True)
        - unit * jnp.mean(scaled * unit, axis=-1, keepdims=True)
    )
    return back, grad * unit


def both_parts(own_ref, got_ref):
    return own_ref[...].astype(F32) + got_ref[...].astype(F32)


def add_rows(ref, rows):
    @pl.when(pl.program_id(0) == 0)
    def _():
        ref[...] = jnp.zeros_like(ref)

    for index, row in rows:
        ref[index : index + 1, :] += jnp.sum(row, axis=0, keepdims=True)


def rows_call(
    kernel, place, tiled, whole, slabs, more, tiled_outs, whole_outs, micros, scratch=(), after=()
):
    rows = tiled[0].shape[-2]

    def tile_spec(shape):
        if len(shape) == 2:
            return pl.BlockSpec((TILE, shape[1]), lambda i, p: (i, 0))
        return pl.BlockSpec((shape[0], TILE, shape[2]), lambda i, p: (0, i, 0))

    def whole_spec(shape):
        return pl.BlockSpec(shape, lambda i, p: (0,) * len(shape))

    slab_arrays, slab_specs = slab_operands(slabs, 1) if slabs is not None else ([], [])

    taken = len(tiled) + len(whole) + len(slab_arrays) + len(more)

    def body(place_ref, *refs):
        kernel(*refs[:taken], *refs[taken + len(after) :])

    return pl.pallas_call(
        body,
        grid_spec=pltpu.PrefetchScalarGridSpec(
            num_scalar_prefetch=1,
            grid=(rows // TILE,),
            in_specs=[tile_spec(a.shape) for a in tiled]
            + [whole_spec(a.shape) for a in whole]
            + slab_specs
            + [whole_spec(a.shape) for a in more]
            + [pl.BlockSpec(memory_space=pl.ANY)] * len(after),
            out_specs=[tile_spec(a.shape) for a in tiled_outs]
            + [whole_spec(a.shape) for a in whole_outs],
            scratch_shapes=list(scratch),
        ),
        out_shape=[*tiled_outs, *whole_outs],
        compiler_params=pltpu.CompilerParams(vmem_limit_bytes=VMEM_LIMIT),
        cost_estimate=cost(micros),
    )(place, *tiled, *whole, *slab_arrays, *more, *after)


def array(shape, dtype):
    return jax.ShapeDtypeStruct(shape, dtype)


def enter_kernel(layer, *refs):
    if layer == 0:
        h_ref, order_ref, gains_ref, bias_ref, *refs = refs
        stream = dot(h_ref[...], order_ref[...], NN)
    else:
        middle_ref, own_ref, got_ref, gains_ref, bias_ref, *refs = refs
        stream = middle_ref[...] + (both_parts(own_ref, got_ref) + gains_ref[layer - 1, 5:6, :])
    width = refs[-4].shape[2] // 3
    slabs_qk, slabs_vo, refs = split_attention(refs, width)
    near_ref, far_ref, start_ref, *refs = refs
    stream_ref, normed_ref, qkv_ref, fit_ref, ahead_ref, signal_ref = refs
    step = pl.program_id(0)
    stream_ref[...] = stream
    unit, _ = norm_stats(stream)
    normed = (unit * gains_ref[layer, 0:1, :] + gains_ref[layer, 1:2, :]).astype(BF16)
    normed_ref[...] = normed
    rows = pl.ds(pl.multiple_of(step * TILE, TILE), TILE)
    low = slabs_qk[1]
    queries_keys = project(normed, slabs_qk[0], low, low + 2 * width)
    low = slabs_vo[1]
    values = project(normed, slabs_vo[0], low, low + width)
    for side in range(2):
        result = jnp.concatenate([queries_keys[side], values[side]], axis=1)
        result = (result + bias_ref[layer, side : side + 1, :]).astype(BF16)
        qkv_ref[side] = result
        signal_ref[side, rows, :] = result[:, width:]

    @pl.when(step == pl.num_programs(0) - 1)
    def _():
        for side in range(2):
            fit_near = dot(near_ref[:, BASIS:], signal_ref[side, :SEG, :], NN)
            fit_far = dot(far_ref[:, BASIS:], signal_ref[side, SEG:, :], NN)
            fit_ref[side] = fit_near
            ahead = dot(near_ref[:, :BASIS], start_ref[layer, side], NN) + fit_near
            ahead = dot(far_ref[:, :BASIS], ahead.astype(BF16), NN) + fit_far
            ahead_ref[side] = ahead.astype(BF16)


def ffn_forward_kernel(layer, stream_ref, own_ref, got_ref, gains_ref, bias_ref, *refs):
    (up, up_low), (down, down_low), refs = split_ffn(refs)
    middle_ref, normed_ref, active_ref, slope_ref, part_ref = refs
    hidden_own = active_ref.shape[2]
    middle = stream_ref[...] + (both_parts(own_ref, got_ref) + gains_ref[layer, 4:5, :])
    middle_ref[...] = middle
    unit, _ = norm_stats(middle)
    normed = (unit * gains_ref[layer, 2:3, :] + gains_ref[layer, 3:4, :]).astype(BF16)
    normed_ref[...] = normed
    sides = []
    for side, hidden in enumerate(project(normed, up, up_low, up_low + hidden_own)):
        hidden = hidden + bias_ref[layer, side : side + 1, :]
        square = hidden * hidden
        bend = jnp.tanh(hidden * (GELU_A + (GELU_A * GELU_B) * square))
        half_more = 0.5 + 0.5 * bend
        active = (hidden * half_more).astype(BF16)
        slope = half_more + (0.5 - 0.5 * bend * bend) * hidden * (
            GELU_A + (3.0 * GELU_A * GELU_B) * square
        )
        active_ref[side] = active
        slope_ref[side] = slope.astype(BF16)
        sides.append(active)
    part_ref[...] = unproject(sides, down, down_low, down_low + hidden_own).astype(BF16)


def ffn_backward_kernel(layer, *refs):
    if layer == LAYERS - 1:
        cot_ref, slope_ref, order_ref, *refs = refs
        (up_slabs, up_low), (down_slabs, down_low), refs = split_ffn(refs)
        stream_grad = dot(cot_ref[...], order_ref[...], NN)
        grad_ref, down_ref, hidden_ref, part_ref, sums_ref = refs
        sums = []
    else:
        before_ref, stream_ref, own_ref, got_ref, slope_ref, gains_ref, *refs = refs
        (up_slabs, up_low), (down_slabs, down_low), refs = split_ffn(refs)
        grad_ref, down_ref, hidden_ref, part_ref, sums_ref = refs
        normed_grad = both_parts(own_ref, got_ref)
        back, gain_rows = norm_backward(
            stream_ref[...], normed_grad, gains_ref[layer + 1, 0:1, :]
        )
        stream_grad = before_ref[...] + back
        sums = [(0, gain_rows), (1, normed_grad)]
    hidden_own = slope_ref.shape[2]
    grad_ref[...] = stream_grad
    down = stream_grad.astype(BF16)
    down_ref[...] = down
    sums.append((2, down.astype(F32)))
    sides = []
    for side, active_grad in enumerate(project(down, down_slabs, down_low, down_low + hidden_own)):
        hidden_grad = (active_grad * slope_ref[side].astype(F32)).astype(BF16)
        hidden_ref[side] = hidden_grad
        sums.append((3 + side, hidden_grad.astype(F32)))
        sides.append(hidden_grad)
    part_ref[...] = unproject(sides, up_slabs, up_low, up_low + hidden_own).astype(BF16)
    add_rows(sums_ref, sums)


def mix_backward_kernel(layer, before_ref, middle_ref, own_ref, got_ref, gains_ref, *refs):
    width = refs[-2].shape[2]
    slabs_qk, (slabs, low), refs = split_attention(refs, width)
    grad_ref, branch_ref, attended_ref, sums_ref = refs
    normed_grad = both_parts(own_ref, got_ref)
    back, gain_rows = norm_backward(middle_ref[...], normed_grad, gains_ref[layer, 2:3, :])
    stream_grad = before_ref[...] + back
    grad_ref[...] = stream_grad
    branch = stream_grad.astype(BF16)
    branch_ref[...] = branch
    for side, result in enumerate(project(branch, slabs, low + width, low + 2 * width)):
        attended_ref[side] = result.astype(BF16)
    add_rows(sums_ref, [(0, gain_rows), (1, normed_grad), (2, branch.astype(F32))])


def leave_kernel(before_ref, stream_ref, own_ref, got_ref, gains_ref, grad_ref, sums_ref):
    normed_grad = both_parts(own_ref, got_ref)
    back, gain_rows = norm_backward(stream_ref[...], normed_grad, gains_ref[0, 0:1, :])
    grad_ref[...] = (before_ref[...] + back).astype(BF16)
    add_rows(sums_ref, [(0, gain_rows), (1, normed_grad)])


def restore_kernel(context_ref, own_ref, got_ref, order_ref, *refs):
    out_ref = refs[-1]
    mine = (pl.program_id(0) // (pl.num_programs(0) // 2)) == context_ref[0]
    rows = jnp.where(mine, own_ref[...].astype(F32), got_ref[...].astype(F32)).astype(BF16)
    out_ref[...] = dot(rows, order_ref[...], NN)


def restore(own, got, order, context, after=()):
    rows, features = own.shape
    tiles = rows // TILE
    block = pl.BlockSpec((TILE, features), lambda i: (i % tiles, 0))
    return pl.pallas_call(
        restore_kernel,
        grid=(2 * tiles,),
        in_specs=[
            pl.BlockSpec(memory_space=pltpu.SMEM),
            block,
            block,
            pl.BlockSpec(order.shape, lambda i: (0, 0)),
            *(pl.BlockSpec(memory_space=pl.ANY) for _ in after),
        ],
        out_specs=pl.BlockSpec((TILE, features), lambda i: (i, 0)),
        out_shape=array((2 * rows, features), F32),
        compiler_params=pltpu.CompilerParams(vmem_limit_bytes=VMEM_LIMIT),
        cost_estimate=cost(4),
    )(context, own, got, order, *after)


def causal(shape):
    return lax.broadcasted_iota(jnp.int32, shape, 0) <= lax.broadcasted_iota(jnp.int32, shape, 1)


def head_lanes(kind, head, heads):
    low = (kind * heads + head) * HEAD_DIM
    return slice(low, low + HEAD_DIM)


def attention_forward_kernel(
    place_ref,
    bias_ref,
    qkv_ref,
    start_ref,
    got_ref,
    fit_ref,
    near_ref,
    *refs,
):
    slabs = refs[:4]
    out_ref, lse_ref, memory_ref, part_ref, rows_ref, total_ref = refs[-6:]
    segment, side = pl.program_id(0), pl.program_id(1)
    heads = qkv_ref.shape[2] // (3 * HEAD_DIM)
    width = heads * HEAD_DIM

    @pl.when(segment == 0)
    def _():
        @pl.when(place_ref[0] == 0)
        def _():
            rows_ref[side, 0] = start_ref[0, 0]

        @pl.when(place_ref[0] != 0)
        def _():
            rows_ref[side, 0] = got_ref[0]

        second = dot(near_ref[:, :BASIS], rows_ref[side, 0], NN) + fit_ref[0]
        rows_ref[side, 1] = second.astype(BF16)

    memory_ref[0, 0] = rows_ref[side, segment]
    memory_bias = bias_ref[segment]
    for tile in range(SEG // QT):
        rows = slice(tile * QT, (tile + 1) * QT)
        stacked = []
        for head in range(heads):
            lanes_q, lanes_k, lanes_v = (head_lanes(kind, head, heads) for kind in range(3))
            query = qkv_ref[0, rows, lanes_q] * HEAD_DIM ** (-0.5)
            scores = []
            values = []
            for part in range(tile + 1):
                keys = slice(part * QT, (part + 1) * QT)
                score = dot(qkv_ref[0, keys, lanes_k], query, NT)
                if part == tile:
                    score = jnp.where(causal(score.shape), score, MASKED)
                scores.append(score)
                values.append(qkv_ref[0, keys, lanes_v])
            memory_key = rows_ref[side, segment, :, head_lanes(0, head, heads)]
            scores.append(dot(memory_key, query, NT) + memory_bias)
            values.append(rows_ref[side, segment, :, head_lanes(1, head, heads)])
            top = scores[0].max(axis=0, keepdims=True)
            for score in scores[1:]:
                top = jnp.maximum(top, score.max(axis=0, keepdims=True))
            total = jnp.zeros_like(top)
            result = jnp.zeros((HEAD_DIM, QT), F32)
            for score, value in zip(scores, values):
                weight = jnp.exp(score - top)
                total = total + weight.sum(axis=0, keepdims=True)
                result = result + dot(value, weight.astype(BF16), TN)
            stacked.append(result / total)
            lse_ref[0, 0, head : head + 1, rows] = top + jnp.log(total)
        out_ref[0, rows, :] = jnp.concatenate(stacked, axis=0).T.astype(BF16)
    attended = out_ref[0]
    low = slabs[0].shape[-1] - width
    own, by_x, by_y, by_both = (slab_columns(slab, low, low + width) for slab in slabs)

    @pl.when(side == 0)
    def _():
        total_ref[...] = jnp.concatenate(
            [dot(attended, own, NT), dot(attended, by_x, NT)], axis=1
        )

    @pl.when(side == 1)
    def _():
        part = total_ref[...] + jnp.concatenate(
            [dot(attended, by_y, NT), dot(attended, by_both, NT)],
            axis=1,
        )
        part_ref[...] = part.astype(BF16)


def attention_forward(layer, place, memory_bias, qkv, starts, got, fit, near, slabs, after=()):
    rows = qkv.shape[1]
    width = qkv.shape[2] // 3
    heads = width // HEAD_DIM
    segs = rows // SEG
    slab_arrays, slab_specs = slab_operands(slabs, 2)
    features = 2 * slab_arrays[0].shape[-2]
    return pl.pallas_call(
        attention_forward_kernel,
        grid_spec=pltpu.PrefetchScalarGridSpec(
            num_scalar_prefetch=1,
            grid=(segs, 2),
            in_specs=[
                pl.BlockSpec(memory_space=pltpu.SMEM),
                pl.BlockSpec((1, SEG, 3 * width), lambda g, s, p: (s, g, 0)),
                pl.BlockSpec((1, 1, BASIS, 2 * width), lambda g, s, p: (layer, s, 0, 0)),
                pl.BlockSpec((1, BASIS, 2 * width), lambda g, s, p: (1 - s, 0, 0)),
                pl.BlockSpec((1, BASIS, 2 * width), lambda g, s, p: (s, 0, 0)),
                pl.BlockSpec(near.shape, lambda g, s, p: (0, 0)),
                *slab_specs,
                *(pl.BlockSpec(memory_space=pl.ANY) for _ in after),
            ],
            out_specs=[
                pl.BlockSpec((1, SEG, width), lambda g, s, p: (s, g, 0)),
                pl.BlockSpec((1, 1, heads, SEG), lambda g, s, p: (g, s, 0, 0)),
                pl.BlockSpec((1, 1, BASIS, 2 * width), lambda g, s, p: (g, s, 0, 0)),
                pl.BlockSpec((SEG, features), lambda g, s, p: (g, 0)),
            ],
            scratch_shapes=[
                pltpu.VMEM((2, segs, BASIS, 2 * width), BF16),
                pltpu.VMEM((SEG, features), F32),
            ],
        ),
        out_shape=[
            array((2, rows, width), BF16),
            array((segs, 2, heads, SEG), F32),
            array((segs, 2, BASIS, 2 * width), BF16),
            array((rows, features), BF16),
        ],
        compiler_params=pltpu.CompilerParams(vmem_limit_bytes=VMEM_LIMIT),
        cost_estimate=cost(13),
    )(place, memory_bias, qkv, starts, got, fit, near, *slab_arrays, *after)


def attention_backward_kernel(
    bias_ref,
    qkv_ref,
    memory_ref,
    lse_ref,
    out_ref,
    grad_ref,
    near_ref,
    *refs,
):
    dq_ref, dkv_ref, last_ref, back_ref, first_ref = refs[-5:]
    segment = pl.program_id(1)
    memory_bias = bias_ref[segment]
    heads = out_ref.shape[2] // HEAD_DIM
    scale = HEAD_DIM ** (-0.5)
    tiles = SEG // QT
    product = (out_ref[0].astype(F32) * grad_ref[0].astype(F32)).T
    query_grads = []
    for head in range(heads):
        lanes = head_lanes(0, head, heads)
        lanes_k, lanes_v = head_lanes(1, head, heads), head_lanes(2, head, heads)
        query = qkv_ref[0, :, lanes] * scale
        grad = grad_ref[0, :, lanes]
        dots = product[lanes, :].sum(axis=0, keepdims=True)
        log_total = lse_ref[0, 0, head : head + 1, :]
        head_grads = [jnp.zeros((HEAD_DIM, QT), F32) for _ in range(tiles)]
        for part in range(tiles + 1):
            if part < tiles:
                keys = slice(part * QT, (part + 1) * QT)
                key, value = qkv_ref[0, keys, lanes_k], qkv_ref[0, keys, lanes_v]
            else:
                key = memory_ref[0, 0, :, head_lanes(0, head, heads)]
                value = memory_ref[0, 0, :, head_lanes(1, head, heads)]
            key_grad = jnp.zeros((QT, HEAD_DIM), F32)
            value_grad = jnp.zeros((QT, HEAD_DIM), F32)
            for tile in range(part if part < tiles else 0, tiles):
                rows = slice(tile * QT, (tile + 1) * QT)
                score = dot(key, query[rows], NT)
                if part == tile:
                    score = jnp.where(causal(score.shape), score, MASKED)
                if part == tiles:
                    score = score + memory_bias
                weight = jnp.exp(score - log_total[:, rows])
                weight_grad = dot(value, grad[rows], NT)
                score_grad = (weight * (weight_grad - dots[:, rows])).astype(BF16)
                value_grad = value_grad + dot(weight.astype(BF16), grad[rows], NN)
                key_grad = key_grad + dot(score_grad, query[rows], NN)
                head_grads[tile] = head_grads[tile] + dot(key, score_grad, TN)
            if part < tiles:
                dkv_ref[0, keys, head_lanes(0, head, heads)] = key_grad
                dkv_ref[0, keys, head_lanes(1, head, heads)] = value_grad
            else:
                last_ref[0, :, head_lanes(0, head, heads)] = key_grad
                last_ref[0, :, head_lanes(1, head, heads)] = value_grad
        query_grads.append(jnp.concatenate(head_grads, axis=1) * scale)
    dq_ref[0] = jnp.concatenate(query_grads, axis=0).T.astype(BF16)

    @pl.when(segment == 0)
    def _():
        first_ref[...] = last_ref[0]

    @pl.when(segment == 1)
    def _():
        back = first_ref[...] + dot(near_ref[:, :BASIS], last_ref[0].astype(BF16), TN)
        back_ref[0] = back.astype(BF16)


def attention_backward(memory_bias, qkv, memory, log_totals, attended, grad, near, after):
    rows, width = attended.shape[1:]
    heads = width // HEAD_DIM
    segs = rows // SEG
    narrow = pl.BlockSpec((1, SEG, width), lambda s, g: (s, g, 0))
    side_block = pl.BlockSpec((1, BASIS, 2 * width), lambda s, g: (s, 0, 0))
    return pl.pallas_call(
        attention_backward_kernel,
        grid=(2, segs),
        in_specs=[
            pl.BlockSpec(memory_space=pltpu.SMEM),
            pl.BlockSpec((1, SEG, 3 * width), lambda s, g: (s, g, 0)),
            pl.BlockSpec((1, 1, BASIS, 2 * width), lambda s, g: (g, s, 0, 0)),
            pl.BlockSpec((1, 1, heads, SEG), lambda s, g: (g, s, 0, 0)),
            narrow,
            narrow,
            pl.BlockSpec(near.shape, lambda s, g: (0, 0)),
            *(pl.BlockSpec(memory_space=pl.ANY) for _ in after),
        ],
        out_specs=[
            narrow,
            pl.BlockSpec((1, SEG, 2 * width), lambda s, g: (s, g, 0)),
            side_block,
            side_block,
        ],
        out_shape=[
            array((2, rows, width), BF16),
            array((2, rows, 2 * width), F32),
            array((2, BASIS, 2 * width), F32),
            array((2, BASIS, 2 * width), BF16),
        ],
        scratch_shapes=[pltpu.VMEM((BASIS, 2 * width), F32)],
        compiler_params=pltpu.CompilerParams(vmem_limit_bytes=VMEM_LIMIT),
        cost_estimate=cost(18),
    )(memory_bias, qkv, memory, log_totals, attended, grad, near, *after)


def memory_backward_kernel(
    place_ref,
    dq_ref,
    dkv_ref,
    last_ref,
    got_ref,
    near_ref,
    far_ref,
    *refs,
):
    width = dq_ref.shape[2]
    slabs_qk, slabs_vo, refs = split_attention(refs, width)
    grads_ref, part_ref, sums_ref, signal_ref = refs[-4:]
    segment = pl.program_id(0)

    @pl.when(segment == 0)
    def _():
        for side in range(2):
            carry = last_ref[side] + dot(far_ref[:, :BASIS], got_ref[1 - side], TN)
            signal_ref[side] = dot(near_ref[:, BASIS:], carry.astype(BF16), TN)

    @pl.when(segment == 1)
    def _():
        for side in range(2):
            signal_ref[side] = dot(far_ref[:, BASIS:], got_ref[1 - side], TN)

    sides = []
    for side in range(2):
        grads_ref[side, :, :width] = dq_ref[side]
        grads_ref[side, :, width:] = (dkv_ref[side] + signal_ref[side]).astype(BF16)
        sides.append(grads_ref[side])
    slabs, low = slabs_qk
    part = unproject([side[:, : 2 * width] for side in sides], slabs, low, low + 2 * width)
    slabs, low = slabs_vo
    part = part + unproject([side[:, 2 * width :] for side in sides], slabs, low, low + width)
    part_ref[...] = part.astype(BF16)
    add_rows(sums_ref, [(side, sides[side].astype(F32)) for side in range(2)])


def memory_backward(place, dq, dkv, last, got, near, far, slabs, after):
    rows, width = dq.shape[1:]
    slab_arrays, slab_specs = slab_operands(slabs, 1)
    features = 2 * slab_arrays[0].shape[-2]
    whole = lambda a: pl.BlockSpec(a.shape, lambda g, p: (0,) * a.ndim)
    return pl.pallas_call(
        memory_backward_kernel,
        grid_spec=pltpu.PrefetchScalarGridSpec(
            num_scalar_prefetch=1,
            grid=(rows // SEG,),
            in_specs=[
                pl.BlockSpec((2, SEG, width), lambda g, p: (0, g, 0)),
                pl.BlockSpec((2, SEG, 2 * width), lambda g, p: (0, g, 0)),
                *(whole(a) for a in (last, got, near, far)),
                *slab_specs,
                *(pl.BlockSpec(memory_space=pl.ANY) for _ in after),
            ],
            out_specs=[
                pl.BlockSpec((2, SEG, 3 * width), lambda g, p: (0, g, 0)),
                pl.BlockSpec((SEG, features), lambda g, p: (g, 0)),
                pl.BlockSpec((8, 3 * width), lambda g, p: (0, 0)),
            ],
            scratch_shapes=[pltpu.VMEM((2, SEG, 2 * width), F32)],
        ),
        out_shape=[
            array((2, rows, 3 * width), BF16),
            array((rows, features), BF16),
            array((8, 3 * width), F32),
        ],
        compiler_params=pltpu.CompilerParams(vmem_limit_bytes=VMEM_LIMIT),
        cost_estimate=cost(5),
    )(place, dq, dkv, last, got, near, far, *slab_arrays, *after)


def weight_grads_kernel(plan, *refs):
    outs = refs[len(refs) - len(plan) :]
    for out_ref, slabs in zip(outs, plan):
        half = out_ref.shape[1]
        for index, products in enumerate(slabs):
            start = 0
            for left, turn, right, side, low, high in products:
                columns = slice(turn * half, (turn + 1) * half)
                result = dot(refs[left][:, columns], refs[right][side, :, low:high], TN)
                out_ref[index, :, start : start + high - low] = result.astype(BF16)
                start += high - low


def weight_grads(operands, plan, half, after=()):
    shapes = [
        array((2, half, sum(high - low for *_, low, high in slabs[0])), BF16) for slabs in plan
    ]
    vmem = pl.BlockSpec(memory_space=pltpu.VMEM)
    return pl.pallas_call(
        partial(weight_grads_kernel, plan),
        in_specs=[vmem] * len(operands) + [pl.BlockSpec(memory_space=pl.ANY)] * len(after),
        out_specs=[vmem] * len(plan),
        out_shape=shapes,
        compiler_params=pltpu.CompilerParams(vmem_limit_bytes=VMEM_LIMIT),
        cost_estimate=cost(6),
    )(*operands, *after)


GIVE_X = ((1, 0), (1, 1))
GIVE_Y = ((0, 1), (1, 1))
KEEP_X = ((0, 0), (0, 1))
KEEP_Y = ((0, 0), (1, 0))


def flip(array, axis):
    return lax.ppermute(array, axis, SWAP)


ALL_BUT_CORE = ("cy", "tx", "tz")


def gather_blocks(shard):
    whole = lax.all_gather(shard, ALL_BUT_CORE, axis=0, tiled=True)
    return whole.reshape(2, 2, -1, shard.shape[1])


def gather_z(shard):
    size = lax.axis_size("tz")
    spread = jnp.broadcast_to(shard[None], (size,) + shard.shape)
    return lax.all_to_all(spread, "tz", 0, 0, tiled=True).reshape(-1, shard.shape[1])


def gather_z_soon(shard):
    size = lax.axis_size("tz")
    here = lax.axis_index("tz")
    rows = jnp.zeros((size,) + shard.shape, shard.dtype)
    for bit in range(size):
        piece = shift(shard, "tz", bit) if bit else shard
        rows = lax.dynamic_update_index_in_dim(rows, piece, here ^ bit, 0)
    return rows.reshape(-1, shard.shape[1])


def shift(array, axis, bit):
    return lax.ppermute(array, axis, [(i, i ^ bit) for i in range(lax.axis_size(axis))])


def gather_second(two, axis):
    own, near = two
    far, both = flip(own, axis), flip(near, axis)
    return (own, far, near, both) if axis == "tx" else (own, near, far, both)


def pieces_of(parts, block_rows):
    total = jnp.concatenate(
        [sum(piece.astype(F32) for piece in three).astype(BF16) for three in parts], axis=1
    )
    return total.reshape(-1, block_rows, total.shape[-1])


def spread_pieces(pieces):
    return lax.all_to_all(pieces, "tz", 0, 0, tiled=True)


def butterfly(array, axes):
    for axis in axes:
        bit = 1
        while bit < lax.axis_size(axis):
            array = array + shift(array, axis, bit)
            bit *= 2
    return array


def adamw(weight, first, second, grad, rate, decay):
    first_new = FIRST_DECAY * first + (1.0 - FIRST_DECAY) * grad
    second_new = SECOND_DECAY * second + (1.0 - SECOND_DECAY) * grad * grad
    first_hat = first_new / (1.0 - FIRST_DECAY**STEP)
    second_hat = second_new / (1.0 - SECOND_DECAY**STEP)
    weight_new = weight * (1.0 - rate * decay) - rate * first_hat / (
        jnp.sqrt(second_hat) + ADAM_EPS
    )
    return (weight_new, first_new, second_new)


def shards(
    h_in,
    cotangent,
    carried,
    centres,
    sticky,
    flags,
    w_qkv,
    w_qkv_first,
    w_qkv_second,
    w_out_t,
    w_out_first,
    w_out_second,
    w_up,
    w_up_first,
    w_up_second,
    w_down_t,
    w_down_first,
    w_down_second,
    vec_d,
    vec_d_first,
    vec_d_second,
    vec_c,
    vec_c_first,
    vec_c_second,
):
    depth = lax.axis_size("tz")
    tok_count = depth * 2
    ch_count = 2 * lax.axis_size("cc")
    context = lax.axis_index("cy")
    core = lax.axis_index("cc")
    x_place = lax.axis_index("tx")
    block_rows = w_qkv.shape[2]
    width = w_qkv.shape[1 + 2] * 1
    features = h_in.shape[1]
    half = features // 2
    rows = h_in.shape[0] // 2
    hidden_own = w_up.shape[2]

    table_index = jnp.where(context == 0, core, 2)
    sticky_row = lax.dynamic_index_in_dim(sticky[0], table_index, 0, keepdims=False)
    table_own = make_tables(centres, sticky_row)
    table_other = flip(table_own, "cc")
    table_near = jnp.where(core == 0, table_own, table_other)
    table_far = jnp.where(core == 0, table_other, table_own)

    def attention_members(layer):
        return [(w_qkv, layer), (w_out_t, layer)]

    def ffn_members(layer):
        return [(w_up, layer), (w_down_t, layer)]

    attn_shard = cast(attention_members(0))
    attn_rows = gather_z_soon(attn_shard)
    more_rows = gather_z(cast(ffn_members(0) + attention_members(1), (attn_shard,)))
    (qk_own, vo_own), zero = split_columns(attn_rows, (2 * width, 2 * width), (table_own,))
    qk_two, vo_two = (qk_own, flip(qk_own, "tx")), (vo_own, flip(vo_own, "cy"))
    (up_own, down_own, qk_above, vo_above), _ = split_columns(
        more_rows, (hidden_own, hidden_own, 2 * width, 2 * width), (qk_own,)
    )
    up_two, down_two = (up_own, flip(up_own, "tx")), (down_own, flip(down_own, "cy"))
    above_two = (qk_above, flip(qk_above, "tx")), (vo_above, flip(vo_above, "cy"))
    attn_slabs = [
        gather_second(qk_two, "cy") + gather_second(vo_two, "tx"),
        gather_second(above_two[0], "cy") + gather_second(above_two[1], "tx"),
    ]
    ffn_slabs = [
        gather_second(up_two, "cy") + gather_second(down_two, "tx"),
        Gathered(gather_blocks(cast(ffn_members(1), (up_own,))), 2 * hidden_own, 0),
    ]

    x_place = x_place + zero
    late_context = context + zero
    spot = jnp.arange(features)
    turned = spot // half
    block_z = (spot % half) // block_rows
    source = block_z * (2 * block_rows) + jnp.where(
        turned == 0, x_place, 1 - x_place
    ) * block_rows + spot % block_rows
    order = (jnp.arange(features)[:, None] == source[None, :]).astype(BF16)
    order_wide = order.astype(F32)
    order_back = (source[:, None] == jnp.arange(features)[None, :]).astype(BF16)
    place = jnp.stack([context, x_place]).astype(jnp.int32)

    vec_c_other = flip(vec_c, "cy")
    gains = jnp.dot(
        vec_d.reshape(-1, features), order_wide, precision=PRECISE
    ).reshape(vec_d.shape)
    both_c = jnp.stack([vec_c, vec_c_other], axis=1)
    in_bias = jnp.concatenate(
        [both_c[:, :, 0], jnp.zeros_like(both_c[:, :, 0]), both_c[:, :, 1]], axis=-1
    )
    up_bias = both_c[:, :, 2:6].transpose(0, 1, 3, 2).reshape(LAYERS, 2, hidden_own)
    flag_on = flags[0] + zero > 0
    carried_own = carried[:, 0].reshape(LAYERS, BASIS, 2 * width)
    starts = jnp.stack([carried_own, flip(carried_own, "cy")], axis=1)
    starts = jnp.where(flag_on, starts, jnp.zeros_like(starts))
    memory_bias = jnp.stack(
        [jnp.where((context == 0) & ~flag_on, MASKED, 0.0), jnp.float32(0.0)]
    ).astype(F32)
    own_h = lax.dynamic_slice_in_dim(h_in, late_context * rows, rows, axis=0)
    own_cot = lax.dynamic_slice_in_dim(cotangent, late_context * rows, rows, axis=0)

    row_f32 = array((rows, features), F32)
    row_b16 = array((rows, features), BF16)
    side_hidden = array((2, rows, hidden_own), BF16)
    side_width = array((2, rows, width), BF16)
    sums_shape = array((8, features), F32)

    saved = []
    for layer in range(LAYERS):
        stream, normed, qkv, fit, ahead = rows_call(
            partial(enter_kernel, layer),
            place,
            (own_h,) if layer == 0 else (middle, part, got),
            ((order,) if layer == 0 else ()) + (gains, in_bias),
            attn_slabs[layer],
            (table_near, table_far, starts),
            (row_f32, row_b16, array((2, rows, 3 * width), BF16)),
            (array((2, BASIS, 2 * width), F32), array((2, BASIS, 2 * width), BF16)),
            7,
            [pltpu.VMEM((2, rows, 2 * width), BF16)],
            after=(up_two[1], down_two[1]) if layer == 0 else (),
        )
        received = lax.ppermute(ahead, "cy", ((0, 1),))
        out_slabs = attn_slabs[layer][4:]
        attended, log_totals, memory, part = attention_forward(
            layer, place, memory_bias, qkv, starts, received, fit, table_near, out_slabs,
            after=ffn_slabs[0][1:4] + ffn_slabs[0][5:8] + (above_two[0][1], above_two[1][1])
            if layer == 0
            else (),
        )
        got = flip(part, "cc")
        middle, normed_two, active, slope, part = rows_call(
            partial(ffn_forward_kernel, layer),
            place,
            (stream, part, got),
            (gains, up_bias),
            ffn_slabs[layer],
            (),
            (row_f32, row_b16, side_hidden, side_hidden, row_b16),
            (),
            11,
        )
        got = flip(part, "cc")
        saved.append(
            (
                stream,
                normed,
                qkv,
                memory,
                log_totals,
                attended,
                middle,
                normed_two,
                active,
                slope,
            )
        )
    final = middle + (part.astype(F32) + got.astype(F32) + gains[LAYERS - 1, 5])
    final = lax.optimization_barrier(final.astype(BF16))
    outputs = final, flip(final, "cy")

    sums_ffn = [None] * (LAYERS + 1)
    sums_mix = [None] * LAYERS
    sums_in = [None] * LAYERS
    reduced = [None] * LAYERS

    def second_hop(keep_x, got_x, keep_y, got_y, after):
        pass_x, pass_y = pass_on(keep_x, got_x, keep_y, got_y, after)
        all_x = (keep_x[0], got_x[0], flip(pass_x, "cy"))
        all_y = (keep_y[0], got_y[0], flip(pass_y, "tx"))
        return pass_x, pieces_of((all_x, all_y), block_rows)

    zero_first = ()
    zero_mix = ()
    zero_attention = ()
    zero_memory = ()
    above_attention = None
    for layer in reversed(range(LAYERS)):
        (
            stream,
            normed,
            qkv,
            memory,
            log_totals,
            attended,
            middle,
            normed_two,
            active,
            slope,
        ) = saved[layer]
        top = layer == LAYERS - 1
        stream_grad, down, hidden_grad, part, sums_ffn[layer] = rows_call(
            partial(ffn_backward_kernel, layer),
            place,
            (own_cot, slope) if top else (stream_grad, stream_above, part, got, slope),
            (order if top else gains,),
            ffn_slabs[layer],
            (),
            (row_f32, row_b16, side_hidden, row_b16),
            (sums_shape,),
            9,
            after=zero_first,
        )
        got = flip(part, "cc")
        if above_attention is not None:
            qk_give, qk_keep, qk_got, vo_keep, vo_got = above_attention
            passed, attn_pieces = second_hop(qk_keep, qk_got, vo_keep, vo_got, (down,))
            zero_mix, zero_attention = (passed,), (attn_pieces,)
            reduced[layer + 1] = (spread_pieces(attn_pieces), spread_ffn)
            zero_memory = (spread_ffn,)
        ffn_operands = (normed_two, down, hidden_grad, active)
        ffn_plans = [
            [
                [[(0, x, 2, y, 0, hidden_own)] for x, y in pair_x],
                [[(1, x, 3, y, 0, hidden_own)] for x, y in pair_y],
            ]
            for pair_x, pair_y in ((GIVE_X, GIVE_Y), (KEEP_X, KEEP_Y))
        ]
        up_give, down_give = weight_grads(ffn_operands, ffn_plans[0], half)
        up_got, down_got = flip(up_give, "tx"), flip(down_give, "cy")
        stream_grad, branch_grad, attended_grad, sums_mix[layer] = rows_call(
            partial(mix_backward_kernel, layer),
            place,
            (stream_grad, middle, part, got),
            (gains,),
            attn_slabs[layer],
            (),
            (row_f32, row_b16, side_width),
            (sums_shape,),
            6,
            after=(up_give, *zero_mix),
        )
        dq, dkv, last, back = attention_backward(
            memory_bias, qkv, memory, log_totals, attended, attended_grad, table_near, zero_attention
        )
        received = lax.ppermute(back, "cy", ((1, 0),))
        up_keep, down_keep = weight_grads(ffn_operands, ffn_plans[1], half, (dq,))
        passed, ffn_pieces = second_hop(up_keep, up_got, down_keep, down_got, (dq,))
        grads_in, part, sums_in[layer] = memory_backward(
            place, dq, dkv, last, received, table_near, table_far, attn_slabs[layer],
            (passed, *zero_memory),
        )
        got = flip(part, "cc")
        spread_ffn = spread_pieces(ffn_pieces)
        attn_plans = [
            [
                [[(0, x, 2, y, 0, 2 * width)] for x, y in pair_x],
                [
                    [(0, x, 2, y, 2 * width, 3 * width), (1, x, 3, y, 0, width)]
                    for x, y in pair_y
                ],
            ]
            for pair_x, pair_y in ((GIVE_X, GIVE_Y), (KEEP_X, KEEP_Y))
        ]
        attn_operands = (normed, branch_grad, grads_in, attended)
        qk_give, vo_give = weight_grads(attn_operands, attn_plans[0], half)
        qk_got, vo_got = flip(qk_give, "tx"), flip(vo_give, "cy")
        if layer > 0:
            qk_keep, vo_keep = weight_grads(attn_operands, attn_plans[1], half)
            above_attention = qk_give, qk_keep, qk_got, vo_keep, vo_got
            zero_first = (qk_give, ffn_pieces)
        stream_above = stream
    final, sums_ffn[LAYERS] = rows_call(
        leave_kernel,
        place,
        (stream_grad, stream, part, got),
        (gains,),
        None,
        (),
        (row_b16,),
        (sums_shape,),
        5,
        after=(qk_give, ffn_pieces),
    )
    qk_keep, vo_keep = weight_grads(attn_operands, attn_plans[1], half, (final,))
    passed, attn_pieces = second_hop(qk_keep, qk_got, vo_keep, vo_got, (final,))
    reduced[0] = (spread_pieces(attn_pieces), spread_ffn)
    reduced = [[piece.astype(F32).sum(axis=0) for piece in pair] for pair in reduced]
    activations = restore(*outputs, order_back, place, (passed,))
    input_grad = restore(final, flip(final, "cy"), order_back, place)

    vector_d = []
    vector_own = []
    vector_other = []
    for layer in range(LAYERS):
        below = sums_ffn[layer - 1] if layer > 0 else sums_ffn[LAYERS]
        vector_d.append(
            jnp.concatenate(
                [below[:2], sums_mix[layer][:3], sums_ffn[layer][2:3]], axis=0
            )
        )
        ups = sums_ffn[layer][3:5].reshape(2, width, 4).transpose(0, 2, 1)
        for side, out in enumerate((vector_own, vector_other)):
            sums = sums_in[layer][side]
            out.append(
                jnp.concatenate(
                    [sums[None, :width], sums[None, 2 * width :], ups[side]], axis=0
                )
            )
    qkv_grads = [
        jnp.stack([r[0][:, i * width : (i + 1) * width] for i in range(3)]) for r in reduced
    ]
    matrix_grads = (
        jnp.stack(qkv_grads),
        jnp.stack([r[0][:, 3 * width :] for r in reduced]),
        jnp.stack([r[1][:, :hidden_own] for r in reduced]),
        jnp.stack([r[1][:, hidden_own:] for r in reduced]),
    )
    vec_d_grad = jnp.dot(
        jnp.stack(vector_d).reshape(-1, features), order_wide.T, precision=PRECISE
    ).reshape(-1)
    own_c = jnp.stack(vector_own).reshape(-1)
    other_c = jnp.stack(vector_other).reshape(-1)
    arrived = flip(jnp.concatenate([vec_d_grad, other_c]), "cy")
    vector = butterfly(jnp.concatenate([vec_d_grad, own_c]) + arrived, ("tx", "tz"))
    vec_d_grad = vector[: vec_d.size].reshape(vec_d.shape)
    vec_c_grad = vector[vec_d.size :].reshape(vec_c.shape)

    square = sum(jnp.sum(grad * grad) for grad in matrix_grads)
    square = (
        square
        + jnp.sum(vec_d_grad * vec_d_grad) / (tok_count * ch_count)
        + jnp.sum(vec_c_grad * vec_c_grad) / tok_count
    )
    everywhere = ("tz", "tx", "cy", "cc")
    squares = lax.all_to_all(
        jnp.full((tok_count * ch_count, 128), square), everywhere, 0, 0, tiled=True
    )
    total_square = jnp.sum(squares[:, 0])
    grad_norm = jnp.sqrt(total_square)
    factor = CLIP_LIMIT / jnp.maximum(grad_norm, CLIP_LIMIT)
    attention_update = adamw(
        w_qkv, w_qkv_first, w_qkv_second, matrix_grads[0] * factor, RATE_QKV, WEIGHT_DECAY
    )
    output_update = adamw(
        w_out_t, w_out_first, w_out_second, matrix_grads[1] * factor, RATE_OUT, WEIGHT_DECAY
    )
    expand_update = adamw(
        w_up, w_up_first, w_up_second, matrix_grads[2] * factor, RATE_UP, WEIGHT_DECAY
    )
    reduce_update = adamw(
        w_down_t, w_down_first, w_down_second, matrix_grads[3] * factor, RATE_DOWN, WEIGHT_DECAY
    )
    width_update = adamw(vec_d, vec_d_first, vec_d_second, vec_d_grad * factor, RATE_VECTOR, 0.0)
    channel_update = adamw(vec_c, vec_c_first, vec_c_second, vec_c_grad * factor, RATE_VECTOR, 0.0)
    return (
        activations,
        input_grad,
        grad_norm,
        *attention_update,
        *output_update,
        *expand_update,
        *reduce_update,
        *width_update,
        *channel_update,
    )


def solution(mesh):
    tok, ch = mesh.shape["tok"], mesh.shape["ch"]
    fine = Mesh(mesh.devices.reshape(tok // 2, 2, 2, ch // 2), ("tz", "tx", "cy", "cc"))
    t, c = ("tz", "tx"), ("cy", "cc")
    cube = P(None, None, t, c)
    matrix = P(None, t, c)
    channel = P(None, None, c)
    return jax.shard_map(
        shards,
        mesh=fine,
        in_specs=(
            P(t, None),
            P(t, None),
            P(None, t, None, None, c),
            P(),
            P(t, None, None),
            P(t),
            *(cube,) * 3,
            *(matrix,) * 9,
            *(P(),) * 3,
            *(channel,) * 3,
        ),
        out_specs=(
            P(t, None),
            P(t, None),
            P(),
            *(cube,) * 3,
            *(matrix,) * 9,
            *(P(),) * 3,
            *(channel,) * 3,
        ),
        check_vma=False,
    )
```

```python
from functools import partial
from typing import NamedTuple

import jax
import jax.numpy as jnp
from jax import lax
from jax.experimental import pallas as pl
from jax.experimental.pallas import tpu as pltpu
from jax.sharding import Mesh
from jax.sharding import PartitionSpec as P

HEAD_DIM = 64
BASIS = 256
SAMPLES = 256
SEG = 512
SEGS = 4
CRES = 1024
LAYERS = 2
STEP = 10

PRECISE = lax.Precision.HIGHEST
STICKY_RATIO = 0.5
RIDGE_WEIGHT = 0.5
BASIS_WIDTH = 0.01
NORM_EPS = 1e-05
CLIP_LIMIT = 1.0
FIRST_DECAY = 0.9
SECOND_DECAY = 0.95
ADAM_EPS = 1e-08
WEIGHT_DECAY = 0.1
RATE_QKV = 0.05
RATE_OUT = 0.5
RATE_UP = 0.05
RATE_DOWN = 0.03
RATE_VECTOR = 0.5
MASKED = -1e30
GELU_A = 0.7978845608028654
GELU_B = 0.044715
F32 = jnp.float32
BF16 = jnp.bfloat16
SWAP = ((0, 1), (1, 0))
NN = (((1,), (0,)), ((), ()))
NT = (((1,), (1,)), ((), ()))
TN = (((0,), (0,)), ((), ()))


def dot(left, right, dims, precision=None):
    return lax.dot_general(left, right, dims, precision=precision, preferred_element_type=F32)


VMEM_LIMIT = 24 * 2**20
TILE = 256
QT = 256


def cost(micros):
    return pl.CostEstimate(flops=int(micros * 1.1e9), bytes_accessed=10**6, transcendentals=0)


def table_kernel(old_ref, design_ref, out_ref, inv_ref, gram_ref):
    design = design_ref[...]
    eye = (
        lax.broadcasted_iota(jnp.int32, (BASIS, BASIS), 0)
        == lax.broadcasted_iota(jnp.int32, (BASIS, BASIS), 1)
    ).astype(F32)
    gram = dot(design, design, NT, PRECISE) + RIDGE_WEIGHT * eye
    gram_ref[...] = gram
    bound = jnp.max(jnp.sum(jnp.abs(gram), axis=0))
    inv_ref[...] = eye * (1.0 / bound)

    def step(low):
        scale = 2.0 / (1.0 + low)
        now = inv_ref[...]
        inner = dot(gram_ref[...], now, NN, PRECISE)
        inv_ref[...] = scale * (2.0 * now - scale * dot(now, inner, NN, PRECISE))
        return 4.0 * low / ((1.0 + low) * (1.0 + low))

    lax.while_loop(lambda low: low < 0.999, step, 0.99 * RIDGE_WEIGHT / bound)
    for _ in range(2):
        now = inv_ref[...]
        inner = dot(gram_ref[...], now, NN, PRECISE)
        inv_ref[...] = 2.0 * now - dot(now, inner, NN, PRECISE)
    fitted = dot(inv_ref[...], design, NN, PRECISE)
    out_ref[:, BASIS:] = fitted[:, SAMPLES:].astype(BF16)
    out_ref[:, :BASIS] = dot(fitted[:, :SAMPLES], old_ref[...], NT, PRECISE).astype(BF16)


def basis_table(centres, times):
    middle = (centres.astype(F32) + 0.5) / CRES
    offset = (times[None, :] - middle[:, None]) / BASIS_WIDTH
    return jnp.exp(-0.5 * offset * offset)


def table_inputs(centres, sticky_row):
    token_times = STICKY_RATIO + (1.0 - STICKY_RATIO) * (jnp.arange(SEG).astype(F32) + 0.5) / SEG
    places = (sticky_row.astype(F32) + 0.5) / CRES
    return (
        basis_table(centres, places),
        basis_table(centres, jnp.concatenate([STICKY_RATIO * places, token_times])),
    )


def make_tables(old_basis, design, after):
    def body(old_ref, design_ref, *refs):
        table_kernel(old_ref, design_ref, *refs[len(after) :])

    vmem = pl.BlockSpec(memory_space=pltpu.VMEM)
    return pl.pallas_call(
        body,
        in_specs=[vmem, vmem] + [pl.BlockSpec(memory_space=pl.ANY)] * len(after),
        out_specs=vmem,
        out_shape=jax.ShapeDtypeStruct((BASIS, BASIS + SEG), BF16),
        scratch_shapes=[pltpu.VMEM((BASIS, BASIS), F32), pltpu.VMEM((BASIS, BASIS), F32)],
        compiler_params=pltpu.CompilerParams(vmem_limit_bytes=VMEM_LIMIT),
        cost_estimate=cost(14),
    )(old_basis, design, *after)


def slab_columns(slab, low, high):
    return slab[:, low:high] if len(slab.shape) == 2 else slab[0, 0, :, low:high]


def project(left, slabs, low, high):
    own, by_x, by_y, by_both = (slab_columns(slab, low, high) for slab in slabs)
    half = own.shape[0]
    first, second = left[:, :half], left[:, half:]
    return (
        dot(first, own, NN) + dot(second, by_x, NN),
        dot(first, by_y, NN) + dot(second, by_both, NN),
    )


def unproject(sides, slabs, low, high):
    own, by_x, by_y, by_both = (slab_columns(slab, low, high) for slab in slabs)
    return jnp.concatenate(
        [
            dot(sides[0], own, NT) + dot(sides[1], by_y, NT),
            dot(sides[0], by_x, NT) + dot(sides[1], by_both, NT),
        ],
        axis=1,
    )


def split_attention(refs, width):
    if len(refs[0].shape) == 2:
        return (refs[:4], 0), (refs[4:8], 0), refs[8:]
    return (refs[:4], 0), (refs[:4], 2 * width), refs[4:]


def split_ffn(refs):
    if len(refs[0].shape) == 2:
        return (refs[:4], 0), (refs[4:8], 0), refs[8:]
    return (refs[:4], 0), (refs[:4], refs[0].shape[-1] // 2), refs[4:]


TURNS = ((0, 0), (0, 1), (1, 0), (1, 1))


def cast_kernel(count, out_ref_index, *refs):
    out_ref = refs[out_ref_index]
    start = 0
    for ref in refs[:count]:
        for index in range(ref.shape[1]):
            columns = ref.shape[3]
            out_ref[:, start : start + columns] = ref[0, index].astype(BF16)
            start += columns


def cast(members, after=()):
    members = [
        (weight if weight.ndim == 4 else weight[:, None], layer) for weight, layer in members
    ]
    rows = members[0][0].shape[2]
    columns = sum(weight.shape[1] * weight.shape[3] for weight, _ in members)
    return pl.pallas_call(
        partial(cast_kernel, len(members), len(members) + len(after)),
        grid=(1,),
        in_specs=[
            pl.BlockSpec((1,) + weight.shape[1:], lambda i, layer=layer: (layer, 0, 0, 0))
            for weight, layer in members
        ]
        + [pl.BlockSpec(memory_space=pl.ANY)] * len(after),
        out_specs=pl.BlockSpec((rows, columns), lambda i: (0, 0)),
        out_shape=array((rows, columns), BF16),
        compiler_params=pltpu.CompilerParams(vmem_limit_bytes=VMEM_LIMIT),
        cost_estimate=cost(1),
    )(*(weight for weight, _ in members), *after)


def split_kernel(count, rows_ref, *refs):
    start = 0
    outs = refs[len(refs) - count - 1 :]
    for out_ref in outs[:count]:
        columns = out_ref.shape[1]
        out_ref[...] = rows_ref[:, start : start + columns]
        start += columns
    outs[count][...] = jnp.zeros_like(outs[count])


def split_columns(rows, widths, after):
    vmem = pl.BlockSpec(memory_space=pltpu.VMEM)
    *groups, zero = pl.pallas_call(
        partial(split_kernel, len(widths)),
        in_specs=[vmem] + [pl.BlockSpec(memory_space=pl.ANY)] * len(after),
        out_specs=[vmem] * (len(widths) + 1),
        out_shape=[array((rows.shape[0], columns), rows.dtype) for columns in widths]
        + [array((8, 128), jnp.int32)],
        compiler_params=pltpu.CompilerParams(vmem_limit_bytes=VMEM_LIMIT),
        cost_estimate=cost(1),
    )(rows, *after)
    return groups, zero[0, 0]


def pass_kernel(keep_a_ref, got_a_ref, keep_b_ref, got_b_ref, *refs):
    for keep_ref, got_ref, out_ref in (
        (keep_a_ref, got_a_ref, refs[-2]),
        (keep_b_ref, got_b_ref, refs[-1]),
    ):
        out_ref[...] = (keep_ref[0].astype(F32) + got_ref[0].astype(F32)).astype(BF16)


def pass_on(keep_a, got_a, keep_b, got_b, after):
    def slab(a):
        return pl.BlockSpec((1,) + a.shape[1:], lambda i: (1, 0, 0))

    def out(a):
        return pl.BlockSpec(a.shape[1:], lambda i: (0, 0))

    return pl.pallas_call(
        pass_kernel,
        grid=(1,),
        in_specs=[slab(a) for a in (keep_a, got_a, keep_b, got_b)]
        + [pl.BlockSpec(memory_space=pl.ANY)] * len(after),
        out_specs=[out(keep_a), out(keep_b)],
        out_shape=[array(keep_a.shape[1:], BF16), array(keep_b.shape[1:], BF16)],
        compiler_params=pltpu.CompilerParams(vmem_limit_bytes=VMEM_LIMIT),
        cost_estimate=cost(2),
    )(keep_a, got_a, keep_b, got_b, *after)


class Gathered(NamedTuple):
    whole: jax.Array
    columns: int
    index: int


def slab_operands(slabs, grid_rank):
    def fixed(shape):
        return pl.BlockSpec(shape, lambda *a: (0,) * len(shape))

    if not isinstance(slabs, Gathered):
        return [in_hbm(slab) for slab in slabs], [fixed(slab.shape) for slab in slabs]
    whole, columns, index = slabs
    specs = []
    for turn_y, turn_x in TURNS:
        specs.append(
            pl.BlockSpec(
                (1, 1, whole.shape[2], columns),
                lambda *a, turn_y=turn_y, turn_x=turn_x: (
                    a[grid_rank][0] ^ turn_y,
                    a[grid_rank][1] ^ turn_x,
                    0,
                    index,
                ),
            )
        )
    return [in_hbm(whole)] * 4, specs


def norm_stats(inputs):
    centred = inputs - jnp.mean(inputs, axis=-1, keepdims=True)
    variance = jnp.mean(centred * centred, axis=-1, keepdims=True)
    rstd = lax.rsqrt(variance + NORM_EPS)
    return centred * rstd, rstd


def norm_backward(inputs, grad, gain_row):
    unit, rstd = norm_stats(inputs)
    scaled = grad * gain_row
    back = rstd * (
        scaled
        - jnp.mean(scaled, axis=-1, keepdims=True)
        - unit * jnp.mean(scaled * unit, axis=-1, keepdims=True)
    )
    return back, grad * unit


def both_parts(own_ref, got_ref):
    return own_ref[...].astype(F32) + got_ref[...].astype(F32)


def add_rows(ref, rows):
    @pl.when(pl.program_id(0) == 0)
    def _():
        ref[...] = jnp.zeros_like(ref)

    for index, row in rows:
        ref[index : index + 1, :] += jnp.sum(row, axis=0, keepdims=True)


def rows_call(
    kernel, place, tiled, whole, slabs, more, tiled_outs, whole_outs, micros, scratch=(), after=()
):
    rows = tiled[0].shape[-2]

    def tile_spec(shape):
        if len(shape) == 2:
            return pl.BlockSpec((TILE, shape[1]), lambda i, p: (i, 0))
        return pl.BlockSpec((shape[0], TILE, shape[2]), lambda i, p: (0, i, 0))

    def whole_spec(shape):
        return pl.BlockSpec(shape, lambda i, p: (0,) * len(shape))

    slab_arrays, slab_specs = slab_operands(slabs, 1) if slabs is not None else ([], [])

    taken = len(tiled) + len(whole) + len(slab_arrays) + len(more)

    def body(place_ref, *refs):
        kernel(*refs[:taken], *refs[taken + len(after) :])

    return pl.pallas_call(
        body,
        grid_spec=pltpu.PrefetchScalarGridSpec(
            num_scalar_prefetch=1,
            grid=(rows // TILE,),
            in_specs=[tile_spec(a.shape) for a in tiled]
            + [whole_spec(a.shape) for a in whole]
            + slab_specs
            + [whole_spec(a.shape) for a in more]
            + [pl.BlockSpec(memory_space=pl.ANY)] * len(after),
            out_specs=[tile_spec(a.shape) for a in tiled_outs]
            + [whole_spec(a.shape) for a in whole_outs],
            scratch_shapes=list(scratch),
        ),
        out_shape=[*tiled_outs, *whole_outs],
        compiler_params=pltpu.CompilerParams(vmem_limit_bytes=VMEM_LIMIT),
        cost_estimate=cost(micros),
    )(place, *tiled, *whole, *slab_arrays, *more, *after)


def in_hbm(operand):
    return pltpu.with_memory_space_constraint(operand, pltpu.HBM)


def kept(shape, dtype):
    return pltpu.HBM(shape, dtype)


def array(shape, dtype):
    return jax.ShapeDtypeStruct(shape, dtype)


def enter_kernel(layer, *refs):
    if layer == 0:
        h_ref, order_ref, gains_ref, bias_ref, *refs = refs
        stream = dot(h_ref[...], order_ref[...], NN)
    else:
        middle_ref, own_ref, got_ref, gains_ref, bias_ref, *refs = refs
        stream = middle_ref[...] + (both_parts(own_ref, got_ref) + gains_ref[layer - 1, 5:6, :])
    width = refs[-4].shape[2] // 3
    slabs_qk, slabs_vo, refs = split_attention(refs, width)
    near_ref, far_ref, start_ref, *refs = refs
    stream_ref, normed_ref, qkv_ref, fit_ref, ahead_ref, signal_ref = refs
    step = pl.program_id(0)
    stream_ref[...] = stream
    unit, _ = norm_stats(stream)
    normed = (unit * gains_ref[layer, 0:1, :] + gains_ref[layer, 1:2, :]).astype(BF16)
    normed_ref[...] = normed
    rows = pl.ds(pl.multiple_of(step * TILE, TILE), TILE)
    low = slabs_qk[1]
    queries_keys = project(normed, slabs_qk[0], low, low + 2 * width)
    low = slabs_vo[1]
    values = project(normed, slabs_vo[0], low, low + width)
    for side in range(2):
        result = jnp.concatenate([queries_keys[side], values[side]], axis=1)
        result = (result + bias_ref[layer, side : side + 1, :]).astype(BF16)
        qkv_ref[side] = result
        signal_ref[side, rows, :] = result[:, width:]

    @pl.when(step == pl.num_programs(0) - 1)
    def _():
        for side in range(2):
            fit_near = dot(near_ref[:, BASIS:], signal_ref[side, :SEG, :], NN)
            fit_far = dot(far_ref[:, BASIS:], signal_ref[side, SEG:, :], NN)
            fit_ref[side] = fit_near
            ahead = dot(near_ref[:, :BASIS], start_ref[layer, side], NN) + fit_near
            ahead = dot(far_ref[:, :BASIS], ahead.astype(BF16), NN) + fit_far
            ahead_ref[side] = ahead.astype(BF16)


def ffn_forward_kernel(layer, stream_ref, own_ref, got_ref, gains_ref, bias_ref, *refs):
    (up, up_low), (down, down_low), refs = split_ffn(refs)
    middle_ref, normed_ref, active_ref, slope_ref, part_ref = refs
    hidden_own = active_ref.shape[2]
    middle = stream_ref[...] + (both_parts(own_ref, got_ref) + gains_ref[layer, 4:5, :])
    middle_ref[...] = middle
    unit, _ = norm_stats(middle)
    normed = (unit * gains_ref[layer, 2:3, :] + gains_ref[layer, 3:4, :]).astype(BF16)
    normed_ref[...] = normed
    sides = []
    for side, hidden in enumerate(project(normed, up, up_low, up_low + hidden_own)):
        hidden = hidden + bias_ref[layer, side : side + 1, :]
        square = hidden * hidden
        bend = jnp.tanh(hidden * (GELU_A + (GELU_A * GELU_B) * square))
        half_more = 0.5 + 0.5 * bend
        active = (hidden * half_more).astype(BF16)
        slope = half_more + (0.5 - 0.5 * bend * bend) * hidden * (
            GELU_A + (3.0 * GELU_A * GELU_B) * square
        )
        active_ref[side] = active
        slope_ref[side] = slope.astype(BF16)
        sides.append(active)
    part_ref[...] = unproject(sides, down, down_low, down_low + hidden_own).astype(BF16)


def ffn_backward_kernel(layer, *refs):
    if layer == LAYERS - 1:
        cot_ref, slope_ref, order_ref, *refs = refs
        (up_slabs, up_low), (down_slabs, down_low), refs = split_ffn(refs)
        stream_grad = dot(cot_ref[...], order_ref[...], NN)
        grad_ref, down_ref, hidden_ref, part_ref, sums_ref = refs
        sums = []
    else:
        before_ref, stream_ref, own_ref, got_ref, slope_ref, gains_ref, *refs = refs
        (up_slabs, up_low), (down_slabs, down_low), refs = split_ffn(refs)
        grad_ref, down_ref, hidden_ref, part_ref, sums_ref = refs
        normed_grad = both_parts(own_ref, got_ref)
        back, gain_rows = norm_backward(
            stream_ref[...], normed_grad, gains_ref[layer + 1, 0:1, :]
        )
        stream_grad = before_ref[...] + back
        sums = [(0, gain_rows), (1, normed_grad)]
    hidden_own = slope_ref.shape[2]
    grad_ref[...] = stream_grad
    down = stream_grad.astype(BF16)
    down_ref[...] = down
    sums.append((2, down.astype(F32)))
    sides = []
    for side, active_grad in enumerate(project(down, down_slabs, down_low, down_low + hidden_own)):
        hidden_grad = (active_grad * slope_ref[side].astype(F32)).astype(BF16)
        hidden_ref[side] = hidden_grad
        sums.append((3 + side, hidden_grad.astype(F32)))
        sides.append(hidden_grad)
    part_ref[...] = unproject(sides, up_slabs, up_low, up_low + hidden_own).astype(BF16)
    add_rows(sums_ref, sums)


def mix_backward_kernel(layer, before_ref, middle_ref, own_ref, got_ref, gains_ref, *refs):
    width = refs[-2].shape[2]
    slabs_qk, (slabs, low), refs = split_attention(refs, width)
    grad_ref, branch_ref, attended_ref, sums_ref = refs
    normed_grad = both_parts(own_ref, got_ref)
    back, gain_rows = norm_backward(middle_ref[...], normed_grad, gains_ref[layer, 2:3, :])
    stream_grad = before_ref[...] + back
    grad_ref[...] = stream_grad
    branch = stream_grad.astype(BF16)
    branch_ref[...] = branch
    for side, result in enumerate(project(branch, slabs, low + width, low + 2 * width)):
        attended_ref[side] = result.astype(BF16)
    add_rows(sums_ref, [(0, gain_rows), (1, normed_grad), (2, branch.astype(F32))])


def leave_kernel(before_ref, stream_ref, own_ref, got_ref, gains_ref, grad_ref, sums_ref):
    normed_grad = both_parts(own_ref, got_ref)
    back, gain_rows = norm_backward(stream_ref[...], normed_grad, gains_ref[0, 0:1, :])
    grad_ref[...] = (before_ref[...] + back).astype(BF16)
    add_rows(sums_ref, [(0, gain_rows), (1, normed_grad)])


def restore_kernel(context_ref, own_ref, got_ref, order_ref, *refs):
    out_ref, zero_ref = refs[-2:]
    zero_ref[...] = jnp.zeros_like(zero_ref)
    mine = (pl.program_id(0) // (pl.num_programs(0) // 2)) == context_ref[0]
    rows = jnp.where(mine, own_ref[...].astype(F32), got_ref[...].astype(F32)).astype(BF16)
    out_ref[...] = dot(rows, order_ref[...], NN)


def restore(own, got, order, context, after=()):
    rows, features = own.shape
    tiles = rows // TILE
    block = pl.BlockSpec((TILE, features), lambda i: (i % tiles, 0))
    return pl.pallas_call(
        restore_kernel,
        grid=(2 * tiles,),
        in_specs=[
            pl.BlockSpec(memory_space=pltpu.SMEM),
            block,
            block,
            pl.BlockSpec(order.shape, lambda i: (0, 0)),
            *(pl.BlockSpec(memory_space=pl.ANY) for _ in after),
        ],
        out_specs=[
            pl.BlockSpec((TILE, features), lambda i: (i, 0)),
            pl.BlockSpec((8, 128), lambda i: (0, 0)),
        ],
        out_shape=[kept((2 * rows, features), F32), array((8, 128), F32)],
        compiler_params=pltpu.CompilerParams(vmem_limit_bytes=VMEM_LIMIT),
        cost_estimate=cost(4),
    )(context, own, got, order, *after)


def causal(shape):
    return lax.broadcasted_iota(jnp.int32, shape, 0) <= lax.broadcasted_iota(jnp.int32, shape, 1)


def head_lanes(kind, head, heads):
    low = (kind * heads + head) * HEAD_DIM
    return slice(low, low + HEAD_DIM)


def attention_forward_kernel(
    place_ref,
    bias_ref,
    qkv_ref,
    start_ref,
    got_ref,
    fit_ref,
    near_ref,
    *refs,
):
    slabs = refs[:4]
    out_ref, lse_ref, memory_ref, part_ref, rows_ref, total_ref = refs[-6:]
    segment, side = pl.program_id(0), pl.program_id(1)
    heads = qkv_ref.shape[2] // (3 * HEAD_DIM)
    width = heads * HEAD_DIM

    @pl.when(segment == 0)
    def _():
        @pl.when(place_ref[0] == 0)
        def _():
            rows_ref[side, 0] = start_ref[0, 0]

        @pl.when(place_ref[0] != 0)
        def _():
            rows_ref[side, 0] = got_ref[0]

        second = dot(near_ref[:, :BASIS], rows_ref[side, 0], NN) + fit_ref[0]
        rows_ref[side, 1] = second.astype(BF16)

    memory_ref[0, 0] = rows_ref[side, segment]
    memory_bias = bias_ref[segment]
    for tile in range(SEG // QT):
        rows = slice(tile * QT, (tile + 1) * QT)
        stacked = []
        for head in range(heads):
            lanes_q, lanes_k, lanes_v = (head_lanes(kind, head, heads) for kind in range(3))
            query = qkv_ref[0, rows, lanes_q] * HEAD_DIM ** (-0.5)
            scores = []
            values = []
            for part in range(tile + 1):
                keys = slice(part * QT, (part + 1) * QT)
                score = dot(qkv_ref[0, keys, lanes_k], query, NT)
                if part == tile:
                    score = jnp.where(causal(score.shape), score, MASKED)
                scores.append(score)
                values.append(qkv_ref[0, keys, lanes_v])
            memory_key = rows_ref[side, segment, :, head_lanes(0, head, heads)]
            scores.append(dot(memory_key, query, NT) + memory_bias)
            values.append(rows_ref[side, segment, :, head_lanes(1, head, heads)])
            top = scores[0].max(axis=0, keepdims=True)
            for score in scores[1:]:
                top = jnp.maximum(top, score.max(axis=0, keepdims=True))
            total = jnp.zeros_like(top)
            result = jnp.zeros((HEAD_DIM, QT), F32)
            for score, value in zip(scores, values):
                weight = jnp.exp(score - top)
                total = total + weight.sum(axis=0, keepdims=True)
                result = result + dot(value, weight.astype(BF16), TN)
            stacked.append(result / total)
            lse_ref[0, 0, head : head + 1, rows] = top + jnp.log(total)
        out_ref[0, rows, :] = jnp.concatenate(stacked, axis=0).T.astype(BF16)
    attended = out_ref[0]
    low = slabs[0].shape[-1] - width
    own, by_x, by_y, by_both = (slab_columns(slab, low, low + width) for slab in slabs)

    @pl.when(side == 0)
    def _():
        total_ref[...] = jnp.concatenate(
            [dot(attended, own, NT), dot(attended, by_x, NT)], axis=1
        )

    @pl.when(side == 1)
    def _():
        part = total_ref[...] + jnp.concatenate(
            [dot(attended, by_y, NT), dot(attended, by_both, NT)],
            axis=1,
        )
        part_ref[...] = part.astype(BF16)


def attention_forward(layer, place, memory_bias, qkv, starts, got, fit, near, slabs, after=()):
    rows = qkv.shape[1]
    width = qkv.shape[2] // 3
    heads = width // HEAD_DIM
    segs = rows // SEG
    slab_arrays, slab_specs = slab_operands(slabs, 2)
    features = 2 * slab_arrays[0].shape[-2]
    return pl.pallas_call(
        attention_forward_kernel,
        grid_spec=pltpu.PrefetchScalarGridSpec(
            num_scalar_prefetch=1,
            grid=(segs, 2),
            in_specs=[
                pl.BlockSpec(memory_space=pltpu.SMEM),
                pl.BlockSpec((1, SEG, 3 * width), lambda g, s, p: (s, g, 0)),
                pl.BlockSpec((1, 1, BASIS, 2 * width), lambda g, s, p: (layer, s, 0, 0)),
                pl.BlockSpec((1, BASIS, 2 * width), lambda g, s, p: (1 - s, 0, 0)),
                pl.BlockSpec((1, BASIS, 2 * width), lambda g, s, p: (s, 0, 0)),
                pl.BlockSpec(near.shape, lambda g, s, p: (0, 0)),
                *slab_specs,
                *(pl.BlockSpec(memory_space=pl.ANY) for _ in after),
            ],
            out_specs=[
                pl.BlockSpec((1, SEG, width), lambda g, s, p: (s, g, 0)),
                pl.BlockSpec((1, 1, heads, SEG), lambda g, s, p: (g, s, 0, 0)),
                pl.BlockSpec((1, 1, BASIS, 2 * width), lambda g, s, p: (g, s, 0, 0)),
                pl.BlockSpec((SEG, features), lambda g, s, p: (g, 0)),
            ],
            scratch_shapes=[
                pltpu.VMEM((2, segs, BASIS, 2 * width), BF16),
                pltpu.VMEM((SEG, features), F32),
            ],
        ),
        out_shape=[
            kept((2, rows, width), BF16),
            kept((segs, 2, heads, SEG), F32),
            kept((segs, 2, BASIS, 2 * width), BF16),
            array((rows, features), BF16),
        ],
        compiler_params=pltpu.CompilerParams(vmem_limit_bytes=VMEM_LIMIT),
        cost_estimate=cost(13),
    )(place, memory_bias, in_hbm(qkv), starts, got, fit, near, *slab_arrays, *after)


def attention_backward_kernel(
    bias_ref,
    qkv_ref,
    memory_ref,
    lse_ref,
    out_ref,
    grad_ref,
    near_ref,
    *refs,
):
    dq_ref, dkv_ref, last_ref, back_ref, first_ref = refs[-5:]
    segment = pl.program_id(1)
    memory_bias = bias_ref[segment]
    heads = out_ref.shape[2] // HEAD_DIM
    scale = HEAD_DIM ** (-0.5)
    tiles = SEG // QT
    product = (out_ref[0].astype(F32) * grad_ref[0].astype(F32)).T
    query_grads = []
    for head in range(heads):
        lanes = head_lanes(0, head, heads)
        lanes_k, lanes_v = head_lanes(1, head, heads), head_lanes(2, head, heads)
        query = qkv_ref[0, :, lanes] * scale
        grad = grad_ref[0, :, lanes]
        dots = product[lanes, :].sum(axis=0, keepdims=True)
        log_total = lse_ref[0, 0, head : head + 1, :]
        head_grads = [jnp.zeros((HEAD_DIM, QT), F32) for _ in range(tiles)]
        for part in range(tiles + 1):
            if part < tiles:
                keys = slice(part * QT, (part + 1) * QT)
                key, value = qkv_ref[0, keys, lanes_k], qkv_ref[0, keys, lanes_v]
            else:
                key = memory_ref[0, 0, :, head_lanes(0, head, heads)]
                value = memory_ref[0, 0, :, head_lanes(1, head, heads)]
            key_grad = jnp.zeros((QT, HEAD_DIM), F32)
            value_grad = jnp.zeros((QT, HEAD_DIM), F32)
            for tile in range(part if part < tiles else 0, tiles):
                rows = slice(tile * QT, (tile + 1) * QT)
                score = dot(key, query[rows], NT)
                if part == tile:
                    score = jnp.where(causal(score.shape), score, MASKED)
                if part == tiles:
                    score = score + memory_bias
                weight = jnp.exp(score - log_total[:, rows])
                weight_grad = dot(value, grad[rows], NT)
                score_grad = (weight * (weight_grad - dots[:, rows])).astype(BF16)
                value_grad = value_grad + dot(weight.astype(BF16), grad[rows], NN)
                key_grad = key_grad + dot(score_grad, query[rows], NN)
                head_grads[tile] = head_grads[tile] + dot(key, score_grad, TN)
            if part < tiles:
                dkv_ref[0, keys, head_lanes(0, head, heads)] = key_grad
                dkv_ref[0, keys, head_lanes(1, head, heads)] = value_grad
            else:
                last_ref[0, :, head_lanes(0, head, heads)] = key_grad
                last_ref[0, :, head_lanes(1, head, heads)] = value_grad
        query_grads.append(jnp.concatenate(head_grads, axis=1) * scale)
    dq_ref[0] = jnp.concatenate(query_grads, axis=0).T.astype(BF16)

    @pl.when(segment == 0)
    def _():
        first_ref[...] = last_ref[0]

    @pl.when(segment == 1)
    def _():
        back = first_ref[...] + dot(near_ref[:, :BASIS], last_ref[0].astype(BF16), TN)
        back_ref[0] = back.astype(BF16)


def attention_backward(memory_bias, qkv, memory, log_totals, attended, grad, near, after):
    rows, width = attended.shape[1:]
    heads = width // HEAD_DIM
    segs = rows // SEG
    narrow = pl.BlockSpec((1, SEG, width), lambda s, g: (s, g, 0))
    side_block = pl.BlockSpec((1, BASIS, 2 * width), lambda s, g: (s, 0, 0))
    return pl.pallas_call(
        attention_backward_kernel,
        grid=(2, segs),
        in_specs=[
            pl.BlockSpec(memory_space=pltpu.SMEM),
            pl.BlockSpec((1, SEG, 3 * width), lambda s, g: (s, g, 0)),
            pl.BlockSpec((1, 1, BASIS, 2 * width), lambda s, g: (g, s, 0, 0)),
            pl.BlockSpec((1, 1, heads, SEG), lambda s, g: (g, s, 0, 0)),
            narrow,
            narrow,
            pl.BlockSpec(near.shape, lambda s, g: (0, 0)),
            *(pl.BlockSpec(memory_space=pl.ANY) for _ in after),
        ],
        out_specs=[
            narrow,
            pl.BlockSpec((1, SEG, 2 * width), lambda s, g: (s, g, 0)),
            side_block,
            side_block,
        ],
        out_shape=[
            array((2, rows, width), BF16),
            array((2, rows, 2 * width), F32),
            array((2, BASIS, 2 * width), F32),
            array((2, BASIS, 2 * width), BF16),
        ],
        scratch_shapes=[pltpu.VMEM((BASIS, 2 * width), F32)],
        compiler_params=pltpu.CompilerParams(vmem_limit_bytes=VMEM_LIMIT),
        cost_estimate=cost(18),
    )(memory_bias, qkv, memory, log_totals, attended, grad, near, *after)


def memory_backward_kernel(
    place_ref,
    dq_ref,
    dkv_ref,
    last_ref,
    got_ref,
    near_ref,
    far_ref,
    *refs,
):
    width = dq_ref.shape[2]
    slabs_qk, slabs_vo, refs = split_attention(refs, width)
    grads_ref, part_ref, sums_ref, signal_ref = refs[-4:]
    segment = pl.program_id(0)

    def arrived(side):
        got = got_ref[1 - side]
        return jnp.where(place_ref[0] == 0, got.astype(F32), 0.0).astype(BF16)

    @pl.when(segment == 0)
    def _():
        for side in range(2):
            carry = last_ref[side] + dot(far_ref[:, :BASIS], arrived(side), TN)
            signal_ref[side] = dot(near_ref[:, BASIS:], carry.astype(BF16), TN)

    @pl.when(segment == 1)
    def _():
        for side in range(2):
            signal_ref[side] = dot(far_ref[:, BASIS:], arrived(side), TN)

    sides = []
    for side in range(2):
        grads_ref[side, :, :width] = dq_ref[side]
        grads_ref[side, :, width:] = (dkv_ref[side] + signal_ref[side]).astype(BF16)
        sides.append(grads_ref[side])
    slabs, low = slabs_qk
    part = unproject([side[:, : 2 * width] for side in sides], slabs, low, low + 2 * width)
    slabs, low = slabs_vo
    part = part + unproject([side[:, 2 * width :] for side in sides], slabs, low, low + width)
    part_ref[...] = part.astype(BF16)
    add_rows(sums_ref, [(side, sides[side].astype(F32)) for side in range(2)])


def memory_backward(place, dq, dkv, last, got, near, far, slabs, after):
    rows, width = dq.shape[1:]
    slab_arrays, slab_specs = slab_operands(slabs, 1)
    features = 2 * slab_arrays[0].shape[-2]
    whole = lambda a: pl.BlockSpec(a.shape, lambda g, p: (0,) * a.ndim)
    return pl.pallas_call(
        memory_backward_kernel,
        grid_spec=pltpu.PrefetchScalarGridSpec(
            num_scalar_prefetch=1,
            grid=(rows // SEG,),
            in_specs=[
                pl.BlockSpec((2, SEG, width), lambda g, p: (0, g, 0)),
                pl.BlockSpec((2, SEG, 2 * width), lambda g, p: (0, g, 0)),
                *(whole(a) for a in (last, got, near, far)),
                *slab_specs,
                *(pl.BlockSpec(memory_space=pl.ANY) for _ in after),
            ],
            out_specs=[
                pl.BlockSpec((2, SEG, 3 * width), lambda g, p: (0, g, 0)),
                pl.BlockSpec((SEG, features), lambda g, p: (g, 0)),
                pl.BlockSpec((8, 3 * width), lambda g, p: (0, 0)),
            ],
            scratch_shapes=[pltpu.VMEM((2, SEG, 2 * width), F32)],
        ),
        out_shape=[
            array((2, rows, 3 * width), BF16),
            array((rows, features), BF16),
            array((8, 3 * width), F32),
        ],
        compiler_params=pltpu.CompilerParams(vmem_limit_bytes=VMEM_LIMIT),
        cost_estimate=cost(5),
    )(place, dq, dkv, last, got, near, far, *slab_arrays, *after)


def weight_grads_kernel(plan, *refs):
    outs = refs[len(refs) - len(plan) :]
    for out_ref, slabs in zip(outs, plan):
        half = out_ref.shape[1]
        for index, products in enumerate(slabs):
            start = 0
            for left, turn, right, side, low, high in products:
                columns = slice(turn * half, (turn + 1) * half)
                result = dot(refs[left][:, columns], refs[right][side, :, low:high], TN)
                out_ref[index, :, start : start + high - low] = result.astype(BF16)
                start += high - low


def weight_grads(operands, plan, half, after=()):
    shapes = [
        array((2, half, sum(high - low for *_, low, high in slabs[0])), BF16) for slabs in plan
    ]
    vmem = pl.BlockSpec(memory_space=pltpu.VMEM)
    return pl.pallas_call(
        partial(weight_grads_kernel, plan),
        in_specs=[vmem] * len(operands) + [pl.BlockSpec(memory_space=pl.ANY)] * len(after),
        out_specs=[vmem] * len(plan),
        out_shape=shapes,
        compiler_params=pltpu.CompilerParams(vmem_limit_bytes=VMEM_LIMIT),
        cost_estimate=cost(6),
    )(*operands, *after)


GIVE_X = ((1, 0), (1, 1))
GIVE_Y = ((0, 1), (1, 1))
KEEP_X = ((0, 0), (0, 1))
KEEP_Y = ((0, 0), (1, 0))


def flip(array, axis):
    return lax.ppermute(array, axis, SWAP)


ALL_BUT_CORE = ("cy", "tx", "tz")


def gather_blocks(shard):
    whole = lax.all_gather(shard, ALL_BUT_CORE, axis=0, tiled=True)
    return whole.reshape(2, 2, -1, shard.shape[1])


def gather_z(shard):
    size = lax.axis_size("tz")
    spread = jnp.broadcast_to(shard[None], (size,) + shard.shape)
    return lax.all_to_all(spread, "tz", 0, 0, tiled=True).reshape(-1, shard.shape[1])


def join_kernel(here_ref, *refs):
    *pieces, first_ref, second_ref, zero_ref = refs
    rows = pieces[0].shape[0]
    columns = first_ref.shape[1]
    for bit, piece_ref in enumerate(pieces):
        place = pl.ds(pl.multiple_of((here_ref[0] ^ bit) * rows, rows), rows)
        first_ref[place, :] = piece_ref[:, :columns]
        second_ref[place, :] = piece_ref[:, columns:]
    zero_ref[...] = jnp.zeros_like(zero_ref)


def gather_split(shard, widths):
    size = lax.axis_size("tz")
    here = lax.axis_index("tz")
    pieces = [shift(shard, "tz", bit) if bit else shard for bit in range(size)]
    if shard.shape[0] % 16:
        rows = jnp.zeros((size,) + shard.shape, shard.dtype)
        for bit, piece in enumerate(pieces):
            rows = lax.dynamic_update_index_in_dim(rows, piece, here ^ bit, 0)
        return split_columns(rows.reshape(-1, shard.shape[1]), widths, ())
    vmem = pl.BlockSpec(memory_space=pltpu.VMEM)
    first, second, zero = pl.pallas_call(
        join_kernel,
        in_specs=[pl.BlockSpec(memory_space=pltpu.SMEM)] + [vmem] * size,
        out_specs=[vmem] * 3,
        out_shape=[array((size * shard.shape[0], columns), BF16) for columns in widths]
        + [array((8, 128), jnp.int32)],
        compiler_params=pltpu.CompilerParams(vmem_limit_bytes=VMEM_LIMIT),
        cost_estimate=cost(1),
    )(here.reshape(1).astype(jnp.int32), *pieces)
    return (first, second), zero[0, 0]


def shift(array, axis, bit):
    return lax.ppermute(array, axis, [(i, i ^ bit) for i in range(lax.axis_size(axis))])


def gather_second(two, axis):
    own, near = two
    far, both = flip(own, axis), flip(near, axis)
    return (own, far, near, both) if axis == "tx" else (own, near, far, both)


def pieces_of(parts, block_rows):
    total = jnp.concatenate(
        [sum(piece.astype(F32) for piece in three).astype(BF16) for three in parts], axis=1
    )
    return total.reshape(-1, block_rows, total.shape[-1])


def spread_pieces(pieces):
    return lax.all_to_all(pieces, "tz", 0, 0, tiled=True)


def butterfly(array, axes):
    for axis in axes:
        bit = 1
        while bit < lax.axis_size(axis):
            array = array + shift(array, axis, bit)
            bit *= 2
    return array


def adamw(weight, first, second, grad, rate, decay):
    first_new = FIRST_DECAY * first + (1.0 - FIRST_DECAY) * grad
    second_new = SECOND_DECAY * second + (1.0 - SECOND_DECAY) * grad * grad
    first_hat = first_new / (1.0 - FIRST_DECAY**STEP)
    second_hat = second_new / (1.0 - SECOND_DECAY**STEP)
    weight_new = weight * (1.0 - rate * decay) - rate * first_hat / (
        jnp.sqrt(second_hat) + ADAM_EPS
    )
    return (weight_new, first_new, second_new)


def shards(
    h_in,
    cotangent,
    carried,
    centres,
    sticky,
    flags,
    w_qkv,
    w_qkv_first,
    w_qkv_second,
    w_out_t,
    w_out_first,
    w_out_second,
    w_up,
    w_up_first,
    w_up_second,
    w_down_t,
    w_down_first,
    w_down_second,
    vec_d,
    vec_d_first,
    vec_d_second,
    vec_c,
    vec_c_first,
    vec_c_second,
):
    depth = lax.axis_size("tz")
    tok_count = depth * 2
    ch_count = 2 * lax.axis_size("cc")
    context = lax.axis_index("cy")
    core = lax.axis_index("cc")
    x_place = lax.axis_index("tx")
    block_rows = w_qkv.shape[2]
    width = w_qkv.shape[1 + 2] * 1
    features = h_in.shape[1]
    half = features // 2
    rows = h_in.shape[0] // 2
    hidden_own = w_up.shape[2]

    table_index = jnp.where(context == 0, core, 2)
    sticky_row = lax.dynamic_index_in_dim(sticky[0], table_index, 0, keepdims=False)
    old_basis, design = table_inputs(centres, sticky_row)

    def attention_members(layer):
        return [(w_qkv, layer), (w_out_t, layer)]

    def ffn_members(layer):
        return [(w_up, layer), (w_down_t, layer)]

    attn_shard = cast(attention_members(0))
    (qk_own, vo_own), zero = gather_split(attn_shard, (2 * width, 2 * width))
    qk_two, vo_two = (qk_own, flip(qk_own, "tx")), (vo_own, flip(vo_own, "cy"))
    ffn_rows = gather_z(cast(ffn_members(0), (attn_shard,)))
    (up_own, down_own), _ = split_columns(ffn_rows, (hidden_own, hidden_own), (qk_own,))
    up_two, down_two = (up_own, flip(up_own, "tx")), (down_own, flip(down_own, "cy"))
    above = cast(attention_members(1), (qk_own,))
    attn_slabs = [
        gather_second(qk_two, "cy") + gather_second(vo_two, "tx"),
        Gathered(gather_blocks(above), 4 * width, 0),
    ]
    ffn_slabs = [
        gather_second(up_two, "cy") + gather_second(down_two, "tx"),
        Gathered(gather_blocks(cast(ffn_members(1), (up_own,))), 2 * hidden_own, 0),
    ]
    table_own = make_tables(old_basis, design, (qk_own,))
    table_other = flip(table_own, "cc")
    table_near = jnp.where(core == 0, table_own, table_other)
    table_far = jnp.where(core == 0, table_other, table_own)

    x_place = x_place + zero
    late_context = context + zero
    spot = jnp.arange(features)
    turned = spot // half
    block_z = (spot % half) // block_rows
    source = block_z * (2 * block_rows) + jnp.where(
        turned == 0, x_place, 1 - x_place
    ) * block_rows + spot % block_rows
    order = (jnp.arange(features)[:, None] == source[None, :]).astype(BF16)
    order_wide = order.astype(F32)
    order_back = (source[:, None] == jnp.arange(features)[None, :]).astype(BF16)
    place = jnp.stack([context, x_place]).astype(jnp.int32)

    vec_c_other = flip(vec_c, "cy")
    gains = jnp.dot(
        vec_d.reshape(-1, features), order_wide, precision=PRECISE
    ).reshape(vec_d.shape)
    both_c = jnp.stack([vec_c, vec_c_other], axis=1)
    in_bias = jnp.concatenate(
        [both_c[:, :, 0], jnp.zeros_like(both_c[:, :, 0]), both_c[:, :, 1]], axis=-1
    )
    up_bias = both_c[:, :, 2:6].transpose(0, 1, 3, 2).reshape(LAYERS, 2, hidden_own)
    flag_on = flags[0] + zero > 0
    carried_own = carried[:, 0].reshape(LAYERS, BASIS, 2 * width)
    starts = jnp.stack([carried_own, flip(carried_own, "cy")], axis=1)
    starts = jnp.where(flag_on, starts, jnp.zeros_like(starts))
    memory_bias = jnp.stack(
        [jnp.where((context == 0) & ~flag_on, MASKED, 0.0), jnp.float32(0.0)]
    ).astype(F32)
    own_h = lax.dynamic_slice_in_dim(h_in, late_context * rows, rows, axis=0)
    own_cot = lax.dynamic_slice_in_dim(cotangent, late_context * rows, rows, axis=0)

    row_f32 = array((rows, features), F32)
    kept_f32 = kept((rows, features), F32)
    kept_b16 = kept((rows, features), BF16)
    kept_hidden = kept((2, rows, hidden_own), BF16)
    row_b16 = array((rows, features), BF16)
    side_hidden = array((2, rows, hidden_own), BF16)
    side_width = array((2, rows, width), BF16)
    sums_shape = array((8, features), F32)

    saved = []
    for layer in range(LAYERS):
        stream, normed, qkv, fit, ahead = rows_call(
            partial(enter_kernel, layer),
            place,
            (in_hbm(own_h),) if layer == 0 else (in_hbm(middle), part, got),
            ((order,) if layer == 0 else ()) + (gains, in_bias),
            attn_slabs[layer],
            (table_near, table_far, starts),
            (kept_f32, kept_b16, kept((2, rows, 3 * width), BF16)),
            (array((2, BASIS, 2 * width), F32), array((2, BASIS, 2 * width), BF16)),
            7,
            [pltpu.VMEM((2, rows, 2 * width), BF16)],
            after=(up_two[1], down_two[1]) if layer == 0 else (),
        )
        received = flip(ahead, "cy")
        out_slabs = attn_slabs[layer][4:] if layer == 0 else attn_slabs[layer]
        attended, log_totals, memory, part = attention_forward(
            layer, place, memory_bias, qkv, starts, received, fit, table_near, out_slabs,
            after=ffn_slabs[0][1:4] + ffn_slabs[0][5:8] if layer == 0 else (),
        )
        got = flip(part, "cc")
        middle, normed_two, active, slope, part = rows_call(
            partial(ffn_forward_kernel, layer),
            place,
            (in_hbm(stream), part, got),
            (gains, up_bias),
            ffn_slabs[layer],
            (),
            (kept_f32, kept_b16, kept_hidden, kept_hidden, row_b16),
            (),
            11,
        )
        got = flip(part, "cc")
        saved.append(
            tuple(in_hbm(member) for member in (
                stream,
                normed,
                qkv,
                memory,
                log_totals,
                attended,
                middle,
                normed_two,
                active,
                slope,
            ))
        )
    final = middle + (part.astype(F32) + got.astype(F32) + gains[LAYERS - 1, 5])
    final = lax.optimization_barrier(final.astype(BF16))
    outputs = final, flip(final, "cy")

    sums_ffn = [None] * (LAYERS + 1)
    sums_mix = [None] * LAYERS
    sums_in = [None] * LAYERS
    reduced = [None] * LAYERS

    def second_hop(keep_x, got_x, keep_y, got_y, after):
        pass_x, pass_y = pass_on(keep_x, got_x, keep_y, got_y, after)
        all_x = (keep_x[0], got_x[0], flip(pass_x, "cy"))
        all_y = (keep_y[0], got_y[0], flip(pass_y, "tx"))
        return pass_x, pieces_of((all_x, all_y), block_rows)

    zero_first = ()
    zero_mix = ()
    zero_attention = ()
    zero_memory = ()
    above_attention = None
    for layer in reversed(range(LAYERS)):
        (
            stream,
            normed,
            qkv,
            memory,
            log_totals,
            attended,
            middle,
            normed_two,
            active,
            slope,
        ) = saved[layer]
        top = layer == LAYERS - 1
        stream_grad, down, hidden_grad, part, sums_ffn[layer] = rows_call(
            partial(ffn_backward_kernel, layer),
            place,
            (in_hbm(own_cot), slope) if top else (stream_grad, stream_above, part, got, slope),
            (order if top else gains,),
            ffn_slabs[layer],
            (),
            (row_f32, row_b16, side_hidden, row_b16),
            (sums_shape,),
            9,
            after=zero_first,
        )
        got = flip(part, "cc")
        if above_attention is not None:
            qk_give, qk_keep, qk_got, vo_keep, vo_got = above_attention
            passed, attn_pieces = second_hop(qk_keep, qk_got, vo_keep, vo_got, (down,))
            zero_mix, zero_attention = (passed,), (attn_pieces,)
            reduced[layer + 1] = (spread_pieces(attn_pieces), spread_ffn)
            zero_memory = (spread_ffn,)
        ffn_operands = (normed_two, down, hidden_grad, active)
        ffn_plans = [
            [
                [[(0, x, 2, y, 0, hidden_own)] for x, y in pair_x],
                [[(1, x, 3, y, 0, hidden_own)] for x, y in pair_y],
            ]
            for pair_x, pair_y in ((GIVE_X, GIVE_Y), (KEEP_X, KEEP_Y))
        ]
        up_give, down_give = weight_grads(ffn_operands, ffn_plans[0], half)
        up_got, down_got = flip(up_give, "tx"), flip(down_give, "cy")
        stream_grad, branch_grad, attended_grad, sums_mix[layer] = rows_call(
            partial(mix_backward_kernel, layer),
            place,
            (stream_grad, middle, part, got),
            (gains,),
            attn_slabs[layer],
            (),
            (row_f32, row_b16, side_width),
            (sums_shape,),
            6,
            after=(up_give, *zero_mix),
        )
        dq, dkv, last, back = attention_backward(
            memory_bias, qkv, memory, log_totals, attended, attended_grad, table_near, zero_attention
        )
        received = flip(back, "cy")
        up_keep, down_keep = weight_grads(ffn_operands, ffn_plans[1], half, (dq,))
        passed, ffn_pieces = second_hop(up_keep, up_got, down_keep, down_got, (dq,))
        grads_in, part, sums_in[layer] = memory_backward(
            place, dq, dkv, last, received, table_near, table_far, attn_slabs[layer],
            (passed, *zero_memory),
        )
        got = flip(part, "cc")
        spread_ffn = spread_pieces(ffn_pieces)
        attn_plans = [
            [
                [[(0, x, 2, y, 0, 2 * width)] for x, y in pair_x],
                [
                    [(0, x, 2, y, 2 * width, 3 * width), (1, x, 3, y, 0, width)]
                    for x, y in pair_y
                ],
            ]
            for pair_x, pair_y in ((GIVE_X, GIVE_Y), (KEEP_X, KEEP_Y))
        ]
        attn_operands = (normed, branch_grad, grads_in, attended)
        qk_give, vo_give = weight_grads(attn_operands, attn_plans[0], half)
        qk_got, vo_got = flip(qk_give, "tx"), flip(vo_give, "cy")
        if layer > 0:
            qk_keep, vo_keep = weight_grads(attn_operands, attn_plans[1], half)
            above_attention = qk_give, qk_keep, qk_got, vo_keep, vo_got
            zero_first = (qk_give, ffn_pieces)
        stream_above = stream
    final, sums_ffn[LAYERS] = rows_call(
        leave_kernel,
        place,
        (stream_grad, stream, part, got),
        (gains,),
        None,
        (),
        (row_b16,),
        (sums_shape,),
        5,
        after=(qk_give, ffn_pieces),
    )
    qk_keep, vo_keep = weight_grads(attn_operands, attn_plans[1], half, (final,))
    passed, attn_pieces = second_hop(qk_keep, qk_got, vo_keep, vo_got, (final,))
    reduced[0] = (spread_pieces(attn_pieces), spread_ffn)
    reduced = [[piece.astype(F32).sum(axis=0) for piece in pair] for pair in reduced]
    activations, zero_act = restore(*outputs, order_back, place, (passed,))
    input_grad, zero_in = restore(final, flip(final, "cy"), order_back, place)

    vector_d = []
    vector_own = []
    vector_other = []
    for layer in range(LAYERS):
        below = sums_ffn[layer - 1] if layer > 0 else sums_ffn[LAYERS]
        vector_d.append(
            jnp.concatenate(
                [below[:2], sums_mix[layer][:3], sums_ffn[layer][2:3]], axis=0
            )
        )
        ups = sums_ffn[layer][3:5].reshape(2, width, 4).transpose(0, 2, 1)
        for side, out in enumerate((vector_own, vector_other)):
            sums = sums_in[layer][side]
            out.append(
                jnp.concatenate(
                    [sums[None, :width], sums[None, 2 * width :], ups[side]], axis=0
                )
            )
    qkv_grads = [
        jnp.stack([r[0][:, i * width : (i + 1) * width] for i in range(3)]) for r in reduced
    ]
    matrix_grads = (
        jnp.stack(qkv_grads),
        jnp.stack([r[0][:, 3 * width :] for r in reduced]),
        jnp.stack([r[1][:, :hidden_own] for r in reduced]),
        jnp.stack([r[1][:, hidden_own:] for r in reduced]),
    )
    vec_d_grad = jnp.dot(
        jnp.stack(vector_d).reshape(-1, features), order_wide.T, precision=PRECISE
    ).reshape(-1)
    own_c = jnp.stack(vector_own).reshape(-1)
    other_c = jnp.stack(vector_other).reshape(-1)
    arrived = flip(jnp.concatenate([vec_d_grad, other_c]), "cy")
    vector = butterfly(jnp.concatenate([vec_d_grad, own_c]) + arrived, ("tx", "tz"))
    vec_d_grad = vector[: vec_d.size].reshape(vec_d.shape)
    vec_c_grad = vector[vec_d.size :].reshape(vec_c.shape)

    square = sum(jnp.sum(grad * grad) for grad in matrix_grads)
    square = (
        square
        + zero_act[0, 0]
        + zero_in[0, 0]
        + jnp.sum(vec_d_grad * vec_d_grad) / (tok_count * ch_count)
        + jnp.sum(vec_c_grad * vec_c_grad) / tok_count
    )
    everywhere = ("tz", "tx", "cy", "cc")
    squares = lax.all_to_all(
        jnp.full((tok_count * ch_count, 128), square), everywhere, 0, 0, tiled=True
    )
    total_square = jnp.sum(squares[:, 0])
    grad_norm = jnp.sqrt(total_square)
    factor = CLIP_LIMIT / jnp.maximum(grad_norm, CLIP_LIMIT)
    attention_update = adamw(
        w_qkv, w_qkv_first, w_qkv_second, matrix_grads[0] * factor, RATE_QKV, WEIGHT_DECAY
    )
    output_update = adamw(
        w_out_t, w_out_first, w_out_second, matrix_grads[1] * factor, RATE_OUT, WEIGHT_DECAY
    )
    expand_update = adamw(
        w_up, w_up_first, w_up_second, matrix_grads[2] * factor, RATE_UP, WEIGHT_DECAY
    )
    reduce_update = adamw(
        w_down_t, w_down_first, w_down_second, matrix_grads[3] * factor, RATE_DOWN, WEIGHT_DECAY
    )
    width_update = adamw(vec_d, vec_d_first, vec_d_second, vec_d_grad * factor, RATE_VECTOR, 0.0)
    channel_update = adamw(vec_c, vec_c_first, vec_c_second, vec_c_grad * factor, RATE_VECTOR, 0.0)
    return (
        activations,
        input_grad,
        grad_norm,
        *attention_update,
        *output_update,
        *expand_update,
        *reduce_update,
        *width_update,
        *channel_update,
    )


def solution(mesh):
    tok, ch = mesh.shape["tok"], mesh.shape["ch"]
    fine = Mesh(mesh.devices.reshape(tok // 2, 2, 2, ch // 2), ("tz", "tx", "cy", "cc"))
    t, c = ("tz", "tx"), ("cy", "cc")
    cube = P(None, None, t, c)
    matrix = P(None, t, c)
    channel = P(None, None, c)
    return jax.shard_map(
        shards,
        mesh=fine,
        in_specs=(
            P(t, None),
            P(t, None),
            P(None, t, None, None, c),
            P(),
            P(t, None, None),
            P(t),
            *(cube,) * 3,
            *(matrix,) * 9,
            *(P(),) * 3,
            *(channel,) * 3,
        ),
        out_specs=(
            P(t, None),
            P(t, None),
            P(),
            *(cube,) * 3,
            *(matrix,) * 9,
            *(P(),) * 3,
            *(channel,) * 3,
        ),
        check_vma=False,
    )
```

```python
from functools import partial
from typing import NamedTuple

import jax
import jax.numpy as jnp
from jax import lax
from jax.experimental import pallas as pl
from jax.experimental.pallas import tpu as pltpu
from jax.sharding import Mesh
from jax.sharding import PartitionSpec as P

HEAD_DIM = 64
BASIS = 256
SAMPLES = 256
SEG = 512
SEGS = 4
CRES = 1024
LAYERS = 2
STEP = 10

PRECISE = lax.Precision.HIGHEST
STICKY_RATIO = 0.5
RIDGE_WEIGHT = 0.5
BASIS_WIDTH = 0.01
NORM_EPS = 1e-05
CLIP_LIMIT = 1.0
FIRST_DECAY = 0.9
SECOND_DECAY = 0.95
ADAM_EPS = 1e-08
WEIGHT_DECAY = 0.1
RATE_QKV = 0.05
RATE_OUT = 0.5
RATE_UP = 0.05
RATE_DOWN = 0.03
RATE_VECTOR = 0.5
MASKED = -1e30
GELU_A = 0.7978845608028654
GELU_B = 0.044715
F32 = jnp.float32
BF16 = jnp.bfloat16
SWAP = ((0, 1), (1, 0))
NN = (((1,), (0,)), ((), ()))
NT = (((1,), (1,)), ((), ()))
TN = (((0,), (0,)), ((), ()))


def dot(left, right, dims, precision=None):
    return lax.dot_general(left, right, dims, precision=precision, preferred_element_type=F32)


VMEM_LIMIT = 40 * 2**20
TILE = 512
QT = 256


def cost(micros):
    return pl.CostEstimate(flops=int(micros * 1.1e9), bytes_accessed=10**6, transcendentals=0)


def table_kernel(old_ref, design_ref, out_ref, inv_ref, gram_ref):
    design = design_ref[...]
    eye = (
        lax.broadcasted_iota(jnp.int32, (BASIS, BASIS), 0)
        == lax.broadcasted_iota(jnp.int32, (BASIS, BASIS), 1)
    ).astype(F32)
    gram = dot(design, design, NT, PRECISE) + RIDGE_WEIGHT * eye
    gram_ref[...] = gram
    bound = jnp.max(jnp.sum(jnp.abs(gram), axis=0))
    inv_ref[...] = eye * (1.0 / bound)

    def step(low):
        scale = 2.0 / (1.0 + low)
        now = inv_ref[...]
        inner = dot(gram_ref[...], now, NN, PRECISE)
        inv_ref[...] = scale * (2.0 * now - scale * dot(now, inner, NN, PRECISE))
        return 4.0 * low / ((1.0 + low) * (1.0 + low))

    lax.while_loop(lambda low: low < 0.999, step, 0.99 * RIDGE_WEIGHT / bound)
    for _ in range(2):
        now = inv_ref[...]
        inner = dot(gram_ref[...], now, NN, PRECISE)
        inv_ref[...] = 2.0 * now - dot(now, inner, NN, PRECISE)
    fitted = dot(inv_ref[...], design, NN, PRECISE)
    out_ref[:, BASIS:] = fitted[:, SAMPLES:].astype(BF16)
    out_ref[:, :BASIS] = dot(fitted[:, :SAMPLES], old_ref[...], NT, PRECISE).astype(BF16)


def basis_table(centres, times):
    middle = (centres.astype(F32) + 0.5) / CRES
    offset = (times[None, :] - middle[:, None]) / BASIS_WIDTH
    return jnp.exp(-0.5 * offset * offset)


def table_inputs(centres, sticky_row):
    token_times = STICKY_RATIO + (1.0 - STICKY_RATIO) * (jnp.arange(SEG).astype(F32) + 0.5) / SEG
    places = (sticky_row.astype(F32) + 0.5) / CRES
    return (
        basis_table(centres, places),
        basis_table(centres, jnp.concatenate([STICKY_RATIO * places, token_times])),
    )


def make_tables(old_basis, design, after):
    def body(old_ref, design_ref, *refs):
        table_kernel(old_ref, design_ref, *refs[len(after) :])

    vmem = pl.BlockSpec(memory_space=pltpu.VMEM)
    return pl.pallas_call(
        body,
        in_specs=[vmem, vmem] + [pl.BlockSpec(memory_space=pl.ANY)] * len(after),
        out_specs=vmem,
        out_shape=jax.ShapeDtypeStruct((BASIS, BASIS + SEG), BF16),
        scratch_shapes=[pltpu.VMEM((BASIS, BASIS), F32), pltpu.VMEM((BASIS, BASIS), F32)],
        compiler_params=pltpu.CompilerParams(vmem_limit_bytes=VMEM_LIMIT),
        cost_estimate=cost(14),
    )(old_basis, design, *after)


def slab_columns(slab, low, high):
    return slab[:, low:high] if len(slab.shape) == 2 else slab[0, 0, :, low:high]


def project(left, slabs, low, high):
    own, by_x, by_y, by_both = (slab_columns(slab, low, high) for slab in slabs)
    return (
        dot(left, jnp.concatenate([own, by_x], axis=0), NN),
        dot(left, jnp.concatenate([by_y, by_both], axis=0), NN),
    )


def unproject(sides, slabs, low, high):
    own, by_x, by_y, by_both = (slab_columns(slab, low, high) for slab in slabs)
    if (high - low) % 128 == 0:
        both = jnp.concatenate(sides, axis=1)
        weights = jnp.concatenate(
            [jnp.concatenate([own, by_y], axis=1), jnp.concatenate([by_x, by_both], axis=1)], axis=0
        )
        return dot(both, weights, NT)
    return jnp.concatenate(
        [
            dot(sides[0], own, NT) + dot(sides[1], by_y, NT),
            dot(sides[0], by_x, NT) + dot(sides[1], by_both, NT),
        ],
        axis=1,
    )


def split_attention(refs, width):
    if len(refs[0].shape) == 2:
        return (refs[:4], 0), (refs[4:8], 0), refs[8:]
    return (refs[:4], 0), (refs[:4], 2 * width), refs[4:]


def split_ffn(refs):
    if len(refs[0].shape) == 2:
        return (refs[:4], 0), (refs[4:8], 0), refs[8:]
    return (refs[:4], 0), (refs[:4], refs[0].shape[-1] // 2), refs[4:]


TURNS = ((0, 0), (0, 1), (1, 0), (1, 1))


def cast_kernel(count, out_ref_index, *refs):
    out_ref = refs[out_ref_index]
    start = 0
    for ref in refs[:count]:
        for index in range(ref.shape[1]):
            columns = ref.shape[3]
            out_ref[:, start : start + columns] = ref[0, index].astype(BF16)
            start += columns


def cast(members, after=()):
    members = [
        (weight if weight.ndim == 4 else weight[:, None], layer) for weight, layer in members
    ]
    rows = members[0][0].shape[2]
    columns = sum(weight.shape[1] * weight.shape[3] for weight, _ in members)
    return pl.pallas_call(
        partial(cast_kernel, len(members), len(members) + len(after)),
        grid=(1,),
        in_specs=[
            pl.BlockSpec((1,) + weight.shape[1:], lambda i, layer=layer: (layer, 0, 0, 0))
            for weight, layer in members
        ]
        + [pl.BlockSpec(memory_space=pl.ANY)] * len(after),
        out_specs=pl.BlockSpec((rows, columns), lambda i: (0, 0)),
        out_shape=array((rows, columns), BF16),
        compiler_params=pltpu.CompilerParams(vmem_limit_bytes=VMEM_LIMIT),
        cost_estimate=cost(1),
    )(*(weight for weight, _ in members), *after)


def split_kernel(count, rows_ref, *refs):
    start = 0
    outs = refs[len(refs) - count - 1 :]
    for out_ref in outs[:count]:
        columns = out_ref.shape[1]
        out_ref[...] = rows_ref[:, start : start + columns]
        start += columns
    outs[count][...] = jnp.zeros_like(outs[count])


def split_columns(rows, widths, after):
    vmem = pl.BlockSpec(memory_space=pltpu.VMEM)
    *groups, zero = pl.pallas_call(
        partial(split_kernel, len(widths)),
        in_specs=[vmem] + [pl.BlockSpec(memory_space=pl.ANY)] * len(after),
        out_specs=[vmem] * (len(widths) + 1),
        out_shape=[array((rows.shape[0], columns), rows.dtype) for columns in widths]
        + [array((8, 128), jnp.int32)],
        compiler_params=pltpu.CompilerParams(vmem_limit_bytes=VMEM_LIMIT),
        cost_estimate=cost(1),
    )(rows, *after)
    return groups, zero[0, 0]


def pass_kernel(keep_a_ref, got_a_ref, keep_b_ref, got_b_ref, *refs):
    for keep_ref, got_ref, out_ref in (
        (keep_a_ref, got_a_ref, refs[-2]),
        (keep_b_ref, got_b_ref, refs[-1]),
    ):
        out_ref[...] = (keep_ref[0].astype(F32) + got_ref[0].astype(F32)).astype(BF16)


def pass_on(keep_a, got_a, keep_b, got_b, after):
    def slab(a):
        return pl.BlockSpec((1,) + a.shape[1:], lambda i: (1, 0, 0))

    def out(a):
        return pl.BlockSpec(a.shape[1:], lambda i: (0, 0))

    return pl.pallas_call(
        pass_kernel,
        grid=(1,),
        in_specs=[slab(a) for a in (keep_a, got_a, keep_b, got_b)]
        + [pl.BlockSpec(memory_space=pl.ANY)] * len(after),
        out_specs=[out(keep_a), out(keep_b)],
        out_shape=[array(keep_a.shape[1:], BF16), array(keep_b.shape[1:], BF16)],
        compiler_params=pltpu.CompilerParams(vmem_limit_bytes=VMEM_LIMIT),
        cost_estimate=cost(2),
    )(keep_a, got_a, keep_b, got_b, *after)


class Gathered(NamedTuple):
    whole: jax.Array
    columns: int
    index: int


def slab_operands(slabs, grid_rank):
    def fixed(shape):
        return pl.BlockSpec(shape, lambda *a: (0,) * len(shape))

    if not isinstance(slabs, Gathered):
        return [in_hbm(slab) for slab in slabs], [fixed(slab.shape) for slab in slabs]
    whole, columns, index = slabs
    specs = []
    for turn_y, turn_x in TURNS:
        specs.append(
            pl.BlockSpec(
                (1, 1, whole.shape[2], columns),
                lambda *a, turn_y=turn_y, turn_x=turn_x: (
                    a[grid_rank][0] ^ turn_y,
                    a[grid_rank][1] ^ turn_x,
                    0,
                    index,
                ),
            )
        )
    return [in_hbm(whole)] * 4, specs


def norm_stats(inputs):
    centred = inputs - jnp.mean(inputs, axis=-1, keepdims=True)
    variance = jnp.mean(centred * centred, axis=-1, keepdims=True)
    rstd = lax.rsqrt(variance + NORM_EPS)
    return centred * rstd, rstd


def norm_backward(inputs, grad, gain_row):
    unit, rstd = norm_stats(inputs)
    scaled = grad * gain_row
    back = rstd * (
        scaled
        - jnp.mean(scaled, axis=-1, keepdims=True)
        - unit * jnp.mean(scaled * unit, axis=-1, keepdims=True)
    )
    return back, grad * unit


def both_parts(own_ref, got_ref):
    return own_ref[...].astype(F32) + got_ref[...].astype(F32)


def add_rows(ref, rows):
    @pl.when(pl.program_id(0) == 0)
    def _():
        ref[...] = jnp.zeros_like(ref)

    for index, row in rows:
        ref[index : index + 1, :] += jnp.sum(row, axis=0, keepdims=True)


def rows_call(
    kernel, place, tiled, whole, slabs, more, tiled_outs, whole_outs, micros, scratch=(), after=()
):
    rows = tiled[0].shape[-2]

    def tile_spec(shape):
        if len(shape) == 2:
            return pl.BlockSpec((TILE, shape[1]), lambda i, p: (i, 0))
        return pl.BlockSpec((shape[0], TILE, shape[2]), lambda i, p: (0, i, 0))

    def whole_spec(shape):
        return pl.BlockSpec(shape, lambda i, p: (0,) * len(shape))

    slab_arrays, slab_specs = slab_operands(slabs, 1) if slabs is not None else ([], [])

    taken = len(tiled) + len(whole) + len(slab_arrays) + len(more)

    def body(place_ref, *refs):
        kernel(*refs[:taken], *refs[taken + len(after) :])

    return pl.pallas_call(
        body,
        grid_spec=pltpu.PrefetchScalarGridSpec(
            num_scalar_prefetch=1,
            grid=(rows // TILE,),
            in_specs=[tile_spec(a.shape) for a in tiled]
            + [whole_spec(a.shape) for a in whole]
            + slab_specs
            + [whole_spec(a.shape) for a in more]
            + [pl.BlockSpec(memory_space=pl.ANY)] * len(after),
            out_specs=[tile_spec(a.shape) for a in tiled_outs]
            + [whole_spec(a.shape) for a in whole_outs],
            scratch_shapes=list(scratch),
        ),
        out_shape=[*tiled_outs, *whole_outs],
        compiler_params=pltpu.CompilerParams(vmem_limit_bytes=VMEM_LIMIT),
        cost_estimate=cost(micros),
    )(place, *tiled, *whole, *slab_arrays, *more, *after)


def in_hbm(operand):
    return pltpu.with_memory_space_constraint(operand, pltpu.HBM)


def kept(shape, dtype):
    return pltpu.HBM(shape, dtype)


def array(shape, dtype):
    return jax.ShapeDtypeStruct(shape, dtype)


def enter_kernel(layer, *refs):
    if layer == 0:
        h_ref, order_ref, gains_ref, bias_ref, *refs = refs
        stream = dot(h_ref[...], order_ref[...], NN)
    else:
        middle_ref, own_ref, got_ref, gains_ref, bias_ref, *refs = refs
        stream = middle_ref[...] + (both_parts(own_ref, got_ref) + gains_ref[layer - 1, 5:6, :])
    width = refs[-4].shape[2] // 3
    slabs_qk, slabs_vo, refs = split_attention(refs, width)
    near_ref, far_ref, start_ref, *refs = refs
    stream_ref, normed_ref, qkv_ref, fit_ref, ahead_ref, signal_ref = refs
    step = pl.program_id(0)
    stream_ref[...] = stream
    unit, _ = norm_stats(stream)
    normed = (unit * gains_ref[layer, 0:1, :] + gains_ref[layer, 1:2, :]).astype(BF16)
    normed_ref[...] = normed
    rows = pl.ds(pl.multiple_of(step * TILE, TILE), TILE)
    low = slabs_qk[1]
    queries_keys = project(normed, slabs_qk[0], low, low + 2 * width)
    low = slabs_vo[1]
    values = project(normed, slabs_vo[0], low, low + width)
    for side in range(2):
        result = jnp.concatenate([queries_keys[side], values[side]], axis=1)
        result = (result + bias_ref[layer, side : side + 1, :]).astype(BF16)
        qkv_ref[side] = result
        signal_ref[side, rows, :] = result[:, width:]

    @pl.when(step == pl.num_programs(0) - 1)
    def _():
        for side in range(2):
            fit_near = dot(near_ref[:, BASIS:], signal_ref[side, :SEG, :], NN)
            fit_far = dot(far_ref[:, BASIS:], signal_ref[side, SEG:, :], NN)
            fit_ref[side] = fit_near
            ahead = dot(near_ref[:, :BASIS], start_ref[layer, side], NN) + fit_near
            ahead = dot(far_ref[:, :BASIS], ahead.astype(BF16), NN) + fit_far
            ahead_ref[side] = ahead.astype(BF16)


def ffn_forward_kernel(layer, stream_ref, own_ref, got_ref, gains_ref, bias_ref, *refs):
    (up, up_low), (down, down_low), refs = split_ffn(refs)
    middle_ref, normed_ref, active_ref, slope_ref, part_ref = refs
    hidden_own = active_ref.shape[2]
    middle = stream_ref[...] + (both_parts(own_ref, got_ref) + gains_ref[layer, 4:5, :])
    middle_ref[...] = middle
    unit, _ = norm_stats(middle)
    normed = (unit * gains_ref[layer, 2:3, :] + gains_ref[layer, 3:4, :]).astype(BF16)
    normed_ref[...] = normed
    sides = []
    for side, hidden in enumerate(project(normed, up, up_low, up_low + hidden_own)):
        hidden = hidden + bias_ref[layer, side : side + 1, :]
        square = hidden * hidden
        bend = jnp.tanh(hidden * (GELU_A + (GELU_A * GELU_B) * square))
        half_more = 0.5 + 0.5 * bend
        active = (hidden * half_more).astype(BF16)
        slope = half_more + (0.5 - 0.5 * bend * bend) * hidden * (
            GELU_A + (3.0 * GELU_A * GELU_B) * square
        )
        active_ref[side] = active
        slope_ref[side] = slope.astype(BF16)
        sides.append(active)
    part_ref[...] = unproject(sides, down, down_low, down_low + hidden_own).astype(BF16)


def ffn_backward_kernel(layer, *refs):
    if layer == LAYERS - 1:
        cot_ref, slope_ref, order_ref, *refs = refs
        (up_slabs, up_low), (down_slabs, down_low), refs = split_ffn(refs)
        stream_grad = dot(cot_ref[...], order_ref[...], NN)
        grad_ref, down_ref, hidden_ref, part_ref, sums_ref = refs
        sums = []
    else:
        before_ref, stream_ref, own_ref, got_ref, slope_ref, gains_ref, *refs = refs
        (up_slabs, up_low), (down_slabs, down_low), refs = split_ffn(refs)
        grad_ref, down_ref, hidden_ref, part_ref, sums_ref = refs
        normed_grad = both_parts(own_ref, got_ref)
        back, gain_rows = norm_backward(
            stream_ref[...], normed_grad, gains_ref[layer + 1, 0:1, :]
        )
        stream_grad = before_ref[...] + back
        sums = [(0, gain_rows), (1, normed_grad)]
    hidden_own = slope_ref.shape[2]
    grad_ref[...] = stream_grad
    down = stream_grad.astype(BF16)
    down_ref[...] = down
    sums.append((2, down.astype(F32)))
    sides = []
    for side, active_grad in enumerate(project(down, down_slabs, down_low, down_low + hidden_own)):
        hidden_grad = (active_grad * slope_ref[side].astype(F32)).astype(BF16)
        hidden_ref[side] = hidden_grad
        sums.append((3 + side, hidden_grad.astype(F32)))
        sides.append(hidden_grad)
    part_ref[...] = unproject(sides, up_slabs, up_low, up_low + hidden_own).astype(BF16)
    add_rows(sums_ref, sums)


def mix_backward_kernel(layer, before_ref, middle_ref, own_ref, got_ref, gains_ref, *refs):
    width = refs[-2].shape[2]
    slabs_qk, (slabs, low), refs = split_attention(refs, width)
    grad_ref, branch_ref, attended_ref, sums_ref = refs
    normed_grad = both_parts(own_ref, got_ref)
    back, gain_rows = norm_backward(middle_ref[...], normed_grad, gains_ref[layer, 2:3, :])
    stream_grad = before_ref[...] + back
    grad_ref[...] = stream_grad
    branch = stream_grad.astype(BF16)
    branch_ref[...] = branch
    for side, result in enumerate(project(branch, slabs, low + width, low + 2 * width)):
        attended_ref[side] = result.astype(BF16)
    add_rows(sums_ref, [(0, gain_rows), (1, normed_grad), (2, branch.astype(F32))])


def leave_kernel(before_ref, stream_ref, own_ref, got_ref, gains_ref, grad_ref, sums_ref):
    normed_grad = both_parts(own_ref, got_ref)
    back, gain_rows = norm_backward(stream_ref[...], normed_grad, gains_ref[0, 0:1, :])
    grad_ref[...] = (before_ref[...] + back).astype(BF16)
    add_rows(sums_ref, [(0, gain_rows), (1, normed_grad)])


def zero_kernel(_, zero_ref):
    zero_ref[...] = jnp.zeros_like(zero_ref)


def zero_after(operand):
    return pl.pallas_call(
        zero_kernel,
        in_specs=[pl.BlockSpec(memory_space=pl.ANY)],
        out_specs=pl.BlockSpec(memory_space=pltpu.VMEM),
        out_shape=array((8, 128), F32),
        cost_estimate=cost(1),
    )(operand)[0, 0]


def restore_kernel(context_ref, own_ref, got_ref, order_ref, *refs):
    out_ref, zero_ref = refs[-2:]
    zero_ref[...] = jnp.zeros_like(zero_ref)
    mine = (pl.program_id(0) // (pl.num_programs(0) // 2)) == context_ref[0]
    rows = jnp.where(mine, own_ref[...].astype(F32), got_ref[...].astype(F32)).astype(BF16)
    out_ref[...] = dot(rows, order_ref[...], NN)


def restore(own, got, order, context, after=()):
    rows, features = own.shape
    tiles = rows // TILE
    block = pl.BlockSpec((TILE, features), lambda i: (i % tiles, 0))
    return pl.pallas_call(
        restore_kernel,
        grid=(2 * tiles,),
        in_specs=[
            pl.BlockSpec(memory_space=pltpu.SMEM),
            block,
            block,
            pl.BlockSpec(order.shape, lambda i: (0, 0)),
            *(pl.BlockSpec(memory_space=pl.ANY) for _ in after),
        ],
        out_specs=[
            pl.BlockSpec((TILE, features), lambda i: (i, 0)),
            pl.BlockSpec((8, 128), lambda i: (0, 0)),
        ],
        out_shape=[kept((2 * rows, features), F32), array((8, 128), F32)],
        compiler_params=pltpu.CompilerParams(vmem_limit_bytes=VMEM_LIMIT),
        cost_estimate=cost(4),
    )(context, own, got, order, *after)


def causal(shape):
    return lax.broadcasted_iota(jnp.int32, shape, 0) <= lax.broadcasted_iota(jnp.int32, shape, 1)


def head_lanes(kind, head, heads):
    low = (kind * heads + head) * HEAD_DIM
    return slice(low, low + HEAD_DIM)


def attention_forward_kernel(
    place_ref,
    bias_ref,
    qkv_ref,
    start_ref,
    got_ref,
    fit_ref,
    near_ref,
    *refs,
):
    slabs = refs[:4]
    out_ref, lse_ref, memory_ref, part_ref, rows_ref, total_ref = refs[-6:]
    segment, side = pl.program_id(0), pl.program_id(1)
    heads = qkv_ref.shape[2] // (3 * HEAD_DIM)
    width = heads * HEAD_DIM

    @pl.when(segment == 0)
    def _():
        @pl.when(place_ref[0] == 0)
        def _():
            rows_ref[side, 0] = start_ref[0, 0]

        @pl.when(place_ref[0] != 0)
        def _():
            rows_ref[side, 0] = got_ref[0]

        second = dot(near_ref[:, :BASIS], rows_ref[side, 0], NN) + fit_ref[0]
        rows_ref[side, 1] = second.astype(BF16)

    memory_ref[0, 0] = rows_ref[side, segment]
    memory_bias = bias_ref[segment]
    for tile in range(SEG // QT):
        rows = slice(tile * QT, (tile + 1) * QT)
        stacked = []
        for head in range(heads):
            lanes_q, lanes_k, lanes_v = (head_lanes(kind, head, heads) for kind in range(3))
            query = qkv_ref[0, rows, lanes_q] * HEAD_DIM ** (-0.5)
            keys = (tile + 1) * QT
            memory_key = rows_ref[side, segment, :, head_lanes(0, head, heads)]
            memory_value = rows_ref[side, segment, :, head_lanes(1, head, heads)]
            all_keys = jnp.concatenate([qkv_ref[0, :keys, lanes_k], memory_key], axis=0)
            all_values = jnp.concatenate([qkv_ref[0, :keys, lanes_v], memory_value], axis=0)
            score = dot(all_keys, query, NT)
            parts = [score[:keys - QT]] if tile else []
            parts.append(jnp.where(causal((QT, QT)), score[keys - QT : keys], MASKED))
            parts.append(score[keys:] + memory_bias)
            top = parts[0].max(axis=0, keepdims=True)
            for part in parts[1:]:
                top = jnp.maximum(top, part.max(axis=0, keepdims=True))
            weights = [jnp.exp(part - top) for part in parts]
            total = sum(weight.sum(axis=0, keepdims=True) for weight in weights)
            weights = jnp.concatenate([weight.astype(BF16) for weight in weights], axis=0)
            result = dot(all_values, weights, TN)
            stacked.append(result / total)
            lse_ref[0, 0, head : head + 1, rows] = top + jnp.log(total)
        out_ref[0, rows, :] = jnp.concatenate(stacked, axis=0).T.astype(BF16)
    attended = out_ref[0]
    low = slabs[0].shape[-1] - width
    own, by_x, by_y, by_both = (slab_columns(slab, low, low + width) for slab in slabs)

    @pl.when(side == 0)
    def _():
        total_ref[...] = jnp.concatenate(
            [dot(attended, own, NT), dot(attended, by_x, NT)], axis=1
        )

    @pl.when(side == 1)
    def _():
        part = total_ref[...] + jnp.concatenate(
            [dot(attended, by_y, NT), dot(attended, by_both, NT)],
            axis=1,
        )
        part_ref[...] = part.astype(BF16)


def attention_forward(layer, place, memory_bias, qkv, starts, got, fit, near, slabs, after=()):
    rows = qkv.shape[1]
    width = qkv.shape[2] // 3
    heads = width // HEAD_DIM
    segs = rows // SEG
    slab_arrays, slab_specs = slab_operands(slabs, 2)
    features = 2 * slab_arrays[0].shape[-2]
    return pl.pallas_call(
        attention_forward_kernel,
        grid_spec=pltpu.PrefetchScalarGridSpec(
            num_scalar_prefetch=1,
            grid=(segs, 2),
            in_specs=[
                pl.BlockSpec(memory_space=pltpu.SMEM),
                pl.BlockSpec((1, SEG, 3 * width), lambda g, s, p: (s, g, 0)),
                pl.BlockSpec((1, 1, BASIS, 2 * width), lambda g, s, p: (layer, s, 0, 0)),
                pl.BlockSpec((1, BASIS, 2 * width), lambda g, s, p: (1 - s, 0, 0)),
                pl.BlockSpec((1, BASIS, 2 * width), lambda g, s, p: (s, 0, 0)),
                pl.BlockSpec(near.shape, lambda g, s, p: (0, 0)),
                *slab_specs,
                *(pl.BlockSpec(memory_space=pl.ANY) for _ in after),
            ],
            out_specs=[
                pl.BlockSpec((1, SEG, width), lambda g, s, p: (s, g, 0)),
                pl.BlockSpec((1, 1, heads, SEG), lambda g, s, p: (g, s, 0, 0)),
                pl.BlockSpec((1, 1, BASIS, 2 * width), lambda g, s, p: (g, s, 0, 0)),
                pl.BlockSpec((SEG, features), lambda g, s, p: (g, 0)),
            ],
            scratch_shapes=[
                pltpu.VMEM((2, segs, BASIS, 2 * width), BF16),
                pltpu.VMEM((SEG, features), F32),
            ],
        ),
        out_shape=[
            kept((2, rows, width), BF16),
            kept((segs, 2, heads, SEG), F32),
            kept((segs, 2, BASIS, 2 * width), BF16),
            array((rows, features), BF16),
        ],
        compiler_params=pltpu.CompilerParams(vmem_limit_bytes=VMEM_LIMIT),
        cost_estimate=cost(13),
    )(place, memory_bias, in_hbm(qkv), starts, got, fit, near, *slab_arrays, *after)


def attention_backward_kernel(
    bias_ref,
    qkv_ref,
    memory_ref,
    lse_ref,
    out_ref,
    grad_ref,
    near_ref,
    *refs,
):
    dq_ref, dkv_ref, last_ref, back_ref, first_ref = refs[-5:]
    segment = pl.program_id(1)
    memory_bias = bias_ref[segment]
    heads = out_ref.shape[2] // HEAD_DIM
    scale = HEAD_DIM ** (-0.5)
    tiles = SEG // QT
    product = (out_ref[0].astype(F32) * grad_ref[0].astype(F32)).T
    query_grads = []
    for head in range(heads):
        lanes = head_lanes(0, head, heads)
        lanes_k, lanes_v = head_lanes(1, head, heads), head_lanes(2, head, heads)
        query = qkv_ref[0, :, lanes] * scale
        grad = grad_ref[0, :, lanes]
        dots = product[lanes, :].sum(axis=0, keepdims=True)
        log_total = lse_ref[0, 0, head : head + 1, :]
        all_keys = []
        score_grads = []
        for part in range(tiles + 1):
            start = part * QT if part < tiles else 0
            if part < tiles:
                keys = slice(start, start + QT)
                key, value = qkv_ref[0, keys, lanes_k], qkv_ref[0, keys, lanes_v]
            else:
                key = memory_ref[0, 0, :, head_lanes(0, head, heads)]
                value = memory_ref[0, 0, :, head_lanes(1, head, heads)]
            score = dot(key, query[start:], NT)
            if part < tiles:
                score = jnp.where(causal(score.shape), score, MASKED)
            else:
                score = score + memory_bias
            weight = jnp.exp(score - log_total[:, start:])
            weight_grad = dot(value, grad[start:], NT)
            score_grad = (weight * (weight_grad - dots[:, start:])).astype(BF16)
            value_grad = dot(weight.astype(BF16), grad[start:], NN)
            key_grad = dot(score_grad, query[start:], NN)
            all_keys.append(key)
            score_grads.append(score_grad)
            if part < tiles:
                dkv_ref[0, keys, head_lanes(0, head, heads)] = key_grad
                dkv_ref[0, keys, head_lanes(1, head, heads)] = value_grad
            else:
                last_ref[0, :, head_lanes(0, head, heads)] = key_grad
                last_ref[0, :, head_lanes(1, head, heads)] = value_grad
        head_grads = []
        for tile in range(tiles):
            members = [part for part in range(tiles + 1) if part <= tile or part == tiles]
            columns = [tile * QT - (part * QT if part < tiles else 0) for part in members]
            head_grads.append(
                dot(
                    jnp.concatenate([all_keys[part] for part in members], axis=0),
                    jnp.concatenate(
                        [score_grads[p][:, low : low + QT] for p, low in zip(members, columns)],
                        axis=0,
                    ),
                    TN,
                )
            )
        query_grads.append(jnp.concatenate(head_grads, axis=1) * scale)
    dq_ref[0] = jnp.concatenate(query_grads, axis=0).T.astype(BF16)

    @pl.when(segment == 0)
    def _():
        first_ref[...] = last_ref[0]

    @pl.when(segment == 1)
    def _():
        back = first_ref[...] + dot(near_ref[:, :BASIS], last_ref[0].astype(BF16), TN)
        back_ref[0] = back.astype(BF16)


def attention_backward(memory_bias, qkv, memory, log_totals, attended, grad, near, after):
    rows, width = attended.shape[1:]
    heads = width // HEAD_DIM
    segs = rows // SEG
    narrow = pl.BlockSpec((1, SEG, width), lambda s, g: (s, g, 0))
    side_block = pl.BlockSpec((1, BASIS, 2 * width), lambda s, g: (s, 0, 0))
    return pl.pallas_call(
        attention_backward_kernel,
        grid=(2, segs),
        in_specs=[
            pl.BlockSpec(memory_space=pltpu.SMEM),
            pl.BlockSpec((1, SEG, 3 * width), lambda s, g: (s, g, 0)),
            pl.BlockSpec((1, 1, BASIS, 2 * width), lambda s, g: (g, s, 0, 0)),
            pl.BlockSpec((1, 1, heads, SEG), lambda s, g: (g, s, 0, 0)),
            narrow,
            narrow,
            pl.BlockSpec(near.shape, lambda s, g: (0, 0)),
            *(pl.BlockSpec(memory_space=pl.ANY) for _ in after),
        ],
        out_specs=[
            narrow,
            pl.BlockSpec((1, SEG, 2 * width), lambda s, g: (s, g, 0)),
            side_block,
            side_block,
        ],
        out_shape=[
            array((2, rows, width), BF16),
            array((2, rows, 2 * width), F32),
            array((2, BASIS, 2 * width), F32),
            array((2, BASIS, 2 * width), BF16),
        ],
        scratch_shapes=[pltpu.VMEM((BASIS, 2 * width), F32)],
        compiler_params=pltpu.CompilerParams(vmem_limit_bytes=VMEM_LIMIT),
        cost_estimate=cost(18),
    )(memory_bias, qkv, memory, log_totals, attended, grad, near, *after)


def memory_backward_kernel(
    place_ref,
    dq_ref,
    dkv_ref,
    last_ref,
    got_ref,
    near_ref,
    far_ref,
    *refs,
):
    width = dq_ref.shape[2]
    slabs_qk, slabs_vo, refs = split_attention(refs, width)
    grads_ref, part_ref, sums_ref, signal_ref = refs[-4:]
    segment = pl.program_id(0)

    def arrived(side):
        got = got_ref[1 - side]
        return jnp.where(place_ref[0] == 0, got.astype(F32), 0.0).astype(BF16)

    @pl.when(segment == 0)
    def _():
        for side in range(2):
            carry = last_ref[side] + dot(far_ref[:, :BASIS], arrived(side), TN)
            signal_ref[side] = dot(near_ref[:, BASIS:], carry.astype(BF16), TN)

    @pl.when(segment == 1)
    def _():
        for side in range(2):
            signal_ref[side] = dot(far_ref[:, BASIS:], arrived(side), TN)

    sides = []
    for side in range(2):
        grads_ref[side, :, :width] = dq_ref[side]
        grads_ref[side, :, width:] = (dkv_ref[side] + signal_ref[side]).astype(BF16)
        sides.append(grads_ref[side])
    slabs, low = slabs_qk
    part = unproject([side[:, : 2 * width] for side in sides], slabs, low, low + 2 * width)
    slabs, low = slabs_vo
    part = part + unproject([side[:, 2 * width :] for side in sides], slabs, low, low + width)
    part_ref[...] = part.astype(BF16)
    add_rows(sums_ref, [(side, sides[side].astype(F32)) for side in range(2)])


def memory_backward(place, dq, dkv, last, got, near, far, slabs, after):
    rows, width = dq.shape[1:]
    slab_arrays, slab_specs = slab_operands(slabs, 1)
    features = 2 * slab_arrays[0].shape[-2]
    whole = lambda a: pl.BlockSpec(a.shape, lambda g, p: (0,) * a.ndim)
    return pl.pallas_call(
        memory_backward_kernel,
        grid_spec=pltpu.PrefetchScalarGridSpec(
            num_scalar_prefetch=1,
            grid=(rows // SEG,),
            in_specs=[
                pl.BlockSpec((2, SEG, width), lambda g, p: (0, g, 0)),
                pl.BlockSpec((2, SEG, 2 * width), lambda g, p: (0, g, 0)),
                *(whole(a) for a in (last, got, near, far)),
                *slab_specs,
                *(pl.BlockSpec(memory_space=pl.ANY) for _ in after),
            ],
            out_specs=[
                pl.BlockSpec((2, SEG, 3 * width), lambda g, p: (0, g, 0)),
                pl.BlockSpec((SEG, features), lambda g, p: (g, 0)),
                pl.BlockSpec((8, 3 * width), lambda g, p: (0, 0)),
            ],
            scratch_shapes=[pltpu.VMEM((2, SEG, 2 * width), F32)],
        ),
        out_shape=[
            array((2, rows, 3 * width), BF16),
            array((rows, features), BF16),
            array((8, 3 * width), F32),
        ],
        compiler_params=pltpu.CompilerParams(vmem_limit_bytes=VMEM_LIMIT),
        cost_estimate=cost(5),
    )(place, dq, dkv, last, got, near, far, *slab_arrays, *after)


def weight_grads_kernel(plan, *refs):
    outs = refs[len(refs) - len(plan) :]
    for out_ref, slabs in zip(outs, plan):
        half = out_ref.shape[1]
        for index, products in enumerate(slabs):
            start = 0
            for left, turn, right, side, low, high in products:
                columns = slice(turn * half, (turn + 1) * half)
                result = dot(refs[left][:, columns], refs[right][side, :, low:high], TN)
                out_ref[index, :, start : start + high - low] = result.astype(BF16)
                start += high - low


def weight_grads(operands, plan, half, after=()):
    shapes = [
        array((2, half, sum(high - low for *_, low, high in slabs[0])), BF16) for slabs in plan
    ]
    vmem = pl.BlockSpec(memory_space=pltpu.VMEM)
    return pl.pallas_call(
        partial(weight_grads_kernel, plan),
        in_specs=[vmem] * len(operands) + [pl.BlockSpec(memory_space=pl.ANY)] * len(after),
        out_specs=[vmem] * len(plan),
        out_shape=shapes,
        compiler_params=pltpu.CompilerParams(vmem_limit_bytes=VMEM_LIMIT),
        cost_estimate=cost(6),
    )(*operands, *after)


GIVE_X = ((1, 0), (1, 1))
GIVE_Y = ((0, 1), (1, 1))
KEEP_X = ((0, 0), (0, 1))
KEEP_Y = ((0, 0), (1, 0))


def flip(array, axis):
    return lax.ppermute(array, axis, SWAP)


ALL_BUT_CORE = ("cy", "tx", "tz")


def gather_blocks(shard):
    whole = lax.all_gather(shard, ALL_BUT_CORE, axis=0, tiled=True)
    return whole.reshape(2, 2, -1, shard.shape[1])


def gather_z(shard):
    size = lax.axis_size("tz")
    spread = jnp.broadcast_to(shard[None], (size,) + shard.shape)
    return lax.all_to_all(spread, "tz", 0, 0, tiled=True).reshape(-1, shard.shape[1])


def join_kernel(here_ref, *refs):
    *pieces, first_ref, second_ref, zero_ref = refs
    rows = pieces[0].shape[0]
    columns = first_ref.shape[1]
    for bit, piece_ref in enumerate(pieces):
        place = pl.ds(pl.multiple_of((here_ref[0] ^ bit) * rows, rows), rows)
        first_ref[place, :] = piece_ref[:, :columns]
        second_ref[place, :] = piece_ref[:, columns:]
    zero_ref[...] = jnp.zeros_like(zero_ref)


def gather_split(shard, widths):
    size = lax.axis_size("tz")
    here = lax.axis_index("tz")
    pieces = [shift(shard, "tz", bit) if bit else shard for bit in range(size)]
    if shard.shape[0] % 16:
        rows = jnp.zeros((size,) + shard.shape, shard.dtype)
        for bit, piece in enumerate(pieces):
            rows = lax.dynamic_update_index_in_dim(rows, piece, here ^ bit, 0)
        return split_columns(rows.reshape(-1, shard.shape[1]), widths, ())
    vmem = pl.BlockSpec(memory_space=pltpu.VMEM)
    first, second, zero = pl.pallas_call(
        join_kernel,
        in_specs=[pl.BlockSpec(memory_space=pltpu.SMEM)] + [vmem] * size,
        out_specs=[vmem] * 3,
        out_shape=[array((size * shard.shape[0], columns), BF16) for columns in widths]
        + [array((8, 128), jnp.int32)],
        compiler_params=pltpu.CompilerParams(vmem_limit_bytes=VMEM_LIMIT),
        cost_estimate=cost(1),
    )(here.reshape(1).astype(jnp.int32), *pieces)
    return (first, second), zero[0, 0]


def shift(array, axis, bit):
    return lax.ppermute(array, axis, [(i, i ^ bit) for i in range(lax.axis_size(axis))])


def gather_second(two, axis):
    own, near = two
    far, both = flip(own, axis), flip(near, axis)
    return (own, far, near, both) if axis == "tx" else (own, near, far, both)


def pieces_of(parts, block_rows):
    total = jnp.concatenate(
        [sum(piece.astype(F32) for piece in three).astype(BF16) for three in parts], axis=1
    )
    return total.reshape(-1, block_rows, total.shape[-1])


def spread_pieces(pieces):
    return lax.all_to_all(pieces, "tz", 0, 0, tiled=True)


def butterfly(array, axes):
    for axis in axes:
        bit = 1
        while bit < lax.axis_size(axis):
            array = array + shift(array, axis, bit)
            bit *= 2
    return array


def adamw(weight, first, second, grad, rate, decay):
    first_new = FIRST_DECAY * first + (1.0 - FIRST_DECAY) * grad
    second_new = SECOND_DECAY * second + (1.0 - SECOND_DECAY) * grad * grad
    first_hat = first_new / (1.0 - FIRST_DECAY**STEP)
    second_hat = second_new / (1.0 - SECOND_DECAY**STEP)
    weight_new = weight * (1.0 - rate * decay) - rate * first_hat / (
        jnp.sqrt(second_hat) + ADAM_EPS
    )
    return (weight_new, first_new, second_new)


def shards(
    h_in,
    cotangent,
    carried,
    centres,
    sticky,
    flags,
    w_qkv,
    w_qkv_first,
    w_qkv_second,
    w_out_t,
    w_out_first,
    w_out_second,
    w_up,
    w_up_first,
    w_up_second,
    w_down_t,
    w_down_first,
    w_down_second,
    vec_d,
    vec_d_first,
    vec_d_second,
    vec_c,
    vec_c_first,
    vec_c_second,
):
    depth = lax.axis_size("tz")
    tok_count = depth * 2
    ch_count = 2 * lax.axis_size("cc")
    context = lax.axis_index("cy")
    core = lax.axis_index("cc")
    x_place = lax.axis_index("tx")
    block_rows = w_qkv.shape[2]
    width = w_qkv.shape[1 + 2] * 1
    features = h_in.shape[1]
    half = features // 2
    rows = h_in.shape[0] // 2
    hidden_own = w_up.shape[2]

    table_index = jnp.where(context == 0, core, 2)
    sticky_row = lax.dynamic_index_in_dim(sticky[0], table_index, 0, keepdims=False)
    old_basis, design = table_inputs(centres, sticky_row)

    def attention_members(layer):
        return [(w_qkv, layer), (w_out_t, layer)]

    def ffn_members(layer):
        return [(w_up, layer), (w_down_t, layer)]

    attn_shard = cast(attention_members(0))
    (qk_own, vo_own), zero = gather_split(attn_shard, (2 * width, 2 * width))
    qk_two, vo_two = (qk_own, flip(qk_own, "tx")), (vo_own, flip(vo_own, "cy"))
    ffn_rows = gather_z(cast(ffn_members(0), (attn_shard,)))
    (up_own, down_own), _ = split_columns(ffn_rows, (hidden_own, hidden_own), (qk_own,))
    up_two, down_two = (up_own, flip(up_own, "tx")), (down_own, flip(down_own, "cy"))
    above = cast(attention_members(1), (qk_own,))
    attn_slabs = [
        gather_second(qk_two, "cy") + gather_second(vo_two, "tx"),
        Gathered(gather_blocks(above), 4 * width, 0),
    ]
    ffn_slabs = [
        gather_second(up_two, "cy") + gather_second(down_two, "tx"),
        Gathered(gather_blocks(cast(ffn_members(1), (up_own,))), 2 * hidden_own, 0),
    ]
    table_own = make_tables(old_basis, design, (qk_own,))
    table_other = flip(table_own, "cc")
    table_near = jnp.where(core == 0, table_own, table_other)
    table_far = jnp.where(core == 0, table_other, table_own)

    x_place = x_place + zero
    late_context = context + zero
    spot = jnp.arange(features)
    turned = spot // half
    block_z = (spot % half) // block_rows
    source = block_z * (2 * block_rows) + jnp.where(
        turned == 0, x_place, 1 - x_place
    ) * block_rows + spot % block_rows
    order = (jnp.arange(features)[:, None] == source[None, :]).astype(BF16)
    order_wide = order.astype(F32)
    order_back = (source[:, None] == jnp.arange(features)[None, :]).astype(BF16)
    place = jnp.stack([context, x_place]).astype(jnp.int32)

    vec_c_other = flip(vec_c, "cy")
    gains = jnp.dot(
        vec_d.reshape(-1, features), order_wide, precision=PRECISE
    ).reshape(vec_d.shape)
    both_c = jnp.stack([vec_c, vec_c_other], axis=1)
    in_bias = jnp.concatenate(
        [both_c[:, :, 0], jnp.zeros_like(both_c[:, :, 0]), both_c[:, :, 1]], axis=-1
    )
    up_bias = both_c[:, :, 2:6].transpose(0, 1, 3, 2).reshape(LAYERS, 2, hidden_own)
    flag_on = flags[0] + zero > 0
    carried_own = carried[:, 0].reshape(LAYERS, BASIS, 2 * width)
    starts = jnp.stack([carried_own, flip(carried_own, "cy")], axis=1)
    starts = jnp.where(flag_on, starts, jnp.zeros_like(starts))
    memory_bias = jnp.stack(
        [jnp.where((context == 0) & ~flag_on, MASKED, 0.0), jnp.float32(0.0)]
    ).astype(F32)
    own_h = lax.dynamic_slice_in_dim(h_in, late_context * rows, rows, axis=0)
    own_cot = lax.dynamic_slice_in_dim(cotangent, late_context * rows, rows, axis=0)

    row_f32 = array((rows, features), F32)
    kept_f32 = kept((rows, features), F32)
    kept_b16 = kept((rows, features), BF16)
    kept_hidden = kept((2, rows, hidden_own), BF16)
    row_b16 = array((rows, features), BF16)
    side_hidden = array((2, rows, hidden_own), BF16)
    side_width = array((2, rows, width), BF16)
    sums_shape = array((8, features), F32)

    saved = []
    for layer in range(LAYERS):
        stream, normed, qkv, fit, ahead = rows_call(
            partial(enter_kernel, layer),
            place,
            (in_hbm(own_h),) if layer == 0 else (in_hbm(middle), part, got),
            ((order,) if layer == 0 else ()) + (gains, in_bias),
            attn_slabs[layer],
            (table_near, table_far, starts),
            (kept_f32, kept_b16, kept((2, rows, 3 * width), BF16)),
            (array((2, BASIS, 2 * width), F32), array((2, BASIS, 2 * width), BF16)),
            7,
            [pltpu.VMEM((2, rows, 2 * width), BF16)],
            after=(up_two[1], down_two[1]) if layer == 0 else (),
        )
        received = flip(ahead, "cy")
        out_slabs = attn_slabs[layer][4:] if layer == 0 else attn_slabs[layer]
        attended, log_totals, memory, part = attention_forward(
            layer, place, memory_bias, qkv, starts, received, fit, table_near, out_slabs,
            after=ffn_slabs[0][1:4] + ffn_slabs[0][5:8] if layer == 0 else (),
        )
        got = flip(part, "cc")
        middle, normed_two, active, slope, part = rows_call(
            partial(ffn_forward_kernel, layer),
            place,
            (in_hbm(stream), part, got),
            (gains, up_bias),
            ffn_slabs[layer],
            (),
            (kept_f32, kept_b16, kept_hidden, kept_hidden, row_b16),
            (),
            11,
        )
        got = flip(part, "cc")
        saved.append(
            tuple(in_hbm(member) for member in (
                stream,
                normed,
                qkv,
                memory,
                log_totals,
                attended,
                middle,
                normed_two,
                active,
                slope,
            ))
        )
    final = middle + (part.astype(F32) + got.astype(F32) + gains[LAYERS - 1, 5])
    final = lax.optimization_barrier(final.astype(BF16))
    outputs = final, flip(final, "cy")

    sums_ffn = [None] * (LAYERS + 1)
    sums_mix = [None] * LAYERS
    sums_in = [None] * LAYERS
    reduced = [None] * LAYERS

    def second_hop(keep_x, got_x, keep_y, got_y, after):
        pass_x, pass_y = pass_on(keep_x, got_x, keep_y, got_y, after)
        all_x = (keep_x[0], got_x[0], flip(pass_x, "cy"))
        all_y = (keep_y[0], got_y[0], flip(pass_y, "tx"))
        return pass_x, pieces_of((all_x, all_y), block_rows)

    zero_first = ()
    zero_mix = ()
    zero_attention = ()
    zero_memory = ()
    above_attention = None
    for layer in reversed(range(LAYERS)):
        (
            stream,
            normed,
            qkv,
            memory,
            log_totals,
            attended,
            middle,
            normed_two,
            active,
            slope,
        ) = saved[layer]
        top = layer == LAYERS - 1
        stream_grad, down, hidden_grad, part, sums_ffn[layer] = rows_call(
            partial(ffn_backward_kernel, layer),
            place,
            (in_hbm(own_cot), slope) if top else (stream_grad, stream_above, part, got, slope),
            (order if top else gains,),
            ffn_slabs[layer],
            (),
            (row_f32, row_b16, side_hidden, row_b16),
            (sums_shape,),
            9,
            after=zero_first,
        )
        got = flip(part, "cc")
        if above_attention is not None:
            qk_give, qk_keep, qk_got, vo_keep, vo_got = above_attention
            passed, attn_pieces = second_hop(qk_keep, qk_got, vo_keep, vo_got, (down,))
            zero_mix, zero_attention = (passed,), (attn_pieces,)
            reduced[layer + 1] = (spread_pieces(attn_pieces), spread_ffn)
            zero_memory = (spread_ffn,)
        ffn_operands = (normed_two, down, hidden_grad, active)
        ffn_plans = [
            [
                [[(0, x, 2, y, 0, hidden_own)] for x, y in pair_x],
                [[(1, x, 3, y, 0, hidden_own)] for x, y in pair_y],
            ]
            for pair_x, pair_y in ((GIVE_X, GIVE_Y), (KEEP_X, KEEP_Y))
        ]
        up_give, down_give = weight_grads(ffn_operands, ffn_plans[0], half)
        up_got, down_got = flip(up_give, "tx"), flip(down_give, "cy")
        stream_grad, branch_grad, attended_grad, sums_mix[layer] = rows_call(
            partial(mix_backward_kernel, layer),
            place,
            (stream_grad, middle, part, got),
            (gains,),
            attn_slabs[layer],
            (),
            (row_f32, row_b16, side_width),
            (sums_shape,),
            6,
            after=(up_give, *zero_mix),
        )
        dq, dkv, last, back = attention_backward(
            memory_bias, qkv, memory, log_totals, attended, attended_grad, table_near, zero_attention
        )
        received = flip(back, "cy")
        up_keep, down_keep = weight_grads(ffn_operands, ffn_plans[1], half, (dq,))
        passed, ffn_pieces = second_hop(up_keep, up_got, down_keep, down_got, (dq,))
        grads_in, part, sums_in[layer] = memory_backward(
            place, dq, dkv, last, received, table_near, table_far, attn_slabs[layer],
            (passed, *zero_memory),
        )
        got = flip(part, "cc")
        spread_ffn = spread_pieces(ffn_pieces)
        attn_plans = [
            [
                [[(0, x, 2, y, 0, 2 * width)] for x, y in pair_x],
                [
                    [(0, x, 2, y, 2 * width, 3 * width), (1, x, 3, y, 0, width)]
                    for x, y in pair_y
                ],
            ]
            for pair_x, pair_y in ((GIVE_X, GIVE_Y), (KEEP_X, KEEP_Y))
        ]
        attn_operands = (normed, branch_grad, grads_in, attended)
        qk_give, vo_give = weight_grads(attn_operands, attn_plans[0], half)
        qk_got, vo_got = flip(qk_give, "tx"), flip(vo_give, "cy")
        if layer > 0:
            qk_keep, vo_keep = weight_grads(attn_operands, attn_plans[1], half)
            above_attention = qk_give, qk_keep, qk_got, vo_keep, vo_got
            zero_first = (qk_give, ffn_pieces)
        stream_above = stream
    final, sums_ffn[LAYERS] = rows_call(
        leave_kernel,
        place,
        (stream_grad, stream, part, got),
        (gains,),
        None,
        (),
        (row_b16,),
        (sums_shape,),
        5,
        after=(qk_give, ffn_pieces),
    )
    qk_keep, vo_keep = weight_grads(attn_operands, attn_plans[1], half, (final,))
    passed, attn_pieces = second_hop(qk_keep, qk_got, vo_keep, vo_got, (final,))
    reduced[0] = (spread_pieces(attn_pieces), spread_ffn)
    reduced = [[piece.astype(F32).sum(axis=0) for piece in pair] for pair in reduced]
    activations, zero_act = restore(*outputs, order_back, place, (passed,))
    final_got = flip(final, "cy")
    input_grad, _ = restore(final, final_got, order_back, place)

    vector_d = []
    vector_own = []
    vector_other = []
    for layer in range(LAYERS):
        below = sums_ffn[layer - 1] if layer > 0 else sums_ffn[LAYERS]
        vector_d.append(
            jnp.concatenate(
                [below[:2], sums_mix[layer][:3], sums_ffn[layer][2:3]], axis=0
            )
        )
        ups = sums_ffn[layer][3:5].reshape(2, width, 4).transpose(0, 2, 1)
        for side, out in enumerate((vector_own, vector_other)):
            sums = sums_in[layer][side]
            out.append(
                jnp.concatenate(
                    [sums[None, :width], sums[None, 2 * width :], ups[side]], axis=0
                )
            )
    qkv_grads = [
        jnp.stack([r[0][:, i * width : (i + 1) * width] for i in range(3)]) for r in reduced
    ]
    matrix_grads = (
        jnp.stack(qkv_grads),
        jnp.stack([r[0][:, 3 * width :] for r in reduced]),
        jnp.stack([r[1][:, :hidden_own] for r in reduced]),
        jnp.stack([r[1][:, hidden_own:] for r in reduced]),
    )
    vec_d_grad = jnp.dot(
        jnp.stack(vector_d).reshape(-1, features), order_wide.T, precision=PRECISE
    ).reshape(-1)
    own_c = jnp.stack(vector_own).reshape(-1)
    other_c = jnp.stack(vector_other).reshape(-1)
    arrived = flip(jnp.concatenate([vec_d_grad, other_c]), "cy")
    vector = butterfly(jnp.concatenate([vec_d_grad, own_c]) + arrived, ("tx", "tz"))
    vec_d_grad = vector[: vec_d.size].reshape(vec_d.shape)
    vec_c_grad = vector[vec_d.size :].reshape(vec_c.shape)

    square = sum(jnp.sum(grad * grad) for grad in matrix_grads)
    square = (
        square
        + zero_act[0, 0]
        + zero_after(final_got)
        + jnp.sum(vec_d_grad * vec_d_grad) / (tok_count * ch_count)
        + jnp.sum(vec_c_grad * vec_c_grad) / tok_count
    )
    everywhere = ("tz", "tx", "cy", "cc")
    squares = lax.all_to_all(
        jnp.full((tok_count * ch_count, 128), square), everywhere, 0, 0, tiled=True
    )
    total_square = jnp.sum(squares[:, 0])
    grad_norm = jnp.sqrt(total_square)
    factor = CLIP_LIMIT / jnp.maximum(grad_norm, CLIP_LIMIT)
    attention_update = adamw(
        w_qkv, w_qkv_first, w_qkv_second, matrix_grads[0] * factor, RATE_QKV, WEIGHT_DECAY
    )
    output_update = adamw(
        w_out_t, w_out_first, w_out_second, matrix_grads[1] * factor, RATE_OUT, WEIGHT_DECAY
    )
    expand_update = adamw(
        w_up, w_up_first, w_up_second, matrix_grads[2] * factor, RATE_UP, WEIGHT_DECAY
    )
    reduce_update = adamw(
        w_down_t, w_down_first, w_down_second, matrix_grads[3] * factor, RATE_DOWN, WEIGHT_DECAY
    )
    width_update = adamw(vec_d, vec_d_first, vec_d_second, vec_d_grad * factor, RATE_VECTOR, 0.0)
    channel_update = adamw(vec_c, vec_c_first, vec_c_second, vec_c_grad * factor, RATE_VECTOR, 0.0)
    return (
        activations,
        input_grad,
        grad_norm,
        *attention_update,
        *output_update,
        *expand_update,
        *reduce_update,
        *width_update,
        *channel_update,
    )


def solution(mesh):
    tok, ch = mesh.shape["tok"], mesh.shape["ch"]
    fine = Mesh(mesh.devices.reshape(tok // 2, 2, 2, ch // 2), ("tz", "tx", "cy", "cc"))
    t, c = ("tz", "tx"), ("cy", "cc")
    cube = P(None, None, t, c)
    matrix = P(None, t, c)
    channel = P(None, None, c)
    return jax.shard_map(
        shards,
        mesh=fine,
        in_specs=(
            P(t, None),
            P(t, None),
            P(None, t, None, None, c),
            P(),
            P(t, None, None),
            P(t),
            *(cube,) * 3,
            *(matrix,) * 9,
            *(P(),) * 3,
            *(channel,) * 3,
        ),
        out_specs=(
            P(t, None),
            P(t, None),
            P(),
            *(cube,) * 3,
            *(matrix,) * 9,
            *(P(),) * 3,
            *(channel,) * 3,
        ),
        check_vma=False,
    )
```

```python
from functools import partial
from typing import NamedTuple

import jax
import jax.numpy as jnp
from jax import lax
from jax.experimental import pallas as pl
from jax.experimental.pallas import tpu as pltpu
from jax.sharding import Mesh
from jax.sharding import PartitionSpec as P

HEAD_DIM = 64
BASIS = 256
SAMPLES = 256
SEG = 512
SEGS = 4
CRES = 1024
LAYERS = 2
STEP = 10

PRECISE = lax.Precision.HIGHEST
STICKY_RATIO = 0.5
RIDGE_WEIGHT = 0.5
BASIS_WIDTH = 0.01
NORM_EPS = 1e-05
CLIP_LIMIT = 1.0
FIRST_DECAY = 0.9
SECOND_DECAY = 0.95
ADAM_EPS = 1e-08
WEIGHT_DECAY = 0.1
RATE_QKV = 0.05
RATE_OUT = 0.5
RATE_UP = 0.05
RATE_DOWN = 0.03
RATE_VECTOR = 0.5
MASKED = -1e30
GELU_A = 0.7978845608028654
GELU_B = 0.044715
F32 = jnp.float32
BF16 = jnp.bfloat16
SWAP = ((0, 1), (1, 0))
NN = (((1,), (0,)), ((), ()))
NT = (((1,), (1,)), ((), ()))
TN = (((0,), (0,)), ((), ()))


def dot(left, right, dims, precision=None):
    return lax.dot_general(left, right, dims, precision=precision, preferred_element_type=F32)


VMEM_LIMIT = 32 * 2**20
TILE = 512
QT = 256


def cost(micros):
    return pl.CostEstimate(flops=int(micros * 1.1e9), bytes_accessed=10**6, transcendentals=0)


def table_kernel(old_ref, design_ref, out_ref, inv_ref, gram_ref):
    design = design_ref[...]
    eye = (
        lax.broadcasted_iota(jnp.int32, (BASIS, BASIS), 0)
        == lax.broadcasted_iota(jnp.int32, (BASIS, BASIS), 1)
    ).astype(F32)
    gram = dot(design, design, NT, PRECISE) + RIDGE_WEIGHT * eye
    gram_ref[...] = gram
    bound = jnp.max(jnp.sum(jnp.abs(gram), axis=0))
    inv_ref[...] = eye * (1.0 / bound)

    def step(low):
        scale = 2.0 / (1.0 + low)
        now = inv_ref[...]
        inner = dot(gram_ref[...], now, NN, PRECISE)
        inv_ref[...] = scale * (2.0 * now - scale * dot(now, inner, NN, PRECISE))
        return 4.0 * low / ((1.0 + low) * (1.0 + low))

    lax.while_loop(lambda low: low < 0.999, step, 0.99 * RIDGE_WEIGHT / bound)
    for _ in range(2):
        now = inv_ref[...]
        inner = dot(gram_ref[...], now, NN, PRECISE)
        inv_ref[...] = 2.0 * now - dot(now, inner, NN, PRECISE)
    fitted = dot(inv_ref[...], design, NN, PRECISE)
    out_ref[:, BASIS:] = fitted[:, SAMPLES:].astype(BF16)
    out_ref[:, :BASIS] = dot(fitted[:, :SAMPLES], old_ref[...], NT, PRECISE).astype(BF16)


def basis_table(centres, times):
    middle = (centres.astype(F32) + 0.5) / CRES
    offset = (times[None, :] - middle[:, None]) / BASIS_WIDTH
    return jnp.exp(-0.5 * offset * offset)


def table_inputs(centres, sticky_row):
    token_times = STICKY_RATIO + (1.0 - STICKY_RATIO) * (jnp.arange(SEG).astype(F32) + 0.5) / SEG
    places = (sticky_row.astype(F32) + 0.5) / CRES
    return (
        basis_table(centres, places),
        basis_table(centres, jnp.concatenate([STICKY_RATIO * places, token_times])),
    )


def make_tables(old_basis, design, after):
    def body(old_ref, design_ref, *refs):
        table_kernel(old_ref, design_ref, *refs[len(after) :])

    vmem = pl.BlockSpec(memory_space=pltpu.VMEM)
    return pl.pallas_call(
        body,
        in_specs=[vmem, vmem] + [pl.BlockSpec(memory_space=pl.ANY)] * len(after),
        out_specs=vmem,
        out_shape=jax.ShapeDtypeStruct((BASIS, BASIS + SEG), BF16),
        scratch_shapes=[pltpu.VMEM((BASIS, BASIS), F32), pltpu.VMEM((BASIS, BASIS), F32)],
        compiler_params=pltpu.CompilerParams(vmem_limit_bytes=VMEM_LIMIT),
        cost_estimate=cost(14),
    )(old_basis, design, *after)


def slab_columns(slab, low, high):
    return slab[:, low:high] if len(slab.shape) == 2 else slab[0, 0, :, low:high]


def project(left, slabs, low, high):
    own, by_x, by_y, by_both = (slab_columns(slab, low, high) for slab in slabs)
    return (
        dot(left, jnp.concatenate([own, by_x], axis=0), NN),
        dot(left, jnp.concatenate([by_y, by_both], axis=0), NN),
    )


def unproject(sides, slabs, low, high):
    own, by_x, by_y, by_both = (slab_columns(slab, low, high) for slab in slabs)
    if (high - low) % 128 == 0:
        both = jnp.concatenate(sides, axis=1)
        weights = jnp.concatenate(
            [jnp.concatenate([own, by_y], axis=1), jnp.concatenate([by_x, by_both], axis=1)], axis=0
        )
        return dot(both, weights, NT)
    return jnp.concatenate(
        [
            dot(sides[0], own, NT) + dot(sides[1], by_y, NT),
            dot(sides[0], by_x, NT) + dot(sides[1], by_both, NT),
        ],
        axis=1,
    )


def split_attention(refs, width):
    if len(refs[0].shape) == 2:
        return (refs[:4], 0), (refs[4:8], 0), refs[8:]
    return (refs[:4], 0), (refs[:4], 2 * width), refs[4:]


def split_ffn(refs):
    if len(refs[0].shape) == 2:
        return (refs[:4], 0), (refs[4:8], 0), refs[8:]
    return (refs[:4], 0), (refs[:4], refs[0].shape[-1] // 2), refs[4:]


TURNS = ((0, 0), (0, 1), (1, 0), (1, 1))


def cast_kernel(count, out_ref_index, *refs):
    out_ref = refs[out_ref_index]
    start = 0
    for ref in refs[:count]:
        for index in range(ref.shape[1]):
            columns = ref.shape[3]
            out_ref[:, start : start + columns] = ref[0, index].astype(BF16)
            start += columns


def cast(members, after=()):
    members = [
        (weight if weight.ndim == 4 else weight[:, None], layer) for weight, layer in members
    ]
    rows = members[0][0].shape[2]
    columns = sum(weight.shape[1] * weight.shape[3] for weight, _ in members)
    return pl.pallas_call(
        partial(cast_kernel, len(members), len(members) + len(after)),
        grid=(1,),
        in_specs=[
            pl.BlockSpec((1,) + weight.shape[1:], lambda i, layer=layer: (layer, 0, 0, 0))
            for weight, layer in members
        ]
        + [pl.BlockSpec(memory_space=pl.ANY)] * len(after),
        out_specs=pl.BlockSpec((rows, columns), lambda i: (0, 0)),
        out_shape=array((rows, columns), BF16),
        compiler_params=pltpu.CompilerParams(vmem_limit_bytes=VMEM_LIMIT),
        cost_estimate=cost(1),
    )(*(weight for weight, _ in members), *after)


def split_kernel(count, rows_ref, *refs):
    start = 0
    outs = refs[len(refs) - count - 1 :]
    for out_ref in outs[:count]:
        columns = out_ref.shape[1]
        out_ref[...] = rows_ref[:, start : start + columns]
        start += columns
    outs[count][...] = jnp.zeros_like(outs[count])


def split_columns(rows, widths, after):
    vmem = pl.BlockSpec(memory_space=pltpu.VMEM)
    *groups, zero = pl.pallas_call(
        partial(split_kernel, len(widths)),
        in_specs=[vmem] + [pl.BlockSpec(memory_space=pl.ANY)] * len(after),
        out_specs=[vmem] * (len(widths) + 1),
        out_shape=[array((rows.shape[0], columns), rows.dtype) for columns in widths]
        + [array((8, 128), jnp.int32)],
        compiler_params=pltpu.CompilerParams(vmem_limit_bytes=VMEM_LIMIT),
        cost_estimate=cost(1),
    )(rows, *after)
    return groups, zero[0, 0]


def pass_kernel(keep_a_ref, got_a_ref, keep_b_ref, got_b_ref, *refs):
    for keep_ref, got_ref, out_ref in (
        (keep_a_ref, got_a_ref, refs[-2]),
        (keep_b_ref, got_b_ref, refs[-1]),
    ):
        out_ref[...] = (keep_ref[0].astype(F32) + got_ref[0].astype(F32)).astype(BF16)


def pass_on(keep_a, got_a, keep_b, got_b, after):
    def slab(a):
        return pl.BlockSpec((1,) + a.shape[1:], lambda i: (1, 0, 0))

    def out(a):
        return pl.BlockSpec(a.shape[1:], lambda i: (0, 0))

    return pl.pallas_call(
        pass_kernel,
        grid=(1,),
        in_specs=[slab(a) for a in (keep_a, got_a, keep_b, got_b)]
        + [pl.BlockSpec(memory_space=pl.ANY)] * len(after),
        out_specs=[out(keep_a), out(keep_b)],
        out_shape=[array(keep_a.shape[1:], BF16), array(keep_b.shape[1:], BF16)],
        compiler_params=pltpu.CompilerParams(vmem_limit_bytes=VMEM_LIMIT),
        cost_estimate=cost(2),
    )(keep_a, got_a, keep_b, got_b, *after)


class Gathered(NamedTuple):
    whole: jax.Array
    columns: int
    index: int


def slab_operands(slabs, grid_rank):
    def fixed(shape):
        return pl.BlockSpec(shape, lambda *a: (0,) * len(shape))

    if not isinstance(slabs, Gathered):
        return [in_hbm(slab) for slab in slabs], [fixed(slab.shape) for slab in slabs]
    whole, columns, index = slabs
    specs = []
    for turn_y, turn_x in TURNS:
        specs.append(
            pl.BlockSpec(
                (1, 1, whole.shape[2], columns),
                lambda *a, turn_y=turn_y, turn_x=turn_x: (
                    a[grid_rank][0] ^ turn_y,
                    a[grid_rank][1] ^ turn_x,
                    0,
                    index,
                ),
            )
        )
    return [in_hbm(whole)] * 4, specs


def norm_stats(inputs):
    centred = inputs - jnp.mean(inputs, axis=-1, keepdims=True)
    variance = jnp.mean(centred * centred, axis=-1, keepdims=True)
    rstd = lax.rsqrt(variance + NORM_EPS)
    return centred * rstd, rstd


def norm_backward(inputs, grad, gain_row):
    unit, rstd = norm_stats(inputs)
    scaled = grad * gain_row
    back = rstd * (
        scaled
        - jnp.mean(scaled, axis=-1, keepdims=True)
        - unit * jnp.mean(scaled * unit, axis=-1, keepdims=True)
    )
    return back, grad * unit


def both_parts(own_ref, got_ref):
    return own_ref[...].astype(F32) + got_ref[...].astype(F32)


def add_rows(ref, rows):
    @pl.when(pl.program_id(0) == 0)
    def _():
        ref[...] = jnp.zeros_like(ref)

    for index, row in rows:
        ref[index : index + 1, :] += jnp.sum(row, axis=0, keepdims=True)


def rows_call(
    kernel, place, tiled, whole, slabs, more, tiled_outs, whole_outs, micros, scratch=(), after=()
):
    rows = tiled[0].shape[-2]

    def tile_spec(shape):
        if len(shape) == 2:
            return pl.BlockSpec((TILE, shape[1]), lambda i, p: (i, 0))
        return pl.BlockSpec((shape[0], TILE, shape[2]), lambda i, p: (0, i, 0))

    def whole_spec(shape):
        return pl.BlockSpec(shape, lambda i, p: (0,) * len(shape))

    slab_arrays, slab_specs = slab_operands(slabs, 1) if slabs is not None else ([], [])

    taken = len(tiled) + len(whole) + len(slab_arrays) + len(more)

    def body(place_ref, *refs):
        kernel(*refs[:taken], *refs[taken + len(after) :])

    return pl.pallas_call(
        body,
        grid_spec=pltpu.PrefetchScalarGridSpec(
            num_scalar_prefetch=1,
            grid=(rows // TILE,),
            in_specs=[tile_spec(a.shape) for a in tiled]
            + [whole_spec(a.shape) for a in whole]
            + slab_specs
            + [whole_spec(a.shape) for a in more]
            + [pl.BlockSpec(memory_space=pl.ANY)] * len(after),
            out_specs=[tile_spec(a.shape) for a in tiled_outs]
            + [whole_spec(a.shape) for a in whole_outs],
            scratch_shapes=list(scratch),
        ),
        out_shape=[*tiled_outs, *whole_outs],
        compiler_params=pltpu.CompilerParams(vmem_limit_bytes=VMEM_LIMIT),
        cost_estimate=cost(micros),
    )(place, *tiled, *whole, *slab_arrays, *more, *after)


def in_hbm(operand):
    return pltpu.with_memory_space_constraint(operand, pltpu.HBM)


def kept(shape, dtype):
    return pltpu.HBM(shape, dtype)


def array(shape, dtype):
    return jax.ShapeDtypeStruct(shape, dtype)


def enter_kernel(layer, *refs):
    if layer == 0:
        h_ref, order_ref, gains_ref, bias_ref, *refs = refs
        stream = dot(h_ref[...], order_ref[...], NN)
    else:
        middle_ref, own_ref, got_ref, gains_ref, bias_ref, *refs = refs
        stream = middle_ref[...] + (both_parts(own_ref, got_ref) + gains_ref[layer - 1, 5:6, :])
    width = refs[-4].shape[2] // 3
    slabs_qk, slabs_vo, refs = split_attention(refs, width)
    near_ref, far_ref, start_ref, *refs = refs
    stream_ref, normed_ref, qkv_ref, fit_ref, ahead_ref, signal_ref = refs
    step = pl.program_id(0)
    stream_ref[...] = stream
    unit, _ = norm_stats(stream)
    normed = (unit * gains_ref[layer, 0:1, :] + gains_ref[layer, 1:2, :]).astype(BF16)
    normed_ref[...] = normed
    rows = pl.ds(pl.multiple_of(step * TILE, TILE), TILE)
    low = slabs_qk[1]
    queries_keys = project(normed, slabs_qk[0], low, low + 2 * width)
    low = slabs_vo[1]
    values = project(normed, slabs_vo[0], low, low + width)
    for side in range(2):
        result = jnp.concatenate([queries_keys[side], values[side]], axis=1)
        result = (result + bias_ref[layer, side : side + 1, :]).astype(BF16)
        qkv_ref[side] = result
        signal_ref[side, rows, :] = result[:, width:]

    @pl.when(step == pl.num_programs(0) - 1)
    def _():
        for side in range(2):
            fit_near = dot(near_ref[:, BASIS:], signal_ref[side, :SEG, :], NN)
            fit_far = dot(far_ref[:, BASIS:], signal_ref[side, SEG:, :], NN)
            fit_ref[side] = fit_near
            ahead = dot(near_ref[:, :BASIS], start_ref[layer, side], NN) + fit_near
            ahead = dot(far_ref[:, :BASIS], ahead.astype(BF16), NN) + fit_far
            ahead_ref[side] = ahead.astype(BF16)


def ffn_forward_kernel(layer, stream_ref, own_ref, got_ref, gains_ref, bias_ref, *refs):
    (up, up_low), (down, down_low), refs = split_ffn(refs)
    middle_ref, normed_ref, active_ref, slope_ref, part_ref = refs
    hidden_own = active_ref.shape[2]
    middle = stream_ref[...] + (both_parts(own_ref, got_ref) + gains_ref[layer, 4:5, :])
    middle_ref[...] = middle
    unit, _ = norm_stats(middle)
    normed = (unit * gains_ref[layer, 2:3, :] + gains_ref[layer, 3:4, :]).astype(BF16)
    normed_ref[...] = normed
    sides = []
    for side, hidden in enumerate(project(normed, up, up_low, up_low + hidden_own)):
        hidden = hidden + bias_ref[layer, side : side + 1, :]
        square = hidden * hidden
        bend = jnp.tanh(hidden * (GELU_A + (GELU_A * GELU_B) * square))
        half_more = 0.5 + 0.5 * bend
        active = (hidden * half_more).astype(BF16)
        slope = half_more + (0.5 - 0.5 * bend * bend) * hidden * (
            GELU_A + (3.0 * GELU_A * GELU_B) * square
        )
        active_ref[side] = active
        slope_ref[side] = slope.astype(BF16)
        sides.append(active)
    part_ref[...] = unproject(sides, down, down_low, down_low + hidden_own).astype(BF16)


def ffn_backward_kernel(layer, *refs):
    if layer == LAYERS - 1:
        cot_ref, slope_ref, order_ref, *refs = refs
        (up_slabs, up_low), (down_slabs, down_low), refs = split_ffn(refs)
        stream_grad = dot(cot_ref[...], order_ref[...], NN)
        grad_ref, down_ref, hidden_ref, part_ref, sums_ref = refs
        sums = []
    else:
        before_ref, stream_ref, own_ref, got_ref, slope_ref, gains_ref, *refs = refs
        (up_slabs, up_low), (down_slabs, down_low), refs = split_ffn(refs)
        grad_ref, down_ref, hidden_ref, part_ref, sums_ref = refs
        normed_grad = both_parts(own_ref, got_ref)
        back, gain_rows = norm_backward(
            stream_ref[...], normed_grad, gains_ref[layer + 1, 0:1, :]
        )
        stream_grad = before_ref[...] + back
        sums = [(0, gain_rows), (1, normed_grad)]
    hidden_own = slope_ref.shape[2]
    grad_ref[...] = stream_grad
    down = stream_grad.astype(BF16)
    down_ref[...] = down
    sums.append((2, down.astype(F32)))
    sides = []
    for side, active_grad in enumerate(project(down, down_slabs, down_low, down_low + hidden_own)):
        hidden_grad = (active_grad * slope_ref[side].astype(F32)).astype(BF16)
        hidden_ref[side] = hidden_grad
        sums.append((3 + side, hidden_grad.astype(F32)))
        sides.append(hidden_grad)
    part_ref[...] = unproject(sides, up_slabs, up_low, up_low + hidden_own).astype(BF16)
    add_rows(sums_ref, sums)


def mix_backward_kernel(layer, before_ref, middle_ref, own_ref, got_ref, gains_ref, *refs):
    width = refs[-2].shape[2]
    slabs_qk, (slabs, low), refs = split_attention(refs, width)
    grad_ref, branch_ref, attended_ref, sums_ref = refs
    normed_grad = both_parts(own_ref, got_ref)
    back, gain_rows = norm_backward(middle_ref[...], normed_grad, gains_ref[layer, 2:3, :])
    stream_grad = before_ref[...] + back
    grad_ref[...] = stream_grad
    branch = stream_grad.astype(BF16)
    branch_ref[...] = branch
    for side, result in enumerate(project(branch, slabs, low + width, low + 2 * width)):
        attended_ref[side] = result.astype(BF16)
    add_rows(sums_ref, [(0, gain_rows), (1, normed_grad), (2, branch.astype(F32))])


def leave_kernel(before_ref, stream_ref, own_ref, got_ref, gains_ref, grad_ref, sums_ref):
    normed_grad = both_parts(own_ref, got_ref)
    back, gain_rows = norm_backward(stream_ref[...], normed_grad, gains_ref[0, 0:1, :])
    grad_ref[...] = (before_ref[...] + back).astype(BF16)
    add_rows(sums_ref, [(0, gain_rows), (1, normed_grad)])


def zero_kernel(_, zero_ref):
    zero_ref[...] = jnp.zeros_like(zero_ref)


def zero_after(operand):
    return pl.pallas_call(
        zero_kernel,
        in_specs=[pl.BlockSpec(memory_space=pl.ANY)],
        out_specs=pl.BlockSpec(memory_space=pltpu.VMEM),
        out_shape=array((8, 128), F32),
        cost_estimate=cost(1),
    )(operand)[0, 0]


def restore_kernel(context_ref, own_ref, got_ref, order_ref, *refs):
    out_ref, zero_ref = refs[-2:]
    zero_ref[...] = jnp.zeros_like(zero_ref)
    mine = (pl.program_id(0) // (pl.num_programs(0) // 2)) == context_ref[0]
    rows = jnp.where(mine, own_ref[...].astype(F32), got_ref[...].astype(F32)).astype(BF16)
    out_ref[...] = dot(rows, order_ref[...], NN)


def restore(own, got, order, context, after=()):
    rows, features = own.shape
    tiles = rows // TILE
    block = pl.BlockSpec((TILE, features), lambda i: (i % tiles, 0))
    return pl.pallas_call(
        restore_kernel,
        grid=(2 * tiles,),
        in_specs=[
            pl.BlockSpec(memory_space=pltpu.SMEM),
            block,
            block,
            pl.BlockSpec(order.shape, lambda i: (0, 0)),
            *(pl.BlockSpec(memory_space=pl.ANY) for _ in after),
        ],
        out_specs=[
            pl.BlockSpec((TILE, features), lambda i: (i, 0)),
            pl.BlockSpec((8, 128), lambda i: (0, 0)),
        ],
        out_shape=[kept((2 * rows, features), F32), array((8, 128), F32)],
        compiler_params=pltpu.CompilerParams(vmem_limit_bytes=VMEM_LIMIT),
        cost_estimate=cost(4),
    )(context, own, got, order, *after)


def causal(shape):
    return lax.broadcasted_iota(jnp.int32, shape, 0) <= lax.broadcasted_iota(jnp.int32, shape, 1)


def head_lanes(kind, head, heads):
    low = (kind * heads + head) * HEAD_DIM
    return slice(low, low + HEAD_DIM)


def attention_forward_kernel(
    place_ref,
    bias_ref,
    qkv_ref,
    start_ref,
    got_ref,
    fit_ref,
    near_ref,
    *refs,
):
    slabs = refs[:4]
    out_ref, lse_ref, memory_ref, part_ref, rows_ref, total_ref = refs[-6:]
    segment, side = pl.program_id(0), pl.program_id(1)
    heads = qkv_ref.shape[2] // (3 * HEAD_DIM)
    width = heads * HEAD_DIM

    @pl.when(segment == 0)
    def _():
        @pl.when(place_ref[0] == 0)
        def _():
            rows_ref[side, 0] = start_ref[0, 0]

        @pl.when(place_ref[0] != 0)
        def _():
            rows_ref[side, 0] = got_ref[0]

        second = dot(near_ref[:, :BASIS], rows_ref[side, 0], NN) + fit_ref[0]
        rows_ref[side, 1] = second.astype(BF16)

    memory_ref[0, 0] = rows_ref[side, segment]
    memory_bias = bias_ref[segment]
    for tile in range(SEG // QT):
        rows = slice(tile * QT, (tile + 1) * QT)
        stacked = []
        for head in range(heads):
            lanes_q, lanes_k, lanes_v = (head_lanes(kind, head, heads) for kind in range(3))
            query = qkv_ref[0, rows, lanes_q] * HEAD_DIM ** (-0.5)
            keys = (tile + 1) * QT
            memory_key = rows_ref[side, segment, :, head_lanes(0, head, heads)]
            memory_value = rows_ref[side, segment, :, head_lanes(1, head, heads)]
            all_keys = jnp.concatenate([qkv_ref[0, :keys, lanes_k], memory_key], axis=0)
            all_values = jnp.concatenate([qkv_ref[0, :keys, lanes_v], memory_value], axis=0)
            score = dot(all_keys, query, NT)
            parts = [score[:keys - QT]] if tile else []
            parts.append(jnp.where(causal((QT, QT)), score[keys - QT : keys], MASKED))
            parts.append(score[keys:] + memory_bias)
            top = parts[0].max(axis=0, keepdims=True)
            for part in parts[1:]:
                top = jnp.maximum(top, part.max(axis=0, keepdims=True))
            weights = [jnp.exp(part - top) for part in parts]
            total = sum(weight.sum(axis=0, keepdims=True) for weight in weights)
            weights = jnp.concatenate([weight.astype(BF16) for weight in weights], axis=0)
            result = dot(all_values, weights, TN)
            stacked.append(result / total)
            lse_ref[0, 0, head : head + 1, rows] = top + jnp.log(total)
        out_ref[0, rows, :] = jnp.concatenate(stacked, axis=0).T.astype(BF16)
    attended = out_ref[0]
    low = slabs[0].shape[-1] - width
    own, by_x, by_y, by_both = (slab_columns(slab, low, low + width) for slab in slabs)

    @pl.when(side == 0)
    def _():
        total_ref[...] = jnp.concatenate(
            [dot(attended, own, NT), dot(attended, by_x, NT)], axis=1
        )

    @pl.when(side == 1)
    def _():
        part = total_ref[...] + jnp.concatenate(
            [dot(attended, by_y, NT), dot(attended, by_both, NT)],
            axis=1,
        )
        part_ref[...] = part.astype(BF16)


def attention_forward(layer, place, memory_bias, qkv, starts, got, fit, near, slabs, after=()):
    rows = qkv.shape[1]
    width = qkv.shape[2] // 3
    heads = width // HEAD_DIM
    segs = rows // SEG
    slab_arrays, slab_specs = slab_operands(slabs, 2)
    features = 2 * slab_arrays[0].shape[-2]
    return pl.pallas_call(
        attention_forward_kernel,
        grid_spec=pltpu.PrefetchScalarGridSpec(
            num_scalar_prefetch=1,
            grid=(segs, 2),
            in_specs=[
                pl.BlockSpec(memory_space=pltpu.SMEM),
                pl.BlockSpec((1, SEG, 3 * width), lambda g, s, p: (s, g, 0)),
                pl.BlockSpec((1, 1, BASIS, 2 * width), lambda g, s, p: (layer, s, 0, 0)),
                pl.BlockSpec((1, BASIS, 2 * width), lambda g, s, p: (1 - s, 0, 0)),
                pl.BlockSpec((1, BASIS, 2 * width), lambda g, s, p: (s, 0, 0)),
                pl.BlockSpec(near.shape, lambda g, s, p: (0, 0)),
                *slab_specs,
                *(pl.BlockSpec(memory_space=pl.ANY) for _ in after),
            ],
            out_specs=[
                pl.BlockSpec((1, SEG, width), lambda g, s, p: (s, g, 0)),
                pl.BlockSpec((1, 1, heads, SEG), lambda g, s, p: (g, s, 0, 0)),
                pl.BlockSpec((1, 1, BASIS, 2 * width), lambda g, s, p: (g, s, 0, 0)),
                pl.BlockSpec((SEG, features), lambda g, s, p: (g, 0)),
            ],
            scratch_shapes=[
                pltpu.VMEM((2, segs, BASIS, 2 * width), BF16),
                pltpu.VMEM((SEG, features), F32),
            ],
        ),
        out_shape=[
            kept((2, rows, width), BF16),
            kept((segs, 2, heads, SEG), F32),
            kept((segs, 2, BASIS, 2 * width), BF16),
            array((rows, features), BF16),
        ],
        compiler_params=pltpu.CompilerParams(vmem_limit_bytes=VMEM_LIMIT),
        cost_estimate=cost(13),
    )(place, memory_bias, in_hbm(qkv), starts, got, fit, near, *slab_arrays, *after)


def attention_backward_kernel(
    bias_ref,
    qkv_ref,
    memory_ref,
    lse_ref,
    out_ref,
    grad_ref,
    near_ref,
    *refs,
):
    dq_ref, dkv_ref, last_ref, back_ref, first_ref = refs[-5:]
    segment = pl.program_id(1)
    memory_bias = bias_ref[segment]
    heads = out_ref.shape[2] // HEAD_DIM
    scale = HEAD_DIM ** (-0.5)
    tiles = SEG // QT
    product = (out_ref[0].astype(F32) * grad_ref[0].astype(F32)).T
    query_grads = []
    for head in range(heads):
        lanes = head_lanes(0, head, heads)
        lanes_k, lanes_v = head_lanes(1, head, heads), head_lanes(2, head, heads)
        query = qkv_ref[0, :, lanes] * scale
        grad = grad_ref[0, :, lanes]
        dots = product[lanes, :].sum(axis=0, keepdims=True)
        log_total = lse_ref[0, 0, head : head + 1, :]
        all_keys = []
        score_grads = []
        for part in range(tiles + 1):
            start = part * QT if part < tiles else 0
            if part < tiles:
                keys = slice(start, start + QT)
                key, value = qkv_ref[0, keys, lanes_k], qkv_ref[0, keys, lanes_v]
            else:
                key = memory_ref[0, 0, :, head_lanes(0, head, heads)]
                value = memory_ref[0, 0, :, head_lanes(1, head, heads)]
            score = dot(key, query[start:], NT)
            if part < tiles:
                score = jnp.where(causal(score.shape), score, MASKED)
            else:
                score = score + memory_bias
            weight = jnp.exp(score - log_total[:, start:])
            weight_grad = dot(value, grad[start:], NT)
            score_grad = (weight * (weight_grad - dots[:, start:])).astype(BF16)
            value_grad = dot(weight.astype(BF16), grad[start:], NN)
            key_grad = dot(score_grad, query[start:], NN)
            all_keys.append(key)
            score_grads.append(score_grad)
            if part < tiles:
                dkv_ref[0, keys, head_lanes(0, head, heads)] = key_grad
                dkv_ref[0, keys, head_lanes(1, head, heads)] = value_grad
            else:
                last_ref[0, :, head_lanes(0, head, heads)] = key_grad
                last_ref[0, :, head_lanes(1, head, heads)] = value_grad
        head_grads = []
        for tile in range(tiles):
            members = [part for part in range(tiles + 1) if part <= tile or part == tiles]
            columns = [tile * QT - (part * QT if part < tiles else 0) for part in members]
            head_grads.append(
                dot(
                    jnp.concatenate([all_keys[part] for part in members], axis=0),
                    jnp.concatenate(
                        [score_grads[p][:, low : low + QT] for p, low in zip(members, columns)],
                        axis=0,
                    ),
                    TN,
                )
            )
        query_grads.append(jnp.concatenate(head_grads, axis=1) * scale)
    dq_ref[0] = jnp.concatenate(query_grads, axis=0).T.astype(BF16)

    @pl.when(segment == 0)
    def _():
        first_ref[...] = last_ref[0]

    @pl.when(segment == 1)
    def _():
        back = first_ref[...] + dot(near_ref[:, :BASIS], last_ref[0].astype(BF16), TN)
        back_ref[0] = back.astype(BF16)


def attention_backward(memory_bias, qkv, memory, log_totals, attended, grad, near, after):
    rows, width = attended.shape[1:]
    heads = width // HEAD_DIM
    segs = rows // SEG
    narrow = pl.BlockSpec((1, SEG, width), lambda s, g: (s, g, 0))
    side_block = pl.BlockSpec((1, BASIS, 2 * width), lambda s, g: (s, 0, 0))
    return pl.pallas_call(
        attention_backward_kernel,
        grid=(2, segs),
        in_specs=[
            pl.BlockSpec(memory_space=pltpu.SMEM),
            pl.BlockSpec((1, SEG, 3 * width), lambda s, g: (s, g, 0)),
            pl.BlockSpec((1, 1, BASIS, 2 * width), lambda s, g: (g, s, 0, 0)),
            pl.BlockSpec((1, 1, heads, SEG), lambda s, g: (g, s, 0, 0)),
            narrow,
            narrow,
            pl.BlockSpec(near.shape, lambda s, g: (0, 0)),
            *(pl.BlockSpec(memory_space=pl.ANY) for _ in after),
        ],
        out_specs=[
            narrow,
            pl.BlockSpec((1, SEG, 2 * width), lambda s, g: (s, g, 0)),
            side_block,
            side_block,
        ],
        out_shape=[
            array((2, rows, width), BF16),
            array((2, rows, 2 * width), F32),
            array((2, BASIS, 2 * width), F32),
            array((2, BASIS, 2 * width), BF16),
        ],
        scratch_shapes=[pltpu.VMEM((BASIS, 2 * width), F32)],
        compiler_params=pltpu.CompilerParams(vmem_limit_bytes=VMEM_LIMIT),
        cost_estimate=cost(18),
    )(memory_bias, qkv, memory, log_totals, attended, grad, near, *after)


def memory_backward_kernel(
    place_ref,
    dq_ref,
    dkv_ref,
    last_ref,
    got_ref,
    near_ref,
    far_ref,
    *refs,
):
    width = dq_ref.shape[2]
    slabs_qk, slabs_vo, refs = split_attention(refs, width)
    grads_ref, part_ref, sums_ref, signal_ref = refs[-4:]
    segment = pl.program_id(0)

    def arrived(side):
        got = got_ref[1 - side]
        return jnp.where(place_ref[0] == 0, got.astype(F32), 0.0).astype(BF16)

    @pl.when(segment == 0)
    def _():
        for side in range(2):
            carry = last_ref[side] + dot(far_ref[:, :BASIS], arrived(side), TN)
            signal_ref[side] = dot(near_ref[:, BASIS:], carry.astype(BF16), TN)

    @pl.when(segment == 1)
    def _():
        for side in range(2):
            signal_ref[side] = dot(far_ref[:, BASIS:], arrived(side), TN)

    sides = []
    for side in range(2):
        grads_ref[side, :, :width] = dq_ref[side]
        grads_ref[side, :, width:] = (dkv_ref[side] + signal_ref[side]).astype(BF16)
        sides.append(grads_ref[side])
    slabs, low = slabs_qk
    part = unproject([side[:, : 2 * width] for side in sides], slabs, low, low + 2 * width)
    slabs, low = slabs_vo
    part = part + unproject([side[:, 2 * width :] for side in sides], slabs, low, low + width)
    part_ref[...] = part.astype(BF16)
    add_rows(sums_ref, [(side, sides[side].astype(F32)) for side in range(2)])


def memory_backward(place, dq, dkv, last, got, near, far, slabs, after):
    rows, width = dq.shape[1:]
    slab_arrays, slab_specs = slab_operands(slabs, 1)
    features = 2 * slab_arrays[0].shape[-2]
    whole = lambda a: pl.BlockSpec(a.shape, lambda g, p: (0,) * a.ndim)
    return pl.pallas_call(
        memory_backward_kernel,
        grid_spec=pltpu.PrefetchScalarGridSpec(
            num_scalar_prefetch=1,
            grid=(rows // SEG,),
            in_specs=[
                pl.BlockSpec((2, SEG, width), lambda g, p: (0, g, 0)),
                pl.BlockSpec((2, SEG, 2 * width), lambda g, p: (0, g, 0)),
                *(whole(a) for a in (last, got, near, far)),
                *slab_specs,
                *(pl.BlockSpec(memory_space=pl.ANY) for _ in after),
            ],
            out_specs=[
                pl.BlockSpec((2, SEG, 3 * width), lambda g, p: (0, g, 0)),
                pl.BlockSpec((SEG, features), lambda g, p: (g, 0)),
                pl.BlockSpec((8, 3 * width), lambda g, p: (0, 0)),
            ],
            scratch_shapes=[pltpu.VMEM((2, SEG, 2 * width), F32)],
        ),
        out_shape=[
            array((2, rows, 3 * width), BF16),
            array((rows, features), BF16),
            array((8, 3 * width), F32),
        ],
        compiler_params=pltpu.CompilerParams(vmem_limit_bytes=VMEM_LIMIT),
        cost_estimate=cost(5),
    )(place, dq, dkv, last, got, near, far, *slab_arrays, *after)


def weight_grads_kernel(plan, *refs):
    outs = refs[len(refs) - len(plan) :]
    for out_ref, slabs in zip(outs, plan):
        half = out_ref.shape[1]
        for index, products in enumerate(slabs):
            start = 0
            for left, turn, right, side, low, high in products:
                columns = slice(turn * half, (turn + 1) * half)
                result = dot(refs[left][:, columns], refs[right][side, :, low:high], TN)
                out_ref[index, :, start : start + high - low] = result.astype(BF16)
                start += high - low


def weight_grads(operands, plan, half, after=()):
    shapes = [
        array((2, half, sum(high - low for *_, low, high in slabs[0])), BF16) for slabs in plan
    ]
    vmem = pl.BlockSpec(memory_space=pltpu.VMEM)
    return pl.pallas_call(
        partial(weight_grads_kernel, plan),
        in_specs=[vmem] * len(operands) + [pl.BlockSpec(memory_space=pl.ANY)] * len(after),
        out_specs=[vmem] * len(plan),
        out_shape=shapes,
        compiler_params=pltpu.CompilerParams(vmem_limit_bytes=VMEM_LIMIT),
        cost_estimate=cost(6),
    )(*operands, *after)


GIVE_X = ((1, 0), (1, 1))
GIVE_Y = ((0, 1), (1, 1))
KEEP_X = ((0, 0), (0, 1))
KEEP_Y = ((0, 0), (1, 0))


def flip(array, axis):
    return lax.ppermute(array, axis, SWAP)


ALL_BUT_CORE = ("cy", "tx", "tz")


def gather_blocks(shard):
    whole = lax.all_gather(shard, ALL_BUT_CORE, axis=0, tiled=True)
    return whole.reshape(2, 2, -1, shard.shape[1])


def gather_z(shard):
    size = lax.axis_size("tz")
    spread = jnp.broadcast_to(shard[None], (size,) + shard.shape)
    return lax.all_to_all(spread, "tz", 0, 0, tiled=True).reshape(-1, shard.shape[1])


def join_kernel(here_ref, *refs):
    *pieces, first_ref, second_ref, zero_ref = refs
    rows = pieces[0].shape[0]
    columns = first_ref.shape[1]
    for bit, piece_ref in enumerate(pieces):
        place = pl.ds(pl.multiple_of((here_ref[0] ^ bit) * rows, rows), rows)
        first_ref[place, :] = piece_ref[:, :columns]
        second_ref[place, :] = piece_ref[:, columns:]
    zero_ref[...] = jnp.zeros_like(zero_ref)


def gather_split(shard, widths):
    size = lax.axis_size("tz")
    here = lax.axis_index("tz")
    pieces = [shift(shard, "tz", bit) if bit else shard for bit in range(size)]
    if shard.shape[0] % 16:
        rows = jnp.zeros((size,) + shard.shape, shard.dtype)
        for bit, piece in enumerate(pieces):
            rows = lax.dynamic_update_index_in_dim(rows, piece, here ^ bit, 0)
        return split_columns(rows.reshape(-1, shard.shape[1]), widths, ())
    vmem = pl.BlockSpec(memory_space=pltpu.VMEM)
    first, second, zero = pl.pallas_call(
        join_kernel,
        in_specs=[pl.BlockSpec(memory_space=pltpu.SMEM)] + [vmem] * size,
        out_specs=[vmem] * 3,
        out_shape=[array((size * shard.shape[0], columns), BF16) for columns in widths]
        + [array((8, 128), jnp.int32)],
        compiler_params=pltpu.CompilerParams(vmem_limit_bytes=VMEM_LIMIT),
        cost_estimate=cost(1),
    )(here.reshape(1).astype(jnp.int32), *pieces)
    return (first, second), zero[0, 0]


def shift(array, axis, bit):
    return lax.ppermute(array, axis, [(i, i ^ bit) for i in range(lax.axis_size(axis))])


def gather_second(two, axis):
    own, near = two
    far, both = flip(own, axis), flip(near, axis)
    return (own, far, near, both) if axis == "tx" else (own, near, far, both)


def pieces_of(parts, block_rows):
    total = jnp.concatenate(
        [sum(piece.astype(F32) for piece in three).astype(BF16) for three in parts], axis=1
    )
    return total.reshape(-1, block_rows, total.shape[-1])


def spread_pieces(pieces):
    return lax.all_to_all(pieces, "tz", 0, 0, tiled=True)


def butterfly(array, axes):
    for axis in axes:
        bit = 1
        while bit < lax.axis_size(axis):
            array = array + shift(array, axis, bit)
            bit *= 2
    return array


def adamw(weight, first, second, grad, rate, decay):
    first_new = FIRST_DECAY * first + (1.0 - FIRST_DECAY) * grad
    second_new = SECOND_DECAY * second + (1.0 - SECOND_DECAY) * grad * grad
    first_hat = first_new / (1.0 - FIRST_DECAY**STEP)
    second_hat = second_new / (1.0 - SECOND_DECAY**STEP)
    weight_new = weight * (1.0 - rate * decay) - rate * first_hat / (
        jnp.sqrt(second_hat) + ADAM_EPS
    )
    return (weight_new, first_new, second_new)


def shards(
    h_in,
    cotangent,
    carried,
    centres,
    sticky,
    flags,
    w_qkv,
    w_qkv_first,
    w_qkv_second,
    w_out_t,
    w_out_first,
    w_out_second,
    w_up,
    w_up_first,
    w_up_second,
    w_down_t,
    w_down_first,
    w_down_second,
    vec_d,
    vec_d_first,
    vec_d_second,
    vec_c,
    vec_c_first,
    vec_c_second,
):
    depth = lax.axis_size("tz")
    tok_count = depth * 2
    ch_count = 2 * lax.axis_size("cc")
    context = lax.axis_index("cy")
    core = lax.axis_index("cc")
    x_place = lax.axis_index("tx")
    block_rows = w_qkv.shape[2]
    width = w_qkv.shape[1 + 2] * 1
    features = h_in.shape[1]
    half = features // 2
    rows = h_in.shape[0] // 2
    hidden_own = w_up.shape[2]

    table_index = jnp.where(context == 0, core, 2)
    sticky_row = lax.dynamic_index_in_dim(sticky[0], table_index, 0, keepdims=False)
    old_basis, design = table_inputs(centres, sticky_row)

    def attention_members(layer):
        return [(w_qkv, layer), (w_out_t, layer)]

    def ffn_members(layer):
        return [(w_up, layer), (w_down_t, layer)]

    attn_shard = cast(attention_members(0))
    (qk_own, vo_own), zero = gather_split(attn_shard, (2 * width, 2 * width))
    qk_two, vo_two = (qk_own, flip(qk_own, "tx")), (vo_own, flip(vo_own, "cy"))
    ffn_rows = gather_z(cast(ffn_members(0), (attn_shard,)))
    (up_own, down_own), _ = split_columns(ffn_rows, (hidden_own, hidden_own), (qk_own,))
    up_two, down_two = (up_own, flip(up_own, "tx")), (down_own, flip(down_own, "cy"))
    above = cast(attention_members(1), (qk_own,))
    attn_slabs = [
        gather_second(qk_two, "cy") + gather_second(vo_two, "tx"),
        Gathered(gather_blocks(above), 4 * width, 0),
    ]
    ffn_slabs = [
        gather_second(up_two, "cy") + gather_second(down_two, "tx"),
        Gathered(gather_blocks(cast(ffn_members(1), (up_own,))), 2 * hidden_own, 0),
    ]
    table_own = make_tables(old_basis, design, (qk_own,))
    table_other = flip(table_own, "cc")
    table_near = jnp.where(core == 0, table_own, table_other)
    table_far = jnp.where(core == 0, table_other, table_own)

    x_place = x_place + zero
    late_context = context + zero
    spot = jnp.arange(features)
    turned = spot // half
    block_z = (spot % half) // block_rows
    source = block_z * (2 * block_rows) + jnp.where(
        turned == 0, x_place, 1 - x_place
    ) * block_rows + spot % block_rows
    order = (jnp.arange(features)[:, None] == source[None, :]).astype(BF16)
    order_wide = order.astype(F32)
    order_back = (source[:, None] == jnp.arange(features)[None, :]).astype(BF16)
    place = jnp.stack([context, x_place]).astype(jnp.int32)

    vec_c_other = flip(vec_c, "cy")
    gains = jnp.dot(
        vec_d.reshape(-1, features), order_wide, precision=PRECISE
    ).reshape(vec_d.shape)
    both_c = jnp.stack([vec_c, vec_c_other], axis=1)
    in_bias = jnp.concatenate(
        [both_c[:, :, 0], jnp.zeros_like(both_c[:, :, 0]), both_c[:, :, 1]], axis=-1
    )
    up_bias = both_c[:, :, 2:6].transpose(0, 1, 3, 2).reshape(LAYERS, 2, hidden_own)
    flag_on = flags[0] + zero > 0
    carried_own = carried[:, 0].reshape(LAYERS, BASIS, 2 * width)
    starts = jnp.stack([carried_own, flip(carried_own, "cy")], axis=1)
    starts = jnp.where(flag_on, starts, jnp.zeros_like(starts))
    memory_bias = jnp.stack(
        [jnp.where((context == 0) & ~flag_on, MASKED, 0.0), jnp.float32(0.0)]
    ).astype(F32)
    own_h = lax.dynamic_slice_in_dim(h_in, late_context * rows, rows, axis=0)
    own_cot = lax.dynamic_slice_in_dim(cotangent, late_context * rows, rows, axis=0)

    row_f32 = array((rows, features), F32)
    kept_f32 = kept((rows, features), F32)
    kept_b16 = kept((rows, features), BF16)
    kept_hidden = kept((2, rows, hidden_own), BF16)
    row_b16 = array((rows, features), BF16)
    side_hidden = array((2, rows, hidden_own), BF16)
    side_width = array((2, rows, width), BF16)
    sums_shape = array((8, features), F32)

    saved = []
    for layer in range(LAYERS):
        stream, normed, qkv, fit, ahead = rows_call(
            partial(enter_kernel, layer),
            place,
            (in_hbm(own_h),) if layer == 0 else (in_hbm(middle), part, got),
            ((order,) if layer == 0 else ()) + (gains, in_bias),
            attn_slabs[layer],
            (table_near, table_far, starts),
            (kept_f32, kept_b16, kept((2, rows, 3 * width), BF16)),
            (array((2, BASIS, 2 * width), F32), array((2, BASIS, 2 * width), BF16)),
            7,
            [pltpu.VMEM((2, rows, 2 * width), BF16)],
            after=(up_two[1], down_two[1]) if layer == 0 else (),
        )
        received = flip(ahead, "cy")
        out_slabs = attn_slabs[layer][4:] if layer == 0 else attn_slabs[layer]
        attended, log_totals, memory, part = attention_forward(
            layer, place, memory_bias, qkv, starts, received, fit, table_near, out_slabs,
            after=ffn_slabs[0][1:4] + ffn_slabs[0][5:8] if layer == 0 else (),
        )
        got = flip(part, "cc")
        middle, normed_two, active, slope, part = rows_call(
            partial(ffn_forward_kernel, layer),
            place,
            (in_hbm(stream), part, got),
            (gains, up_bias),
            ffn_slabs[layer],
            (),
            (kept_f32, kept_b16, kept_hidden, kept_hidden, row_b16),
            (),
            11,
        )
        got = flip(part, "cc")
        saved.append(
            tuple(in_hbm(member) for member in (
                stream,
                normed,
                qkv,
                memory,
                log_totals,
                attended,
                middle,
                normed_two,
                active,
                slope,
            ))
        )
    final = middle + (part.astype(F32) + got.astype(F32) + gains[LAYERS - 1, 5])
    final = lax.optimization_barrier(final.astype(BF16))
    outputs = final, flip(final, "cy")

    sums_ffn = [None] * (LAYERS + 1)
    sums_mix = [None] * LAYERS
    sums_in = [None] * LAYERS
    reduced = [None] * LAYERS

    def second_hop(keep_x, got_x, keep_y, got_y, after):
        pass_x, pass_y = pass_on(keep_x, got_x, keep_y, got_y, after)
        all_x = (keep_x[0], got_x[0], flip(pass_x, "cy"))
        all_y = (keep_y[0], got_y[0], flip(pass_y, "tx"))
        return pass_x, pieces_of((all_x, all_y), block_rows)

    zero_first = ()
    zero_mix = ()
    zero_attention = ()
    zero_memory = ()
    above_attention = None
    for layer in reversed(range(LAYERS)):
        (
            stream,
            normed,
            qkv,
            memory,
            log_totals,
            attended,
            middle,
            normed_two,
            active,
            slope,
        ) = saved[layer]
        top = layer == LAYERS - 1
        stream_grad, down, hidden_grad, part, sums_ffn[layer] = rows_call(
            partial(ffn_backward_kernel, layer),
            place,
            (in_hbm(own_cot), slope) if top else (stream_grad, stream_above, part, got, slope),
            (order if top else gains,),
            ffn_slabs[layer],
            (),
            (row_f32, row_b16, side_hidden, row_b16),
            (sums_shape,),
            9,
            after=zero_first,
        )
        got = flip(part, "cc")
        if above_attention is not None:
            qk_give, qk_keep, qk_got, vo_keep, vo_got = above_attention
            passed, attn_pieces = second_hop(qk_keep, qk_got, vo_keep, vo_got, (hidden_grad, slope))
            zero_mix, zero_attention = (passed,), (attn_pieces,)
            reduced[layer + 1] = (spread_pieces(attn_pieces), spread_ffn)
            zero_memory = (spread_ffn,)
        ffn_operands = (normed_two, down, hidden_grad, active)
        ffn_plans = [
            [
                [[(0, x, 2, y, 0, hidden_own)] for x, y in pair_x],
                [[(1, x, 3, y, 0, hidden_own)] for x, y in pair_y],
            ]
            for pair_x, pair_y in ((GIVE_X, GIVE_Y), (KEEP_X, KEEP_Y))
        ]
        up_give, down_give = weight_grads(ffn_operands, ffn_plans[0], half)
        up_got, down_got = flip(up_give, "tx"), flip(down_give, "cy")
        stream_grad, branch_grad, attended_grad, sums_mix[layer] = rows_call(
            partial(mix_backward_kernel, layer),
            place,
            (stream_grad, middle, part, got),
            (gains,),
            attn_slabs[layer],
            (),
            (row_f32, row_b16, side_width),
            (sums_shape,),
            6,
            after=(up_give, *zero_mix),
        )
        dq, dkv, last, back = attention_backward(
            memory_bias, qkv, memory, log_totals, attended, attended_grad, table_near, zero_attention
        )
        received = flip(back, "cy")
        up_keep, down_keep = weight_grads(ffn_operands, ffn_plans[1], half, (dq,))
        passed, ffn_pieces = second_hop(up_keep, up_got, down_keep, down_got, (dq,))
        grads_in, part, sums_in[layer] = memory_backward(
            place, dq, dkv, last, received, table_near, table_far, attn_slabs[layer],
            (passed, *zero_memory),
        )
        got = flip(part, "cc")
        spread_ffn = spread_pieces(ffn_pieces)
        attn_plans = [
            [
                [[(0, x, 2, y, 0, 2 * width)] for x, y in pair_x],
                [
                    [(0, x, 2, y, 2 * width, 3 * width), (1, x, 3, y, 0, width)]
                    for x, y in pair_y
                ],
            ]
            for pair_x, pair_y in ((GIVE_X, GIVE_Y), (KEEP_X, KEEP_Y))
        ]
        attn_operands = (normed, branch_grad, grads_in, attended)
        qk_give, vo_give = weight_grads(attn_operands, attn_plans[0], half)
        qk_got, vo_got = flip(qk_give, "tx"), flip(vo_give, "cy")
        if layer > 0:
            qk_keep, vo_keep = weight_grads(attn_operands, attn_plans[1], half)
            above_attention = qk_give, qk_keep, qk_got, vo_keep, vo_got
            zero_first = (qk_give, ffn_pieces)
        stream_above = stream
    final, sums_ffn[LAYERS] = rows_call(
        leave_kernel,
        place,
        (stream_grad, stream, part, got),
        (gains,),
        None,
        (),
        (row_b16,),
        (sums_shape,),
        5,
        after=(qk_give, ffn_pieces),
    )
    qk_keep, vo_keep = weight_grads(attn_operands, attn_plans[1], half, (final,))
    passed, attn_pieces = second_hop(qk_keep, qk_got, vo_keep, vo_got, (final,))
    reduced[0] = (spread_pieces(attn_pieces), spread_ffn)
    reduced = [[piece.astype(F32).sum(axis=0) for piece in pair] for pair in reduced]
    activations, zero_act = restore(*outputs, order_back, place, (passed,))
    final_got = flip(final, "cy")
    input_grad, _ = restore(final, final_got, order_back, place)

    vector_d = []
    vector_own = []
    vector_other = []
    for layer in range(LAYERS):
        below = sums_ffn[layer - 1] if layer > 0 else sums_ffn[LAYERS]
        vector_d.append(
            jnp.concatenate(
                [below[:2], sums_mix[layer][:3], sums_ffn[layer][2:3]], axis=0
            )
        )
        ups = sums_ffn[layer][3:5].reshape(2, width, 4).transpose(0, 2, 1)
        for side, out in enumerate((vector_own, vector_other)):
            sums = sums_in[layer][side]
            out.append(
                jnp.concatenate(
                    [sums[None, :width], sums[None, 2 * width :], ups[side]], axis=0
                )
            )
    qkv_grads = [
        jnp.stack([r[0][:, i * width : (i + 1) * width] for i in range(3)]) for r in reduced
    ]
    matrix_grads = (
        jnp.stack(qkv_grads),
        jnp.stack([r[0][:, 3 * width :] for r in reduced]),
        jnp.stack([r[1][:, :hidden_own] for r in reduced]),
        jnp.stack([r[1][:, hidden_own:] for r in reduced]),
    )
    vec_d_grad = jnp.dot(
        jnp.stack(vector_d).reshape(-1, features), order_wide.T, precision=PRECISE
    ).reshape(-1)
    own_c = jnp.stack(vector_own).reshape(-1)
    other_c = jnp.stack(vector_other).reshape(-1)
    arrived = flip(jnp.concatenate([vec_d_grad, other_c]), "cy")
    vector = butterfly(jnp.concatenate([vec_d_grad, own_c]) + arrived, ("tx", "tz"))
    vec_d_grad = vector[: vec_d.size].reshape(vec_d.shape)
    vec_c_grad = vector[vec_d.size :].reshape(vec_c.shape)

    square = sum(jnp.sum(grad * grad) for grad in matrix_grads)
    square = (
        square
        + zero_act[0, 0]
        + zero_after(final_got)
        + jnp.sum(vec_d_grad * vec_d_grad) / (tok_count * ch_count)
        + jnp.sum(vec_c_grad * vec_c_grad) / tok_count
    )
    everywhere = ("tz", "tx", "cy", "cc")
    squares = lax.all_to_all(
        jnp.full((tok_count * ch_count, 128), square), everywhere, 0, 0, tiled=True
    )
    total_square = jnp.sum(squares[:, 0])
    grad_norm = jnp.sqrt(total_square)
    factor = CLIP_LIMIT / jnp.maximum(grad_norm, CLIP_LIMIT)
    attention_update = adamw(
        w_qkv, w_qkv_first, w_qkv_second, matrix_grads[0] * factor, RATE_QKV, WEIGHT_DECAY
    )
    output_update = adamw(
        w_out_t, w_out_first, w_out_second, matrix_grads[1] * factor, RATE_OUT, WEIGHT_DECAY
    )
    expand_update = adamw(
        w_up, w_up_first, w_up_second, matrix_grads[2] * factor, RATE_UP, WEIGHT_DECAY
    )
    reduce_update = adamw(
        w_down_t, w_down_first, w_down_second, matrix_grads[3] * factor, RATE_DOWN, WEIGHT_DECAY
    )
    width_update = adamw(vec_d, vec_d_first, vec_d_second, vec_d_grad * factor, RATE_VECTOR, 0.0)
    channel_update = adamw(vec_c, vec_c_first, vec_c_second, vec_c_grad * factor, RATE_VECTOR, 0.0)
    return (
        activations,
        input_grad,
        grad_norm,
        *attention_update,
        *output_update,
        *expand_update,
        *reduce_update,
        *width_update,
        *channel_update,
    )


def solution(mesh):
    tok, ch = mesh.shape["tok"], mesh.shape["ch"]
    fine = Mesh(mesh.devices.reshape(tok // 2, 2, 2, ch // 2), ("tz", "tx", "cy", "cc"))
    t, c = ("tz", "tx"), ("cy", "cc")
    cube = P(None, None, t, c)
    matrix = P(None, t, c)
    channel = P(None, None, c)
    return jax.shard_map(
        shards,
        mesh=fine,
        in_specs=(
            P(t, None),
            P(t, None),
            P(None, t, None, None, c),
            P(),
            P(t, None, None),
            P(t),
            *(cube,) * 3,
            *(matrix,) * 9,
            *(P(),) * 3,
            *(channel,) * 3,
        ),
        out_specs=(
            P(t, None),
            P(t, None),
            P(),
            *(cube,) * 3,
            *(matrix,) * 9,
            *(P(),) * 3,
            *(channel,) * 3,
        ),
        check_vma=False,
    )
```

```python
from functools import partial
from typing import NamedTuple

import jax
import jax.numpy as jnp
from jax import lax
from jax.experimental import pallas as pl
from jax.experimental.pallas import tpu as pltpu
from jax.sharding import Mesh
from jax.sharding import PartitionSpec as P

HEAD_DIM = 64
BASIS = 256
SAMPLES = 256
SEG = 512
SEGS = 4
CRES = 1024
LAYERS = 2
STEP = 10

PRECISE = lax.Precision.HIGHEST
STICKY_RATIO = 0.5
RIDGE_WEIGHT = 0.5
BASIS_WIDTH = 0.01
NORM_EPS = 1e-05
CLIP_LIMIT = 1.0
FIRST_DECAY = 0.9
SECOND_DECAY = 0.95
ADAM_EPS = 1e-08
WEIGHT_DECAY = 0.1
RATE_QKV = 0.05
RATE_OUT = 0.5
RATE_UP = 0.05
RATE_DOWN = 0.03
RATE_VECTOR = 0.5
MASKED = -1e30
GELU_A = 0.7978845608028654
GELU_B = 0.044715
F32 = jnp.float32
BF16 = jnp.bfloat16
SWAP = ((0, 1), (1, 0))
NN = (((1,), (0,)), ((), ()))
NT = (((1,), (1,)), ((), ()))
TN = (((0,), (0,)), ((), ()))


def dot(left, right, dims, precision=None):
    return lax.dot_general(left, right, dims, precision=precision, preferred_element_type=F32)


VMEM_LIMIT = 32 * 2**20
TILE = 512
QT = 256


def cost(micros):
    return pl.CostEstimate(flops=int(micros * 1.1e9), bytes_accessed=10**6, transcendentals=0)


def table_kernel(old_ref, design_ref, out_ref, inv_ref, gram_ref):
    design = design_ref[...]
    eye = (
        lax.broadcasted_iota(jnp.int32, (BASIS, BASIS), 0)
        == lax.broadcasted_iota(jnp.int32, (BASIS, BASIS), 1)
    ).astype(F32)
    gram = dot(design, design, NT, PRECISE) + RIDGE_WEIGHT * eye
    gram_ref[...] = gram
    bound = jnp.max(jnp.sum(jnp.abs(gram), axis=0))
    inv_ref[...] = eye * (1.0 / bound)

    def step(low):
        scale = 2.0 / (1.0 + low)
        now = inv_ref[...]
        inner = dot(gram_ref[...], now, NN, PRECISE)
        inv_ref[...] = scale * (2.0 * now - scale * dot(now, inner, NN, PRECISE))
        return 4.0 * low / ((1.0 + low) * (1.0 + low))

    lax.while_loop(lambda low: low < 0.999, step, 0.99 * RIDGE_WEIGHT / bound)
    for _ in range(2):
        now = inv_ref[...]
        inner = dot(gram_ref[...], now, NN, PRECISE)
        inv_ref[...] = 2.0 * now - dot(now, inner, NN, PRECISE)
    fitted = dot(inv_ref[...], design, NN, PRECISE)
    out_ref[:, BASIS:] = fitted[:, SAMPLES:].astype(BF16)
    out_ref[:, :BASIS] = dot(fitted[:, :SAMPLES], old_ref[...], NT, PRECISE).astype(BF16)


def basis_table(centres, times):
    middle = (centres.astype(F32) + 0.5) / CRES
    offset = (times[None, :] - middle[:, None]) / BASIS_WIDTH
    return jnp.exp(-0.5 * offset * offset)


def table_inputs(centres, sticky_row):
    token_times = STICKY_RATIO + (1.0 - STICKY_RATIO) * (jnp.arange(SEG).astype(F32) + 0.5) / SEG
    places = (sticky_row.astype(F32) + 0.5) / CRES
    return (
        basis_table(centres, places),
        basis_table(centres, jnp.concatenate([STICKY_RATIO * places, token_times])),
    )


def make_tables(old_basis, design, after):
    def body(old_ref, design_ref, *refs):
        table_kernel(old_ref, design_ref, *refs[len(after) :])

    vmem = pl.BlockSpec(memory_space=pltpu.VMEM)
    return pl.pallas_call(
        body,
        in_specs=[vmem, vmem] + [pl.BlockSpec(memory_space=pl.ANY)] * len(after),
        out_specs=vmem,
        out_shape=jax.ShapeDtypeStruct((BASIS, BASIS + SEG), BF16),
        scratch_shapes=[pltpu.VMEM((BASIS, BASIS), F32), pltpu.VMEM((BASIS, BASIS), F32)],
        compiler_params=pltpu.CompilerParams(vmem_limit_bytes=VMEM_LIMIT),
        cost_estimate=cost(14),
    )(old_basis, design, *after)


def slab_columns(slab, low, high):
    return slab[:, low:high] if len(slab.shape) == 2 else slab[0, 0, :, low:high]


def project(left, slabs, low, high):
    own, by_x, by_y, by_both = (slab_columns(slab, low, high) for slab in slabs)
    return (
        dot(left, jnp.concatenate([own, by_x], axis=0), NN),
        dot(left, jnp.concatenate([by_y, by_both], axis=0), NN),
    )


def unproject(sides, slabs, low, high):
    own, by_x, by_y, by_both = (slab_columns(slab, low, high) for slab in slabs)
    if (high - low) % 128 == 0:
        both = jnp.concatenate(sides, axis=1)
        weights = jnp.concatenate(
            [jnp.concatenate([own, by_y], axis=1), jnp.concatenate([by_x, by_both], axis=1)], axis=0
        )
        return dot(both, weights, NT)
    return jnp.concatenate(
        [
            dot(sides[0], own, NT) + dot(sides[1], by_y, NT),
            dot(sides[0], by_x, NT) + dot(sides[1], by_both, NT),
        ],
        axis=1,
    )


def split_attention(refs, width):
    if len(refs[0].shape) == 2:
        return (refs[:4], 0), (refs[4:8], 0), refs[8:]
    return (refs[:4], 0), (refs[:4], 2 * width), refs[4:]


def split_ffn(refs):
    if len(refs[0].shape) == 2:
        return (refs[:4], 0), (refs[4:8], 0), refs[8:]
    return (refs[:4], 0), (refs[:4], refs[0].shape[-1] // 2), refs[4:]


TURNS = ((0, 0), (0, 1), (1, 0), (1, 1))


def cast_kernel(count, out_ref_index, *refs):
    out_ref = refs[out_ref_index]
    start = 0
    for ref in refs[:count]:
        for index in range(ref.shape[1]):
            columns = ref.shape[3]
            out_ref[:, start : start + columns] = ref[0, index].astype(BF16)
            start += columns


def cast(members, after=()):
    members = [
        (weight if weight.ndim == 4 else weight[:, None], layer) for weight, layer in members
    ]
    rows = members[0][0].shape[2]
    columns = sum(weight.shape[1] * weight.shape[3] for weight, _ in members)
    return pl.pallas_call(
        partial(cast_kernel, len(members), len(members) + len(after)),
        grid=(1,),
        in_specs=[
            pl.BlockSpec((1,) + weight.shape[1:], lambda i, layer=layer: (layer, 0, 0, 0))
            for weight, layer in members
        ]
        + [pl.BlockSpec(memory_space=pl.ANY)] * len(after),
        out_specs=pl.BlockSpec((rows, columns), lambda i: (0, 0)),
        out_shape=array((rows, columns), BF16),
        compiler_params=pltpu.CompilerParams(vmem_limit_bytes=VMEM_LIMIT),
        cost_estimate=cost(1),
    )(*(weight for weight, _ in members), *after)


def split_kernel(count, rows_ref, *refs):
    start = 0
    outs = refs[len(refs) - count - 1 :]
    for out_ref in outs[:count]:
        columns = out_ref.shape[1]
        out_ref[...] = rows_ref[:, start : start + columns]
        start += columns
    outs[count][...] = jnp.zeros_like(outs[count])


def split_columns(rows, widths, after):
    vmem = pl.BlockSpec(memory_space=pltpu.VMEM)
    *groups, zero = pl.pallas_call(
        partial(split_kernel, len(widths)),
        in_specs=[vmem] + [pl.BlockSpec(memory_space=pl.ANY)] * len(after),
        out_specs=[vmem] * (len(widths) + 1),
        out_shape=[array((rows.shape[0], columns), rows.dtype) for columns in widths]
        + [array((8, 128), jnp.int32)],
        compiler_params=pltpu.CompilerParams(vmem_limit_bytes=VMEM_LIMIT),
        cost_estimate=cost(1),
    )(rows, *after)
    return groups, zero[0, 0]


def pass_kernel(keep_a_ref, got_a_ref, keep_b_ref, got_b_ref, *refs):
    for keep_ref, got_ref, out_ref in (
        (keep_a_ref, got_a_ref, refs[-2]),
        (keep_b_ref, got_b_ref, refs[-1]),
    ):
        out_ref[...] = (keep_ref[0].astype(F32) + got_ref[0].astype(F32)).astype(BF16)


def pass_on(keep_a, got_a, keep_b, got_b, after):
    def slab(a):
        return pl.BlockSpec((1,) + a.shape[1:], lambda i: (1, 0, 0))

    def out(a):
        return pl.BlockSpec(a.shape[1:], lambda i: (0, 0))

    return pl.pallas_call(
        pass_kernel,
        grid=(1,),
        in_specs=[slab(a) for a in (keep_a, got_a, keep_b, got_b)]
        + [pl.BlockSpec(memory_space=pl.ANY)] * len(after),
        out_specs=[out(keep_a), out(keep_b)],
        out_shape=[array(keep_a.shape[1:], BF16), array(keep_b.shape[1:], BF16)],
        compiler_params=pltpu.CompilerParams(vmem_limit_bytes=VMEM_LIMIT),
        cost_estimate=cost(2),
    )(keep_a, got_a, keep_b, got_b, *after)


class Gathered(NamedTuple):
    whole: jax.Array
    columns: int
    index: int


def slab_operands(slabs, grid_rank):
    def fixed(shape):
        return pl.BlockSpec(shape, lambda *a: (0,) * len(shape))

    if not isinstance(slabs, Gathered):
        return [in_hbm(slab) for slab in slabs], [fixed(slab.shape) for slab in slabs]
    whole, columns, index = slabs
    specs = []
    for turn_y, turn_x in TURNS:
        specs.append(
            pl.BlockSpec(
                (1, 1, whole.shape[2], columns),
                lambda *a, turn_y=turn_y, turn_x=turn_x: (
                    a[grid_rank][0] ^ turn_y,
                    a[grid_rank][1] ^ turn_x,
                    0,
                    index,
                ),
            )
        )
    return [in_hbm(whole)] * 4, specs


def norm_stats(inputs):
    centred = inputs - jnp.mean(inputs, axis=-1, keepdims=True)
    variance = jnp.mean(centred * centred, axis=-1, keepdims=True)
    rstd = lax.rsqrt(variance + NORM_EPS)
    return centred * rstd, rstd


def norm_backward(inputs, grad, gain_row):
    unit, rstd = norm_stats(inputs)
    scaled = grad * gain_row
    back = rstd * (
        scaled
        - jnp.mean(scaled, axis=-1, keepdims=True)
        - unit * jnp.mean(scaled * unit, axis=-1, keepdims=True)
    )
    return back, grad * unit


def both_parts(own_ref, got_ref):
    return own_ref[...].astype(F32) + got_ref[...].astype(F32)


def add_rows(ref, rows):
    @pl.when(pl.program_id(0) == 0)
    def _():
        ref[...] = jnp.zeros_like(ref)

    for index, row in rows:
        ref[index : index + 1, :] += jnp.sum(row, axis=0, keepdims=True)


def rows_call(
    kernel, place, tiled, whole, slabs, more, tiled_outs, whole_outs, micros, scratch=(), after=()
):
    rows = tiled[0].shape[-2]

    def tile_spec(shape):
        if len(shape) == 2:
            return pl.BlockSpec((TILE, shape[1]), lambda i, p: (i, 0))
        return pl.BlockSpec((shape[0], TILE, shape[2]), lambda i, p: (0, i, 0))

    def whole_spec(shape):
        return pl.BlockSpec(shape, lambda i, p: (0,) * len(shape))

    slab_arrays, slab_specs = slab_operands(slabs, 1) if slabs is not None else ([], [])

    taken = len(tiled) + len(whole) + len(slab_arrays) + len(more)

    def body(place_ref, *refs):
        kernel(*refs[:taken], *refs[taken + len(after) :])

    return pl.pallas_call(
        body,
        grid_spec=pltpu.PrefetchScalarGridSpec(
            num_scalar_prefetch=1,
            grid=(rows // TILE,),
            in_specs=[tile_spec(a.shape) for a in tiled]
            + [whole_spec(a.shape) for a in whole]
            + slab_specs
            + [whole_spec(a.shape) for a in more]
            + [pl.BlockSpec(memory_space=pl.ANY)] * len(after),
            out_specs=[tile_spec(a.shape) for a in tiled_outs]
            + [whole_spec(a.shape) for a in whole_outs],
            scratch_shapes=list(scratch),
        ),
        out_shape=[*tiled_outs, *whole_outs],
        compiler_params=pltpu.CompilerParams(vmem_limit_bytes=VMEM_LIMIT),
        cost_estimate=cost(micros),
    )(place, *tiled, *whole, *slab_arrays, *more, *after)


def in_hbm(operand):
    return pltpu.with_memory_space_constraint(operand, pltpu.HBM)


def kept(shape, dtype):
    return pltpu.HBM(shape, dtype)


def array(shape, dtype):
    return jax.ShapeDtypeStruct(shape, dtype)


def enter_kernel(layer, *refs):
    if layer == 0:
        h_ref, order_ref, gains_ref, bias_ref, *refs = refs
        stream = dot(h_ref[...], order_ref[...], NN)
    else:
        middle_ref, own_ref, got_ref, gains_ref, bias_ref, *refs = refs
        stream = middle_ref[...] + (both_parts(own_ref, got_ref) + gains_ref[layer - 1, 5:6, :])
    width = refs[-4].shape[2] // 3
    slabs_qk, slabs_vo, refs = split_attention(refs, width)
    near_ref, far_ref, start_ref, *refs = refs
    stream_ref, normed_ref, qkv_ref, fit_ref, ahead_ref, signal_ref = refs
    step = pl.program_id(0)
    stream_ref[...] = stream
    unit, _ = norm_stats(stream)
    normed = (unit * gains_ref[layer, 0:1, :] + gains_ref[layer, 1:2, :]).astype(BF16)
    normed_ref[...] = normed
    rows = pl.ds(pl.multiple_of(step * TILE, TILE), TILE)
    low = slabs_qk[1]
    queries_keys = project(normed, slabs_qk[0], low, low + 2 * width)
    low = slabs_vo[1]
    values = project(normed, slabs_vo[0], low, low + width)
    for side in range(2):
        result = jnp.concatenate([queries_keys[side], values[side]], axis=1)
        result = (result + bias_ref[layer, side : side + 1, :]).astype(BF16)
        qkv_ref[side] = result
        signal_ref[side, rows, :] = result[:, width:]

    @pl.when(step == pl.num_programs(0) - 1)
    def _():
        for side in range(2):
            fit_near = dot(near_ref[:, BASIS:], signal_ref[side, :SEG, :], NN)
            fit_far = dot(far_ref[:, BASIS:], signal_ref[side, SEG:, :], NN)
            fit_ref[side] = fit_near
            ahead = dot(near_ref[:, :BASIS], start_ref[layer, side], NN) + fit_near
            ahead = dot(far_ref[:, :BASIS], ahead.astype(BF16), NN) + fit_far
            ahead_ref[side] = ahead.astype(BF16)


def ffn_forward_kernel(layer, stream_ref, own_ref, got_ref, gains_ref, bias_ref, *refs):
    (up, up_low), (down, down_low), refs = split_ffn(refs)
    middle_ref, normed_ref, active_ref, slope_ref, part_ref = refs
    hidden_own = active_ref.shape[2]
    middle = stream_ref[...] + (both_parts(own_ref, got_ref) + gains_ref[layer, 4:5, :])
    middle_ref[...] = middle
    unit, _ = norm_stats(middle)
    normed = (unit * gains_ref[layer, 2:3, :] + gains_ref[layer, 3:4, :]).astype(BF16)
    normed_ref[...] = normed
    sides = []
    for side, hidden in enumerate(project(normed, up, up_low, up_low + hidden_own)):
        hidden = hidden + bias_ref[layer, side : side + 1, :]
        square = hidden * hidden
        bend = jnp.tanh(hidden * (GELU_A + (GELU_A * GELU_B) * square))
        half_more = 0.5 + 0.5 * bend
        active = (hidden * half_more).astype(BF16)
        slope = half_more + (0.5 - 0.5 * bend * bend) * hidden * (
            GELU_A + (3.0 * GELU_A * GELU_B) * square
        )
        active_ref[side] = active
        slope_ref[side] = slope.astype(BF16)
        sides.append(active)
    part_ref[...] = unproject(sides, down, down_low, down_low + hidden_own).astype(BF16)


def ffn_backward_kernel(layer, *refs):
    if layer == LAYERS - 1:
        cot_ref, slope_ref, order_ref, *refs = refs
        (up_slabs, up_low), (down_slabs, down_low), refs = split_ffn(refs)
        stream_grad = dot(cot_ref[...], order_ref[...], NN)
        grad_ref, down_ref, hidden_ref, part_ref, sums_ref = refs
        sums = []
    else:
        before_ref, stream_ref, own_ref, got_ref, slope_ref, gains_ref, *refs = refs
        (up_slabs, up_low), (down_slabs, down_low), refs = split_ffn(refs)
        grad_ref, down_ref, hidden_ref, part_ref, sums_ref = refs
        normed_grad = both_parts(own_ref, got_ref)
        back, gain_rows = norm_backward(
            stream_ref[...], normed_grad, gains_ref[layer + 1, 0:1, :]
        )
        stream_grad = before_ref[...] + back
        sums = [(0, gain_rows), (1, normed_grad)]
    hidden_own = slope_ref.shape[2]
    grad_ref[...] = stream_grad
    down = stream_grad.astype(BF16)
    down_ref[...] = down
    sums.append((2, down.astype(F32)))
    sides = []
    for side, active_grad in enumerate(project(down, down_slabs, down_low, down_low + hidden_own)):
        hidden_grad = (active_grad * slope_ref[side].astype(F32)).astype(BF16)
        hidden_ref[side] = hidden_grad
        sums.append((3 + side, hidden_grad.astype(F32)))
        sides.append(hidden_grad)
    part_ref[...] = unproject(sides, up_slabs, up_low, up_low + hidden_own).astype(BF16)
    add_rows(sums_ref, sums)


def mix_backward_kernel(layer, before_ref, middle_ref, own_ref, got_ref, gains_ref, *refs):
    width = refs[-2].shape[2]
    slabs_qk, (slabs, low), refs = split_attention(refs, width)
    grad_ref, branch_ref, attended_ref, sums_ref = refs
    normed_grad = both_parts(own_ref, got_ref)
    back, gain_rows = norm_backward(middle_ref[...], normed_grad, gains_ref[layer, 2:3, :])
    stream_grad = before_ref[...] + back
    grad_ref[...] = stream_grad
    branch = stream_grad.astype(BF16)
    branch_ref[...] = branch
    for side, result in enumerate(project(branch, slabs, low + width, low + 2 * width)):
        attended_ref[side] = result.astype(BF16)
    add_rows(sums_ref, [(0, gain_rows), (1, normed_grad), (2, branch.astype(F32))])


def leave_kernel(before_ref, stream_ref, own_ref, got_ref, gains_ref, grad_ref, sums_ref):
    normed_grad = both_parts(own_ref, got_ref)
    back, gain_rows = norm_backward(stream_ref[...], normed_grad, gains_ref[0, 0:1, :])
    grad_ref[...] = (before_ref[...] + back).astype(BF16)
    add_rows(sums_ref, [(0, gain_rows), (1, normed_grad)])


def zero_kernel(_, zero_ref):
    zero_ref[...] = jnp.zeros_like(zero_ref)


def zero_after(operand):
    return pl.pallas_call(
        zero_kernel,
        in_specs=[pl.BlockSpec(memory_space=pl.ANY)],
        out_specs=pl.BlockSpec(memory_space=pltpu.VMEM),
        out_shape=array((8, 128), F32),
        cost_estimate=cost(1),
    )(operand)[0, 0]


def restore_kernel(context_ref, own_ref, got_ref, order_ref, *refs):
    out_ref, zero_ref = refs[-2:]
    zero_ref[...] = jnp.zeros_like(zero_ref)
    mine = (pl.program_id(0) // (pl.num_programs(0) // 2)) == context_ref[0]
    rows = jnp.where(mine, own_ref[...].astype(F32), got_ref[...].astype(F32)).astype(BF16)
    out_ref[...] = dot(rows, order_ref[...], NN)


def restore(own, got, order, context, after=()):
    rows, features = own.shape
    tiles = rows // TILE
    block = pl.BlockSpec((TILE, features), lambda i: (i % tiles, 0))
    return pl.pallas_call(
        restore_kernel,
        grid=(2 * tiles,),
        in_specs=[
            pl.BlockSpec(memory_space=pltpu.SMEM),
            block,
            block,
            pl.BlockSpec(order.shape, lambda i: (0, 0)),
            *(pl.BlockSpec(memory_space=pl.ANY) for _ in after),
        ],
        out_specs=[
            pl.BlockSpec((TILE, features), lambda i: (i, 0)),
            pl.BlockSpec((8, 128), lambda i: (0, 0)),
        ],
        out_shape=[kept((2 * rows, features), F32), array((8, 128), F32)],
        compiler_params=pltpu.CompilerParams(vmem_limit_bytes=VMEM_LIMIT),
        cost_estimate=cost(4),
    )(context, own, got, order, *after)


def causal(shape):
    return lax.broadcasted_iota(jnp.int32, shape, 0) <= lax.broadcasted_iota(jnp.int32, shape, 1)


def head_lanes(kind, head, heads):
    low = (kind * heads + head) * HEAD_DIM
    return slice(low, low + HEAD_DIM)


def attention_forward_kernel(
    place_ref,
    bias_ref,
    qkv_ref,
    start_ref,
    got_ref,
    fit_ref,
    near_ref,
    *refs,
):
    slabs = refs[:4]
    out_ref, lse_ref, memory_ref, part_ref, rows_ref, total_ref = refs[-6:]
    segment, side = pl.program_id(0), pl.program_id(1)
    heads = qkv_ref.shape[2] // (3 * HEAD_DIM)
    width = heads * HEAD_DIM

    @pl.when(segment == 0)
    def _():
        @pl.when(place_ref[0] == 0)
        def _():
            rows_ref[side, 0] = start_ref[0, 0]

        @pl.when(place_ref[0] != 0)
        def _():
            rows_ref[side, 0] = got_ref[0]

        second = dot(near_ref[:, :BASIS], rows_ref[side, 0], NN) + fit_ref[0]
        rows_ref[side, 1] = second.astype(BF16)

    memory_ref[0, 0] = rows_ref[side, segment]
    memory_bias = bias_ref[segment]
    for tile in range(SEG // QT):
        rows = slice(tile * QT, (tile + 1) * QT)
        stacked = []
        for head in range(heads):
            lanes_q, lanes_k, lanes_v = (head_lanes(kind, head, heads) for kind in range(3))
            query = qkv_ref[0, rows, lanes_q] * HEAD_DIM ** (-0.5)
            scores = []
            values = []
            for part in range(tile + 1):
                keys = slice(part * QT, (part + 1) * QT)
                score = dot(qkv_ref[0, keys, lanes_k], query, NT)
                if part == tile:
                    score = jnp.where(causal(score.shape), score, MASKED)
                scores.append(score)
                values.append(qkv_ref[0, keys, lanes_v])
            memory_key = rows_ref[side, segment, :, head_lanes(0, head, heads)]
            scores.append(dot(memory_key, query, NT) + memory_bias)
            values.append(rows_ref[side, segment, :, head_lanes(1, head, heads)])
            top = scores[0].max(axis=0, keepdims=True)
            for score in scores[1:]:
                top = jnp.maximum(top, score.max(axis=0, keepdims=True))
            total = jnp.zeros_like(top)
            result = jnp.zeros((HEAD_DIM, QT), F32)
            for score, value in zip(scores, values):
                weight = jnp.exp(score - top)
                total = total + weight.sum(axis=0, keepdims=True)
                result = result + dot(value, weight.astype(BF16), TN)
            stacked.append(result / total)
            lse_ref[0, 0, head : head + 1, rows] = top + jnp.log(total)
        out_ref[0, rows, :] = jnp.concatenate(stacked, axis=0).T.astype(BF16)
    attended = out_ref[0]
    low = slabs[0].shape[-1] - width
    own, by_x, by_y, by_both = (slab_columns(slab, low, low + width) for slab in slabs)

    @pl.when(side == 0)
    def _():
        total_ref[...] = jnp.concatenate(
            [dot(attended, own, NT), dot(attended, by_x, NT)], axis=1
        )

    @pl.when(side == 1)
    def _():
        part = total_ref[...] + jnp.concatenate(
            [dot(attended, by_y, NT), dot(attended, by_both, NT)],
            axis=1,
        )
        part_ref[...] = part.astype(BF16)


def attention_forward(layer, place, memory_bias, qkv, starts, got, fit, near, slabs, after=()):
    rows = qkv.shape[1]
    width = qkv.shape[2] // 3
    heads = width // HEAD_DIM
    segs = rows // SEG
    slab_arrays, slab_specs = slab_operands(slabs, 2)
    features = 2 * slab_arrays[0].shape[-2]
    return pl.pallas_call(
        attention_forward_kernel,
        grid_spec=pltpu.PrefetchScalarGridSpec(
            num_scalar_prefetch=1,
            grid=(segs, 2),
            in_specs=[
                pl.BlockSpec(memory_space=pltpu.SMEM),
                pl.BlockSpec((1, SEG, 3 * width), lambda g, s, p: (s, g, 0)),
                pl.BlockSpec((1, 1, BASIS, 2 * width), lambda g, s, p: (layer, s, 0, 0)),
                pl.BlockSpec((1, BASIS, 2 * width), lambda g, s, p: (1 - s, 0, 0)),
                pl.BlockSpec((1, BASIS, 2 * width), lambda g, s, p: (s, 0, 0)),
                pl.BlockSpec(near.shape, lambda g, s, p: (0, 0)),
                *slab_specs,
                *(pl.BlockSpec(memory_space=pl.ANY) for _ in after),
            ],
            out_specs=[
                pl.BlockSpec((1, SEG, width), lambda g, s, p: (s, g, 0)),
                pl.BlockSpec((1, 1, heads, SEG), lambda g, s, p: (g, s, 0, 0)),
                pl.BlockSpec((1, 1, BASIS, 2 * width), lambda g, s, p: (g, s, 0, 0)),
                pl.BlockSpec((SEG, features), lambda g, s, p: (g, 0)),
            ],
            scratch_shapes=[
                pltpu.VMEM((2, segs, BASIS, 2 * width), BF16),
                pltpu.VMEM((SEG, features), F32),
            ],
        ),
        out_shape=[
            kept((2, rows, width), BF16),
            kept((segs, 2, heads, SEG), F32),
            kept((segs, 2, BASIS, 2 * width), BF16),
            array((rows, features), BF16),
        ],
        compiler_params=pltpu.CompilerParams(vmem_limit_bytes=VMEM_LIMIT),
        cost_estimate=cost(13),
    )(place, memory_bias, in_hbm(qkv), starts, got, fit, near, *slab_arrays, *after)


def attention_backward_kernel(
    bias_ref,
    qkv_ref,
    memory_ref,
    lse_ref,
    out_ref,
    grad_ref,
    near_ref,
    *refs,
):
    dq_ref, dkv_ref, last_ref, back_ref, first_ref = refs[-5:]
    segment = pl.program_id(1)
    memory_bias = bias_ref[segment]
    heads = out_ref.shape[2] // HEAD_DIM
    scale = HEAD_DIM ** (-0.5)
    tiles = SEG // QT
    product = (out_ref[0].astype(F32) * grad_ref[0].astype(F32)).T
    query_grads = []
    for head in range(heads):
        lanes = head_lanes(0, head, heads)
        lanes_k, lanes_v = head_lanes(1, head, heads), head_lanes(2, head, heads)
        query = qkv_ref[0, :, lanes] * scale
        grad = grad_ref[0, :, lanes]
        dots = product[lanes, :].sum(axis=0, keepdims=True)
        log_total = lse_ref[0, 0, head : head + 1, :]
        all_keys = []
        score_grads = []
        for part in range(tiles + 1):
            start = part * QT if part < tiles else 0
            if part < tiles:
                keys = slice(start, start + QT)
                key, value = qkv_ref[0, keys, lanes_k], qkv_ref[0, keys, lanes_v]
            else:
                key = memory_ref[0, 0, :, head_lanes(0, head, heads)]
                value = memory_ref[0, 0, :, head_lanes(1, head, heads)]
            score = dot(key, query[start:], NT)
            if part < tiles:
                score = jnp.where(causal(score.shape), score, MASKED)
            else:
                score = score + memory_bias
            weight = jnp.exp(score - log_total[:, start:])
            weight_grad = dot(value, grad[start:], NT)
            score_grad = (weight * (weight_grad - dots[:, start:])).astype(BF16)
            value_grad = dot(weight.astype(BF16), grad[start:], NN)
            key_grad = dot(score_grad, query[start:], NN)
            all_keys.append(key)
            score_grads.append(score_grad)
            if part < tiles:
                dkv_ref[0, keys, head_lanes(0, head, heads)] = key_grad
                dkv_ref[0, keys, head_lanes(1, head, heads)] = value_grad
            else:
                last_ref[0, :, head_lanes(0, head, heads)] = key_grad
                last_ref[0, :, head_lanes(1, head, heads)] = value_grad
        head_grads = []
        for tile in range(tiles):
            members = [part for part in range(tiles + 1) if part <= tile or part == tiles]
            columns = [tile * QT - (part * QT if part < tiles else 0) for part in members]
            head_grads.append(
                dot(
                    jnp.concatenate([all_keys[part] for part in members], axis=0),
                    jnp.concatenate(
                        [score_grads[p][:, low : low + QT] for p, low in zip(members, columns)],
                        axis=0,
                    ),
                    TN,
                )
            )
        query_grads.append(jnp.concatenate(head_grads, axis=1) * scale)
    dq_ref[0] = jnp.concatenate(query_grads, axis=0).T.astype(BF16)

    @pl.when(segment == 0)
    def _():
        first_ref[...] = last_ref[0]

    @pl.when(segment == 1)
    def _():
        back = first_ref[...] + dot(near_ref[:, :BASIS], last_ref[0].astype(BF16), TN)
        back_ref[0] = back.astype(BF16)


def attention_backward(memory_bias, qkv, memory, log_totals, attended, grad, near, after):
    rows, width = attended.shape[1:]
    heads = width // HEAD_DIM
    segs = rows // SEG
    narrow = pl.BlockSpec((1, SEG, width), lambda s, g: (s, g, 0))
    side_block = pl.BlockSpec((1, BASIS, 2 * width), lambda s, g: (s, 0, 0))
    return pl.pallas_call(
        attention_backward_kernel,
        grid=(2, segs),
        in_specs=[
            pl.BlockSpec(memory_space=pltpu.SMEM),
            pl.BlockSpec((1, SEG, 3 * width), lambda s, g: (s, g, 0)),
            pl.BlockSpec((1, 1, BASIS, 2 * width), lambda s, g: (g, s, 0, 0)),
            pl.BlockSpec((1, 1, heads, SEG), lambda s, g: (g, s, 0, 0)),
            narrow,
            narrow,
            pl.BlockSpec(near.shape, lambda s, g: (0, 0)),
            *(pl.BlockSpec(memory_space=pl.ANY) for _ in after),
        ],
        out_specs=[
            narrow,
            pl.BlockSpec((1, SEG, 2 * width), lambda s, g: (s, g, 0)),
            side_block,
            side_block,
        ],
        out_shape=[
            array((2, rows, width), BF16),
            array((2, rows, 2 * width), F32),
            array((2, BASIS, 2 * width), F32),
            array((2, BASIS, 2 * width), BF16),
        ],
        scratch_shapes=[pltpu.VMEM((BASIS, 2 * width), F32)],
        compiler_params=pltpu.CompilerParams(vmem_limit_bytes=VMEM_LIMIT),
        cost_estimate=cost(18),
    )(memory_bias, qkv, memory, log_totals, attended, grad, near, *after)


def memory_backward_kernel(
    place_ref,
    dq_ref,
    dkv_ref,
    last_ref,
    got_ref,
    near_ref,
    far_ref,
    *refs,
):
    width = dq_ref.shape[2]
    slabs_qk, slabs_vo, refs = split_attention(refs, width)
    grads_ref, part_ref, sums_ref, signal_ref = refs[-4:]
    segment = pl.program_id(0)

    def arrived(side):
        got = got_ref[1 - side]
        return jnp.where(place_ref[0] == 0, got.astype(F32), 0.0).astype(BF16)

    @pl.when(segment == 0)
    def _():
        for side in range(2):
            carry = last_ref[side] + dot(far_ref[:, :BASIS], arrived(side), TN)
            signal_ref[side] = dot(near_ref[:, BASIS:], carry.astype(BF16), TN)

    @pl.when(segment == 1)
    def _():
        for side in range(2):
            signal_ref[side] = dot(far_ref[:, BASIS:], arrived(side), TN)

    sides = []
    for side in range(2):
        grads_ref[side, :, :width] = dq_ref[side]
        grads_ref[side, :, width:] = (dkv_ref[side] + signal_ref[side]).astype(BF16)
        sides.append(grads_ref[side])
    slabs, low = slabs_qk
    part = unproject([side[:, : 2 * width] for side in sides], slabs, low, low + 2 * width)
    slabs, low = slabs_vo
    part = part + unproject([side[:, 2 * width :] for side in sides], slabs, low, low + width)
    part_ref[...] = part.astype(BF16)
    add_rows(sums_ref, [(side, sides[side].astype(F32)) for side in range(2)])


def memory_backward(place, dq, dkv, last, got, near, far, slabs, after):
    rows, width = dq.shape[1:]
    slab_arrays, slab_specs = slab_operands(slabs, 1)
    features = 2 * slab_arrays[0].shape[-2]
    whole = lambda a: pl.BlockSpec(a.shape, lambda g, p: (0,) * a.ndim)
    return pl.pallas_call(
        memory_backward_kernel,
        grid_spec=pltpu.PrefetchScalarGridSpec(
            num_scalar_prefetch=1,
            grid=(rows // SEG,),
            in_specs=[
                pl.BlockSpec((2, SEG, width), lambda g, p: (0, g, 0)),
                pl.BlockSpec((2, SEG, 2 * width), lambda g, p: (0, g, 0)),
                *(whole(a) for a in (last, got, near, far)),
                *slab_specs,
                *(pl.BlockSpec(memory_space=pl.ANY) for _ in after),
            ],
            out_specs=[
                pl.BlockSpec((2, SEG, 3 * width), lambda g, p: (0, g, 0)),
                pl.BlockSpec((SEG, features), lambda g, p: (g, 0)),
                pl.BlockSpec((8, 3 * width), lambda g, p: (0, 0)),
            ],
            scratch_shapes=[pltpu.VMEM((2, SEG, 2 * width), F32)],
        ),
        out_shape=[
            array((2, rows, 3 * width), BF16),
            array((rows, features), BF16),
            array((8, 3 * width), F32),
        ],
        compiler_params=pltpu.CompilerParams(vmem_limit_bytes=VMEM_LIMIT),
        cost_estimate=cost(5),
    )(place, dq, dkv, last, got, near, far, *slab_arrays, *after)


def weight_grads_kernel(plan, *refs):
    outs = refs[len(refs) - len(plan) :]
    for out_ref, slabs in zip(outs, plan):
        half = out_ref.shape[1]
        for index, products in enumerate(slabs):
            start = 0
            for left, turn, right, side, low, high in products:
                columns = slice(turn * half, (turn + 1) * half)
                result = dot(refs[left][:, columns], refs[right][side, :, low:high], TN)
                out_ref[index, :, start : start + high - low] = result.astype(BF16)
                start += high - low


def weight_grads(operands, plan, half, after=()):
    shapes = [
        array((2, half, sum(high - low for *_, low, high in slabs[0])), BF16) for slabs in plan
    ]
    vmem = pl.BlockSpec(memory_space=pltpu.VMEM)
    return pl.pallas_call(
        partial(weight_grads_kernel, plan),
        in_specs=[vmem] * len(operands) + [pl.BlockSpec(memory_space=pl.ANY)] * len(after),
        out_specs=[vmem] * len(plan),
        out_shape=shapes,
        compiler_params=pltpu.CompilerParams(vmem_limit_bytes=VMEM_LIMIT),
        cost_estimate=cost(6),
    )(*operands, *after)


GIVE_X = ((1, 0), (1, 1))
GIVE_Y = ((0, 1), (1, 1))
KEEP_X = ((0, 0), (0, 1))
KEEP_Y = ((0, 0), (1, 0))


def flip(array, axis):
    return lax.ppermute(array, axis, SWAP)


ALL_BUT_CORE = ("cy", "tx", "tz")


def gather_blocks(shard):
    whole = lax.all_gather(shard, ALL_BUT_CORE, axis=0, tiled=True)
    return whole.reshape(2, 2, -1, shard.shape[1])


def gather_z(shard):
    size = lax.axis_size("tz")
    spread = jnp.broadcast_to(shard[None], (size,) + shard.shape)
    return lax.all_to_all(spread, "tz", 0, 0, tiled=True).reshape(-1, shard.shape[1])


def join_kernel(here_ref, *refs):
    *pieces, first_ref, second_ref, zero_ref = refs
    rows = pieces[0].shape[0]
    columns = first_ref.shape[1]
    for bit, piece_ref in enumerate(pieces):
        place = pl.ds(pl.multiple_of((here_ref[0] ^ bit) * rows, rows), rows)
        first_ref[place, :] = piece_ref[:, :columns]
        second_ref[place, :] = piece_ref[:, columns:]
    zero_ref[...] = jnp.zeros_like(zero_ref)


def gather_split(shard, widths):
    size = lax.axis_size("tz")
    here = lax.axis_index("tz")
    pieces = [shift(shard, "tz", bit) if bit else shard for bit in range(size)]
    if shard.shape[0] % 16:
        rows = jnp.zeros((size,) + shard.shape, shard.dtype)
        for bit, piece in enumerate(pieces):
            rows = lax.dynamic_update_index_in_dim(rows, piece, here ^ bit, 0)
        return split_columns(rows.reshape(-1, shard.shape[1]), widths, ())
    vmem = pl.BlockSpec(memory_space=pltpu.VMEM)
    first, second, zero = pl.pallas_call(
        join_kernel,
        in_specs=[pl.BlockSpec(memory_space=pltpu.SMEM)] + [vmem] * size,
        out_specs=[vmem] * 3,
        out_shape=[array((size * shard.shape[0], columns), BF16) for columns in widths]
        + [array((8, 128), jnp.int32)],
        compiler_params=pltpu.CompilerParams(vmem_limit_bytes=VMEM_LIMIT),
        cost_estimate=cost(1),
    )(here.reshape(1).astype(jnp.int32), *pieces)
    return (first, second), zero[0, 0]


def shift(array, axis, bit):
    return lax.ppermute(array, axis, [(i, i ^ bit) for i in range(lax.axis_size(axis))])


def gather_second(two, axis):
    own, near = two
    far, both = flip(own, axis), flip(near, axis)
    return (own, far, near, both) if axis == "tx" else (own, near, far, both)


def pieces_of(parts, block_rows):
    total = jnp.concatenate(
        [sum(piece.astype(F32) for piece in three).astype(BF16) for three in parts], axis=1
    )
    return total.reshape(-1, block_rows, total.shape[-1])


def spread_pieces(pieces):
    return lax.all_to_all(pieces, "tz", 0, 0, tiled=True)


def butterfly(array, axes):
    for axis in axes:
        bit = 1
        while bit < lax.axis_size(axis):
            array = array + shift(array, axis, bit)
            bit *= 2
    return array


def adamw(weight, first, second, grad, rate, decay):
    first_new = FIRST_DECAY * first + (1.0 - FIRST_DECAY) * grad
    second_new = SECOND_DECAY * second + (1.0 - SECOND_DECAY) * grad * grad
    first_hat = first_new / (1.0 - FIRST_DECAY**STEP)
    second_hat = second_new / (1.0 - SECOND_DECAY**STEP)
    weight_new = weight * (1.0 - rate * decay) - rate * first_hat / (
        jnp.sqrt(second_hat) + ADAM_EPS
    )
    return (weight_new, first_new, second_new)


def shards(
    h_in,
    cotangent,
    carried,
    centres,
    sticky,
    flags,
    w_qkv,
    w_qkv_first,
    w_qkv_second,
    w_out_t,
    w_out_first,
    w_out_second,
    w_up,
    w_up_first,
    w_up_second,
    w_down_t,
    w_down_first,
    w_down_second,
    vec_d,
    vec_d_first,
    vec_d_second,
    vec_c,
    vec_c_first,
    vec_c_second,
):
    depth = lax.axis_size("tz")
    tok_count = depth * 2
    ch_count = 2 * lax.axis_size("cc")
    context = lax.axis_index("cy")
    core = lax.axis_index("cc")
    x_place = lax.axis_index("tx")
    block_rows = w_qkv.shape[2]
    width = w_qkv.shape[1 + 2] * 1
    features = h_in.shape[1]
    half = features // 2
    rows = h_in.shape[0] // 2
    hidden_own = w_up.shape[2]

    table_index = jnp.where(context == 0, core, 2)
    sticky_row = lax.dynamic_index_in_dim(sticky[0], table_index, 0, keepdims=False)
    old_basis, design = table_inputs(centres, sticky_row)

    def attention_members(layer):
        return [(w_qkv, layer), (w_out_t, layer)]

    def ffn_members(layer):
        return [(w_up, layer), (w_down_t, layer)]

    attn_shard = cast(attention_members(0))
    (qk_own, vo_own), zero = gather_split(attn_shard, (2 * width, 2 * width))
    qk_two, vo_two = (qk_own, flip(qk_own, "tx")), (vo_own, flip(vo_own, "cy"))
    ffn_rows = gather_z(cast(ffn_members(0), (attn_shard,)))
    (up_own, down_own), _ = split_columns(ffn_rows, (hidden_own, hidden_own), (qk_own,))
    up_two, down_two = (up_own, flip(up_own, "tx")), (down_own, flip(down_own, "cy"))
    above = cast(attention_members(1), (qk_own,))
    attn_slabs = [
        gather_second(qk_two, "cy") + gather_second(vo_two, "tx"),
        Gathered(gather_blocks(above), 4 * width, 0),
    ]
    ffn_slabs = [
        gather_second(up_two, "cy") + gather_second(down_two, "tx"),
        Gathered(gather_blocks(cast(ffn_members(1), (up_own,))), 2 * hidden_own, 0),
    ]
    table_own = make_tables(old_basis, design, (qk_own,))
    table_other = flip(table_own, "cc")
    table_near = jnp.where(core == 0, table_own, table_other)
    table_far = jnp.where(core == 0, table_other, table_own)

    x_place = x_place + zero
    late_context = context + zero
    spot = jnp.arange(features)
    turned = spot // half
    block_z = (spot % half) // block_rows
    source = block_z * (2 * block_rows) + jnp.where(
        turned == 0, x_place, 1 - x_place
    ) * block_rows + spot % block_rows
    order = (jnp.arange(features)[:, None] == source[None, :]).astype(BF16)
    order_wide = order.astype(F32)
    order_back = (source[:, None] == jnp.arange(features)[None, :]).astype(BF16)
    place = jnp.stack([context, x_place]).astype(jnp.int32)

    vec_c_other = flip(vec_c, "cy")
    gains = jnp.dot(
        vec_d.reshape(-1, features), order_wide, precision=PRECISE
    ).reshape(vec_d.shape)
    both_c = jnp.stack([vec_c, vec_c_other], axis=1)
    in_bias = jnp.concatenate(
        [both_c[:, :, 0], jnp.zeros_like(both_c[:, :, 0]), both_c[:, :, 1]], axis=-1
    )
    up_bias = both_c[:, :, 2:6].transpose(0, 1, 3, 2).reshape(LAYERS, 2, hidden_own)
    flag_on = flags[0] + zero > 0
    carried_own = carried[:, 0].reshape(LAYERS, BASIS, 2 * width)
    starts = jnp.stack([carried_own, flip(carried_own, "cy")], axis=1)
    starts = jnp.where(flag_on, starts, jnp.zeros_like(starts))
    memory_bias = jnp.stack(
        [jnp.where((context == 0) & ~flag_on, MASKED, 0.0), jnp.float32(0.0)]
    ).astype(F32)
    own_h = lax.dynamic_slice_in_dim(h_in, late_context * rows, rows, axis=0)
    own_cot = lax.dynamic_slice_in_dim(cotangent, late_context * rows, rows, axis=0)

    row_f32 = array((rows, features), F32)
    kept_f32 = kept((rows, features), F32)
    kept_b16 = kept((rows, features), BF16)
    kept_hidden = kept((2, rows, hidden_own), BF16)
    row_b16 = array((rows, features), BF16)
    side_hidden = array((2, rows, hidden_own), BF16)
    side_width = array((2, rows, width), BF16)
    sums_shape = array((8, features), F32)

    saved = []
    for layer in range(LAYERS):
        stream, normed, qkv, fit, ahead = rows_call(
            partial(enter_kernel, layer),
            place,
            (in_hbm(own_h),) if layer == 0 else (in_hbm(middle), part, got),
            ((order,) if layer == 0 else ()) + (gains, in_bias),
            attn_slabs[layer],
            (table_near, table_far, starts),
            (kept_f32, kept_b16, kept((2, rows, 3 * width), BF16)),
            (array((2, BASIS, 2 * width), F32), array((2, BASIS, 2 * width), BF16)),
            7,
            [pltpu.VMEM((2, rows, 2 * width), BF16)],
            after=(up_two[1], down_two[1]) if layer == 0 else (),
        )
        received = flip(ahead, "cy")
        out_slabs = attn_slabs[layer][4:] if layer == 0 else attn_slabs[layer]
        attended, log_totals, memory, part = attention_forward(
            layer, place, memory_bias, qkv, starts, received, fit, table_near, out_slabs,
            after=ffn_slabs[0][1:4] + ffn_slabs[0][5:8] if layer == 0 else (),
        )
        got = flip(part, "cc")
        middle, normed_two, active, slope, part = rows_call(
            partial(ffn_forward_kernel, layer),
            place,
            (in_hbm(stream), part, got),
            (gains, up_bias),
            ffn_slabs[layer],
            (),
            (kept_f32, kept_b16, kept_hidden, kept_hidden, row_b16),
            (),
            11,
        )
        got = flip(part, "cc")
        saved.append(
            tuple(in_hbm(member) for member in (
                stream,
                normed,
                qkv,
                memory,
                log_totals,
                attended,
                middle,
                normed_two,
                active,
                slope,
            ))
        )
    final = middle + (part.astype(F32) + got.astype(F32) + gains[LAYERS - 1, 5])
    final = lax.optimization_barrier(final.astype(BF16))
    outputs = final, flip(final, "cy")

    sums_ffn = [None] * (LAYERS + 1)
    sums_mix = [None] * LAYERS
    sums_in = [None] * LAYERS
    reduced = [None] * LAYERS

    def second_hop(keep_x, got_x, keep_y, got_y, after):
        pass_x, pass_y = pass_on(keep_x, got_x, keep_y, got_y, after)
        all_x = (keep_x[0], got_x[0], flip(pass_x, "cy"))
        all_y = (keep_y[0], got_y[0], flip(pass_y, "tx"))
        return pass_x, pieces_of((all_x, all_y), block_rows)

    zero_first = ()
    zero_mix = ()
    zero_attention = ()
    zero_memory = ()
    above_attention = None
    for layer in reversed(range(LAYERS)):
        (
            stream,
            normed,
            qkv,
            memory,
            log_totals,
            attended,
            middle,
            normed_two,
            active,
            slope,
        ) = saved[layer]
        top = layer == LAYERS - 1
        stream_grad, down, hidden_grad, part, sums_ffn[layer] = rows_call(
            partial(ffn_backward_kernel, layer),
            place,
            (in_hbm(own_cot), slope) if top else (stream_grad, stream_above, part, got, slope),
            (order if top else gains,),
            ffn_slabs[layer],
            (),
            (row_f32, row_b16, side_hidden, row_b16),
            (sums_shape,),
            9,
            after=zero_first,
        )
        got = flip(part, "cc")
        if above_attention is not None:
            qk_give, qk_keep, qk_got, vo_keep, vo_got = above_attention
            passed, attn_pieces = second_hop(qk_keep, qk_got, vo_keep, vo_got, (hidden_grad, slope))
            zero_mix, zero_attention = (passed,), (attn_pieces,)
            reduced[layer + 1] = (spread_pieces(attn_pieces), spread_ffn)
            zero_memory = (spread_ffn,)
        ffn_operands = (normed_two, down, hidden_grad, active)
        ffn_plans = [
            [
                [[(0, x, 2, y, 0, hidden_own)] for x, y in pair_x],
                [[(1, x, 3, y, 0, hidden_own)] for x, y in pair_y],
            ]
            for pair_x, pair_y in ((GIVE_X, GIVE_Y), (KEEP_X, KEEP_Y))
        ]
        up_give, down_give = weight_grads(ffn_operands, ffn_plans[0], half)
        up_got, down_got = flip(up_give, "tx"), flip(down_give, "cy")
        stream_grad, branch_grad, attended_grad, sums_mix[layer] = rows_call(
            partial(mix_backward_kernel, layer),
            place,
            (stream_grad, middle, part, got),
            (gains,),
            attn_slabs[layer],
            (),
            (row_f32, row_b16, side_width),
            (sums_shape,),
            6,
            after=(up_give, *zero_mix),
        )
        dq, dkv, last, back = attention_backward(
            memory_bias, qkv, memory, log_totals, attended, attended_grad, table_near, zero_attention
        )
        received = flip(back, "cy")
        up_keep, down_keep = weight_grads(ffn_operands, ffn_plans[1], half, (dq,))
        passed, ffn_pieces = second_hop(up_keep, up_got, down_keep, down_got, (dq,))
        grads_in, part, sums_in[layer] = memory_backward(
            place, dq, dkv, last, received, table_near, table_far, attn_slabs[layer],
            (passed, *zero_memory),
        )
        got = flip(part, "cc")
        spread_ffn = spread_pieces(ffn_pieces)
        attn_plans = [
            [
                [[(0, x, 2, y, 0, 2 * width)] for x, y in pair_x],
                [
                    [(0, x, 2, y, 2 * width, 3 * width), (1, x, 3, y, 0, width)]
                    for x, y in pair_y
                ],
            ]
            for pair_x, pair_y in ((GIVE_X, GIVE_Y), (KEEP_X, KEEP_Y))
        ]
        attn_operands = (normed, branch_grad, grads_in, attended)
        qk_give, vo_give = weight_grads(attn_operands, attn_plans[0], half)
        qk_got, vo_got = flip(qk_give, "tx"), flip(vo_give, "cy")
        if layer > 0:
            qk_keep, vo_keep = weight_grads(attn_operands, attn_plans[1], half)
            above_attention = qk_give, qk_keep, qk_got, vo_keep, vo_got
            zero_first = (qk_give, ffn_pieces)
        stream_above = stream
    final, sums_ffn[LAYERS] = rows_call(
        leave_kernel,
        place,
        (stream_grad, stream, part, got),
        (gains,),
        None,
        (),
        (row_b16,),
        (sums_shape,),
        5,
        after=(qk_give, ffn_pieces),
    )
    qk_keep, vo_keep = weight_grads(attn_operands, attn_plans[1], half, (final,))
    passed, attn_pieces = second_hop(qk_keep, qk_got, vo_keep, vo_got, (final,))
    reduced[0] = (spread_pieces(attn_pieces), spread_ffn)
    reduced = [[piece.astype(F32).sum(axis=0) for piece in pair] for pair in reduced]
    activations, zero_act = restore(*outputs, order_back, place, (passed,))
    final_got = flip(final, "cy")
    input_grad, _ = restore(final, final_got, order_back, place)

    vector_d = []
    vector_own = []
    vector_other = []
    for layer in range(LAYERS):
        below = sums_ffn[layer - 1] if layer > 0 else sums_ffn[LAYERS]
        vector_d.append(
            jnp.concatenate(
                [below[:2], sums_mix[layer][:3], sums_ffn[layer][2:3]], axis=0
            )
        )
        ups = sums_ffn[layer][3:5].reshape(2, width, 4).transpose(0, 2, 1)
        for side, out in enumerate((vector_own, vector_other)):
            sums = sums_in[layer][side]
            out.append(
                jnp.concatenate(
                    [sums[None, :width], sums[None, 2 * width :], ups[side]], axis=0
                )
            )
    qkv_grads = [
        jnp.stack([r[0][:, i * width : (i + 1) * width] for i in range(3)]) for r in reduced
    ]
    matrix_grads = (
        jnp.stack(qkv_grads),
        jnp.stack([r[0][:, 3 * width :] for r in reduced]),
        jnp.stack([r[1][:, :hidden_own] for r in reduced]),
        jnp.stack([r[1][:, hidden_own:] for r in reduced]),
    )
    vec_d_grad = jnp.dot(
        jnp.stack(vector_d).reshape(-1, features), order_wide.T, precision=PRECISE
    ).reshape(-1)
    own_c = jnp.stack(vector_own).reshape(-1)
    other_c = jnp.stack(vector_other).reshape(-1)
    arrived = flip(jnp.concatenate([vec_d_grad, other_c]), "cy")
    vector = butterfly(jnp.concatenate([vec_d_grad, own_c]) + arrived, ("tx", "tz"))
    vec_d_grad = vector[: vec_d.size].reshape(vec_d.shape)
    vec_c_grad = vector[vec_d.size :].reshape(vec_c.shape)

    square = sum(jnp.sum(grad * grad) for grad in matrix_grads)
    square = (
        square
        + zero_act[0, 0]
        + zero_after(final_got)
        + jnp.sum(vec_d_grad * vec_d_grad) / (tok_count * ch_count)
        + jnp.sum(vec_c_grad * vec_c_grad) / tok_count
    )
    everywhere = ("tz", "tx", "cy", "cc")
    squares = lax.all_to_all(
        jnp.full((tok_count * ch_count, 128), square), everywhere, 0, 0, tiled=True
    )
    total_square = jnp.sum(squares[:, 0])
    grad_norm = jnp.sqrt(total_square)
    factor = CLIP_LIMIT / jnp.maximum(grad_norm, CLIP_LIMIT)
    attention_update = adamw(
        w_qkv, w_qkv_first, w_qkv_second, matrix_grads[0] * factor, RATE_QKV, WEIGHT_DECAY
    )
    output_update = adamw(
        w_out_t, w_out_first, w_out_second, matrix_grads[1] * factor, RATE_OUT, WEIGHT_DECAY
    )
    expand_update = adamw(
        w_up, w_up_first, w_up_second, matrix_grads[2] * factor, RATE_UP, WEIGHT_DECAY
    )
    reduce_update = adamw(
        w_down_t, w_down_first, w_down_second, matrix_grads[3] * factor, RATE_DOWN, WEIGHT_DECAY
    )
    width_update = adamw(vec_d, vec_d_first, vec_d_second, vec_d_grad * factor, RATE_VECTOR, 0.0)
    channel_update = adamw(vec_c, vec_c_first, vec_c_second, vec_c_grad * factor, RATE_VECTOR, 0.0)
    return (
        activations,
        input_grad,
        grad_norm,
        *attention_update,
        *output_update,
        *expand_update,
        *reduce_update,
        *width_update,
        *channel_update,
    )


def solution(mesh):
    tok, ch = mesh.shape["tok"], mesh.shape["ch"]
    fine = Mesh(mesh.devices.reshape(tok // 2, 2, 2, ch // 2), ("tz", "tx", "cy", "cc"))
    t, c = ("tz", "tx"), ("cy", "cc")
    cube = P(None, None, t, c)
    matrix = P(None, t, c)
    channel = P(None, None, c)
    return jax.shard_map(
        shards,
        mesh=fine,
        in_specs=(
            P(t, None),
            P(t, None),
            P(None, t, None, None, c),
            P(),
            P(t, None, None),
            P(t),
            *(cube,) * 3,
            *(matrix,) * 9,
            *(P(),) * 3,
            *(channel,) * 3,
        ),
        out_specs=(
            P(t, None),
            P(t, None),
            P(),
            *(cube,) * 3,
            *(matrix,) * 9,
            *(P(),) * 3,
            *(channel,) * 3,
        ),
        check_vma=False,
    )
```
